32 devices in a mesh: dp: 8 (over z, core), mp: 4 (over y, x).
Axes of the slice: x: 2, y: 2, z: 4, core: 2. Of those that a mesh axis runs over, the one named last changes fastest.
Arguments:
- tokens: bfloat16 [7680, 2048], P('dp'), may hold values from -6 to 6
- segment_ids: int32 [8, 960], P('dp'), may hold values from 0 to 3, never falling along the last dimension, each value on 1 to 480 neighbouring positions
- cotangent: bfloat16 [7680, 2048], P(('dp', 'mp')), may hold values from -6 to 6
- gain_in: float32 [2048], replicated, may hold values from 0.5 to 1.5
- w_in: bfloat16 [2048, 2048], P('dp'), may hold values from -0.125 to 0.125
- w_forget: bfloat16 [2048, 2048], P('dp'), may hold values from -0.125 to 0.125
- w_outgate: bfloat16 [2048, 2048], P('dp'), may hold values from -0.125 to 0.125
- bound_logit: float32 [1024], replicated, may hold values from -1 to 3
- gain_mix: float32 [2048], replicated, may hold values from 0.5 to 1.5
- w_mix: bfloat16 [2048, 2048], P('dp'), may hold values from -0.125 to 0.125
- gain_ffn: float32 [2048], replicated, may hold values from 0.5 to 1.5
- w_gate: bfloat16 [2048, 5632], P('dp', 'mp'), may hold values from -0.125 to 0.125
- w_up: bfloat16 [2048, 5632], P('dp', 'mp'), may hold values from -0.125 to 0.125
- w_down: bfloat16 [5632, 2048], P('mp', 'dp'), may hold values from -0.078125 to 0.078125
Outputs:
- mixed: bfloat16 [7680, 2048], P(('dp', 'mp'))
- grad_tokens: float32 [7680, 2048], P(('dp', 'mp'))
- grad_gain_in: float32 [2048], P('dp')
- grad_w_in: float32 [2048, 2048], P('dp')
- grad_w_forget: float32 [2048, 2048], P('dp')
- grad_w_outgate: float32 [2048, 2048], P('dp')
- grad_bound: float32 [1024], P('dp')
- grad_gain_mix: float32 [2048], P('dp')
- grad_w_mix: float32 [2048, 2048], P('dp')
- grad_gain_ffn: float32 [2048], P('dp')
- grad_w_gate: float32 [2048, 5632], P('dp', 'mp')
- grad_w_up: float32 [2048, 5632], P('dp', 'mp')
- grad_w_down: float32 [5632, 2048], P('mp', 'dp')
The draws below stay inside these ranges and needn't reach their ends.
Inputs may be any that keep to these rules, and one draw needn't show every extreme that they name: `segment_ids`: within each row ids never fall; 4 sequences, each 1 to 480 tokens, one exactly 480.
All inputs are finite; a program needn't handle non-finite values.
Results may differ from the reference program's by a relative error of at most 0.012.
The reference program's roundings to bfloat16 on the way count: a program that leaves them out, or rounds other values in their place, can miss the bound.
Values may be sent and summed in bfloat16 or wider, within the bound.
A program may use at most 384 MiB of HBM per device.

```python
import math
import jax
import jax.numpy as jnp
import numpy as np
from jax import lax

D = 2048
FF = 5632
HALF = 1024
TOK_DEV = 960
SEQS_DEV = 4
LONGEST = 480
TOKENS = 7680
N_DP = 8


def levels(stream_key, extent, split, least, top_value):
    def one(axis_at, parts):
        draws = jax.random.uniform(jax.random.fold_in(jax.random.fold_in(stream_key, 6), axis_at), (parts,), jnp.float32, least / len(split), top_value / len(split))
        return jnp.repeat(jnp.exp(draws), extent[axis_at] // parts).reshape((-1,) + (1,) * (len(extent) - axis_at - 1))

    loudness = one(*split[0])
    for cut in split[1:]:
        loudness = loudness * one(*cut)
    return loudness


def split_up(amount, total, reach, skew):
    weights = [(1 << 20) // math.isqrt(rank ** skew) + 1 for rank in range(2, amount + 1)]
    spare, counts = total - reach - (amount - 1), [1] * (amount - 1)
    while spare > 0:
        free = [i for i in range(amount - 1) if counts[i] < reach]
        whole, budget = sum([weights[i] for i in free]), spare
        for i in free:
            addition = min(reach - counts[i], max(1, budget * weights[i] // whole), spare)
            counts[i] = counts[i] + addition
            spare = spare - addition
    return np.array([reach] + counts)


def ragged(own_key, count, total, bound, skew):
    if count == 2:
        one = jax.random.randint(own_key, (), max(1, total - bound), min(bound, total - 1) + 1)
        return jnp.stack([one, total - one])
    tallies = jnp.asarray(split_up(count, total, bound, skew), jnp.int32)
    couples = (count - 1) // 2
    source_of, taker = tallies[1:1 + 2 * couples:2], tallies[2:2 + 2 * couples:2]
    margin = jnp.minimum(source_of - 1, bound - taker)
    moved = jax.random.randint(jax.random.fold_in(own_key, 1), (couples,), 0, 1 << 20) % (margin + 1)
    tallies = tallies.at[1:1 + 2 * couples:2].set(source_of - moved).at[2:2 + 2 * couples:2].set(taker + moved)
    return tallies[jax.random.permutation(jax.random.fold_in(own_key, 2), count)]


def bell_draw(key, shape, spread, most, shards=(), kind=jnp.bfloat16):
    array = jax.random.normal(key, shape, jnp.float32) * spread
    if len(shards) > 0:
        array = levels(key, shape, shards, -0.22, 0.18) * array
    return jnp.clip(array, min=-most, max=most).astype(kind)


def setup_inputs(seed: int = 0) -> dict:
    streams_of = jax.random.split(jax.random.key(seed), 15)
    return {
        "tokens": bell_draw(streams_of[0], (TOKENS, D), 1.0, 6.0, ((0, 8),)),
        "segment_ids": jax.vmap(lambda own: jnp.searchsorted(jnp.cumsum(ragged(own, SEQS_DEV, TOK_DEV, LONGEST, 0)), jnp.arange(TOK_DEV), side="right"))(jax.random.split(streams_of[1], N_DP)).reshape((N_DP, TOK_DEV)).astype(jnp.int32),
        "cotangent": bell_draw(streams_of[2], (TOKENS, D), 1.0, 6.0, ((0, 32),)),
        "gain_in": jnp.clip(1.0 + 0.1 * jax.random.normal(streams_of[3], (D,), jnp.float32), 0.5, 1.5),
        "w_in": bell_draw(streams_of[4], (D, D), D ** -0.5, 0.125, ((0, 8),)),
        "w_forget": bell_draw(streams_of[5], (D, D), D ** -0.5, 0.125, ((0, 8),)),
        "w_outgate": bell_draw(streams_of[6], (D, D), D ** -0.5, 0.125, ((0, 8),)),
        "bound_logit": jnp.clip(jax.random.uniform(streams_of[7], (HALF,), jnp.float32, -1.0, 3.0), -1.0, 3.0),
        "gain_mix": jnp.clip(1.0 + 0.1 * jax.random.normal(streams_of[8], (D,), jnp.float32), 0.5, 1.5),
        "w_mix": bell_draw(streams_of[9], (D, D), D ** -0.5, 0.125, ((0, 8),)),
        "gain_ffn": jnp.clip(1.0 + 0.1 * jax.random.normal(streams_of[10], (D,), jnp.float32), 0.5, 1.5),
        "w_gate": bell_draw(streams_of[11], (D, FF), D ** -0.5, 0.125, ((0, 8), (1, 4))),
        "w_up": bell_draw(streams_of[12], (D, FF), D ** -0.5, 0.125, ((0, 8), (1, 4))),
        "w_down": bell_draw(streams_of[13], (FF, D), FF ** -0.5, 0.078125, ((0, 4), (1, 8))),
    }


@jax.custom_vjp
def low(v):
    return lax.optimization_barrier(v.astype(jnp.bfloat16)).astype(jnp.float32)

@jax.custom_vjp
def low_back(v):
    return v

def low_keep(v):
    return (low(v), None)

def low_pass(kept, grad):
    return (grad,)

def back_keep(v):
    return (v, None)

def back_low(kept, grad):
    return (low(grad),)
low.defvjp(low_keep, low_pass)
low_back.defvjp(back_keep, back_low)
epsilon = 1e-06

def root_norm(values, gain):
    return values * lax.rsqrt(lax.optimization_barrier(jnp.mean(values * values, axis=-1, keepdims=True)) + epsilon) * gain

def product(left, right):
    return jnp.dot(left, right, precision=lax.Precision.HIGHEST, preferred_element_type=jnp.float32)

def combine(former, latter):
    decay_re = latter[0] * former[0] - latter[1] * former[1]
    decay_im = latter[0] * former[1] + latter[1] * former[0]
    state_re = latter[0] * former[2] - latter[1] * former[3] + latter[2]
    state_im = latter[0] * former[3] + latter[1] * former[2] + latter[3]
    return (decay_re, decay_im, state_re, state_im)

def segment_starts(ident):
    previous = jnp.concatenate([ident[:1] - 1, ident[:-1]])
    return jnp.where(ident != previous, 1.0, 0.0).astype(jnp.float32)

def recurrent_mix(proj_in, proj_forget, proj_gate, gain_mix, bound_logit, starts):
    half_width = proj_forget.shape[1] // 2
    low_bound = jax.nn.sigmoid(bound_logit)
    forget = low_bound + (1.0 - low_bound) * jax.nn.sigmoid(proj_forget[:, :half_width])
    phase_angle = proj_forget[:, half_width:]
    carry_on = (1.0 - starts)[:, None]
    decay_re = forget * jnp.cos(phase_angle) * carry_on
    decay_im = forget * jnp.sin(phase_angle) * carry_on
    inflow = 1.0 - forget
    input_re = jax.nn.silu(proj_in[:, :half_width]) * inflow
    input_im = jax.nn.silu(proj_in[:, half_width:]) * inflow
    scanned = lax.associative_scan(combine, (decay_re, decay_im, input_re, input_im), axis=0)
    states = jnp.concatenate([scanned[2], scanned[3]], axis=1)
    return root_norm(states, gain_mix) * jax.nn.silu(proj_gate)

def block_forward(stream, gain_in, w_in, w_forget, w_outgate, bound_logit, gain_mix, w_mix, gain_ffn, w_gate, w_up, w_down, starts):
    normed = low(root_norm(stream, gain_in))
    proj_in = low_back(product(normed, w_in))
    proj_forget = low_back(product(normed, w_forget))
    proj_gate = low_back(product(normed, w_outgate))
    mixer_out = recurrent_mix(proj_in, proj_forget, proj_gate, gain_mix, bound_logit, starts)
    branch = low_back(product(low(mixer_out), w_mix))
    middle = stream + branch
    ffn_in = low(root_norm(middle, gain_ffn))
    gate_val = low_back(product(ffn_in, w_gate))
    up_val = low_back(product(ffn_in, w_up))
    hidden = low(jax.nn.silu(gate_val) * up_val)
    return middle + product(hidden, w_down)

def reference(tokens, segment_ids, cotangent, gain_in, w_in, w_forget, w_outgate, bound_logit, gain_mix, w_mix, gain_ffn, w_gate, w_up, w_down):
    width = tokens.shape[1]
    params = tuple((param.astype(jnp.float32) for param in (gain_in, w_in, w_forget, w_outgate, bound_logit, gain_mix, w_mix, gain_ffn, w_gate, w_up, w_down)))
    group_tokens = tokens.astype(jnp.float32).reshape(N_DP, -1, width)
    group_cot = cotangent.astype(jnp.float32).reshape(N_DP, -1, width)

    def one_group(totals, inputs):
        stream, ident, grad_out = inputs
        starts = segment_starts(ident)

        def forward(stream, *weights):
            return block_forward(stream, *weights, starts)
        output, pullback = jax.vjp(forward, stream, *params)
        grads = pullback(grad_out)
        summed = tuple((total + grad for total, grad in zip(totals, grads[1:])))
        return (summed, (output, grads[0]))
    init = tuple((jnp.zeros_like(param) for param in params))
    sums, (outputs, grad_stream) = lax.scan(one_group, init, (group_tokens, segment_ids, group_cot))
    return (outputs.reshape(tokens.shape).astype(jnp.bfloat16), grad_stream.reshape(tokens.shape), sums[0], sums[1], sums[2], sums[3], sums[4], sums[5], sums[6], sums[7], sums[8], sums[9], sums[10])
```

```python
import functools

import jax
import jax.numpy as jnp
from jax import lax
from jax.experimental import pallas as pl
from jax.experimental.pallas import tpu as pltpu
from jax.sharding import PartitionSpec as P

EPS = 1e-06
F32, BF16 = jnp.float32, jnp.bfloat16
LANE = 128
CHUNKS = 8


def dot(left, right):
    return jnp.dot(left, right, preferred_element_type=F32)


def dot_trans(left, right):
    return lax.dot_general(left, right, (((1,), (1,)), ((), ())), preferred_element_type=F32)


def dot_rows(left, right):
    return lax.dot_general(left, right, (((0,), (0,)), ((), ())), preferred_element_type=F32)


def sigmoid(v):
    return 1.0 / (1.0 + jnp.exp(-v))


def scan_forward(pin, pf, starts, bl, st, phasor, rowsq, a_re, a_im, b_re, b_im):
    rows, half = pin.shape[0], pin.shape[1] // 2
    span = rows // CHUNKS
    lanes = half // LANE
    low = sigmoid(bl[...])
    step = 48

    def prepare(i, _):
        at = pl.ds(pl.multiple_of(i * step, 8), step)
        forget = low + (1.0 - low) * sigmoid(pf[at, :half])
        phase = pf[at, half:]
        keep = 1.0 - starts[at, :]
        cos, sin = jnp.cos(phase) * keep, jnp.sin(phase) * keep
        phasor[at, :half] = cos
        phasor[at, half:] = sin
        x_re, x_im = pin[at, :half], pin[at, half:]
        inflow = 1.0 - forget
        in_re, in_im = x_re * sigmoid(x_re) * inflow, x_im * sigmoid(x_im) * inflow
        d_re, d_im = forget * cos, forget * sin
        for j in range(lanes):
            cut = slice(j * LANE, (j + 1) * LANE)
            a_re[j, at, :] = d_re[:, cut]
            a_im[j, at, :] = d_im[:, cut]
            b_re[j, at, :] = in_re[:, cut]
            b_im[j, at, :] = in_im[:, cut]
        return 0

    lax.fori_loop(0, rows // step, prepare, 0)
    zero, one = jnp.zeros((CHUNKS, LANE), F32), jnp.ones((CHUNKS, LANE), F32)

    def local(s, carry):
        at = pl.ds(s, CHUNKS, stride=span)
        out = []
        for j in range(lanes):
            p_re, p_im, s_re, s_im = carry[4 * j : 4 * j + 4]
            d_re, d_im = a_re.at[j][at, :], a_im.at[j][at, :]
            i_re, i_im = b_re.at[j][at, :], b_im.at[j][at, :]
            p_re, p_im = d_re * p_re - d_im * p_im, d_re * p_im + d_im * p_re
            s_re, s_im = d_re * s_re - d_im * s_im + i_re, d_re * s_im + d_im * s_re + i_im
            a_re.at[j][at, :] = p_re
            a_im.at[j][at, :] = p_im
            b_re.at[j][at, :] = s_re
            b_im.at[j][at, :] = s_im
            out += [p_re, p_im, s_re, s_im]
        return tuple(out)

    last = lax.fori_loop(0, span, local, (one, zero, zero, zero) * lanes, unroll=2)
    carries = []
    for j in range(lanes):
        p_re, p_im, s_re, s_im = last[4 * j : 4 * j + 4]
        c_re = c_im = jnp.zeros((1, LANE), F32)
        held = []
        for k in range(CHUNKS):
            held.append((c_re, c_im))
            q_re, q_im = p_re[k : k + 1], p_im[k : k + 1]
            c_re, c_im = (
                q_re * c_re - q_im * c_im + s_re[k : k + 1],
                q_re * c_im + q_im * c_re + s_im[k : k + 1],
            )
        carries.append(held)
    fix = 40
    for k in range(CHUNKS):

        def finish(i, _):
            at = pl.ds(pl.multiple_of(k * span + i * fix, 8), fix)
            total = jnp.zeros((fix, LANE), F32)
            for j in range(lanes):
                c_re, c_im = carries[j][k]
                p_re, p_im = a_re[j, at, :], a_im[j, at, :]
                s_re = b_re[j, at, :] + p_re * c_re - p_im * c_im
                s_im = b_im[j, at, :] + p_re * c_im + p_im * c_re
                st[at, j * LANE : (j + 1) * LANE] = s_re
                st[at, half + j * LANE : half + (j + 1) * LANE] = s_im
                total = total + s_re * s_re + s_im * s_im
            rowsq[at, :] = jnp.sum(total, axis=1, keepdims=True)
            return 0

        lax.fori_loop(0, span // fix, finish, 0)


def scan_backward(
    gm, pin, pf, pg, st, phasor, r, rowdot, bl, gain, gin, gf, gg, dgain, dbound, a_re, a_im, b_re, b_im
):
    rows, half = pin.shape[0], pin.shape[1] // 2
    width = 2 * half
    span = rows // CHUNKS
    lanes = half // LANE
    low = sigmoid(bl[...])
    step = 48

    def prepare(i, total):
        at = pl.ds(pl.multiple_of(i * step, 16), step)
        g, gate = gm[at, :], pg[at, :]
        sig = sigmoid(gate)
        silu = gate * sig
        n = st[at, :] * r[at, :]
        gs = g * silu
        gg[at, :] = (g * n * gain[...] * (sig * (1.0 + gate * (1.0 - sig)))).astype(gg.dtype)
        total = total + jnp.sum((gs * n).reshape(step // 8, 8, width), axis=0)
        d_st = r[at, :] * (gs * gain[...] - n * rowdot[at, :])
        forget = low + (1.0 - low) * sigmoid(pf[at, :half])
        d_re, d_im = forget * phasor[at, :half], forget * phasor[at, half:]
        for j in range(lanes):
            a_re[j, at, :] = d_re[:, j * LANE : (j + 1) * LANE]
            a_im[j, at, :] = d_im[:, j * LANE : (j + 1) * LANE]
            b_re[j, at, :] = d_st[:, j * LANE : (j + 1) * LANE]
            b_im[j, at, :] = d_st[:, half + j * LANE : half + (j + 1) * LANE]
        return total

    total = lax.fori_loop(0, rows // step, prepare, jnp.zeros((8, width), F32))
    dgain[...] = jnp.sum(total, axis=0, keepdims=True)
    zero, one = jnp.zeros((CHUNKS, LANE), F32), jnp.ones((CHUNKS, LANE), F32)

    def local(i, carry):
        at = pl.ds(span - 1 - i, CHUNKS, stride=span)
        out = []
        for j in range(lanes):
            p_re, p_im, s_re, s_im = carry[4 * j : 4 * j + 4]
            d_re, d_im = a_re.at[j][at, :], a_im.at[j][at, :]
            s_re, s_im = s_re + b_re.at[j][at, :], s_im + b_im.at[j][at, :]
            a_re.at[j][at, :] = p_re
            a_im.at[j][at, :] = p_im
            b_re.at[j][at, :] = s_re
            b_im.at[j][at, :] = s_im
            p_re, p_im = d_re * p_re + d_im * p_im, d_re * p_im - d_im * p_re
            s_re, s_im = d_re * s_re + d_im * s_im, d_re * s_im - d_im * s_re
            out += [p_re, p_im, s_re, s_im]
        return tuple(out)

    last = lax.fori_loop(0, span, local, (one, zero, zero, zero) * lanes, unroll=2)
    carries = []
    for j in range(lanes):
        p_re, p_im, s_re, s_im = last[4 * j : 4 * j + 4]
        c_re = c_im = jnp.zeros((1, LANE), F32)
        held = [None] * CHUNKS
        for k in reversed(range(CHUNKS)):
            held[k] = (c_re, c_im)
            q_re, q_im = p_re[k : k + 1], p_im[k : k + 1]
            c_re, c_im = (
                q_re * c_re - q_im * c_im + s_re[k : k + 1],
                q_re * c_im + q_im * c_re + s_im[k : k + 1],
            )
        carries.append(held)
    fix = 40
    for k in range(CHUNKS):

        def carry_in(i, _):
            at = pl.ds(pl.multiple_of(k * span + i * fix, 8), fix)
            for j in range(lanes):
                c_re, c_im = carries[j][k]
                p_re, p_im = a_re[j, at, :], a_im[j, at, :]
                b_re[j, at, :] += p_re * c_re - p_im * c_im
                b_im[j, at, :] += p_re * c_im + p_im * c_re
            return 0

        lax.fori_loop(0, span // fix, carry_in, 0)

    def finish(i, carry):
        before, total = carry
        at = pl.ds(pl.multiple_of(i * step, 16), step)
        g_re = jnp.concatenate([b_re[j, at, :] for j in range(lanes)], axis=1)
        g_im = jnp.concatenate([b_im[j, at, :] for j in range(lanes)], axis=1)
        now = st[at, :]
        prev = jnp.concatenate([before, now[:-1]], axis=0)
        q_re, q_im = prev[:, :half], prev[:, half:]
        dd_re, dd_im = g_re * q_re + g_im * q_im, g_im * q_re - g_re * q_im
        mag = sigmoid(pf[at, :half])
        forget = low + (1.0 - low) * mag
        cos, sin = phasor[at, :half], phasor[at, half:]
        x_re, x_im = pin[at, :half], pin[at, half:]
        sig_re, sig_im = sigmoid(x_re), sigmoid(x_im)
        inflow = 1.0 - forget
        d_forget = dd_re * cos + dd_im * sin - g_re * x_re * sig_re - g_im * x_im * sig_im
        gf[at, :half] = (d_forget * (1.0 - low) * mag * (1.0 - mag)).astype(gf.dtype)
        gf[at, half:] = (forget * (dd_im * cos - dd_re * sin)).astype(gf.dtype)
        gin[at, :half] = (g_re * inflow * sig_re * (1.0 + x_re * (1.0 - sig_re))).astype(gin.dtype)
        gin[at, half:] = (g_im * inflow * sig_im * (1.0 + x_im * (1.0 - sig_im))).astype(gin.dtype)
        total = total + jnp.sum((d_forget * (1.0 - mag)).reshape(step // 8, 8, half), axis=0)
        return now[step - 1 :], total

    first = (jnp.zeros((1, width), F32), jnp.zeros((8, half), F32))
    total = lax.fori_loop(0, rows // step, finish, first)[1]
    dbound[...] = jnp.sum(total, axis=0, keepdims=True) * low * (1.0 - low)


def call_local(body, outs, scratch, *args, name):
    return pl.pallas_call(
        body,
        out_shape=outs,
        scratch_shapes=scratch,
        compiler_params=pltpu.CompilerParams(vmem_limit_bytes=48 * 2**20),
        name=name,
    )(*args)


def per_device(n_dp, n_mp, tokens, segment_ids, cotangent, gain_in, w_in, w_forget, w_outgate, bound_logit, gain_mix,
               w_mix, gain_ffn, w_gate, w_up, w_down):
    m, d = lax.axis_index("mp"), lax.axis_index("dp")
    rows, width = tokens.shape
    half = bound_logit.shape[0]
    ch = half // n_mp
    mine = 2 * ch
    own = rows // n_mp
    ffn = w_gate.shape[1]
    shard = w_in.shape[0]

    def from_peer(x, j):
        return lax.ppermute(x, "mp", [(q, q ^ j) for q in range(n_mp)])

    def cols(x, at, size):
        return lax.dynamic_slice_in_dim(x, at, size, 1)

    def own_channels(x):
        return jnp.concatenate([cols(x, m * ch, ch), cols(x, half + m * ch, ch)], axis=1)

    def gather_rows(x):
        out = jnp.zeros((x.shape[0] * n_mp, x.shape[1]), x.dtype)
        for j in range(n_mp):
            part = x if j == 0 else from_peer(x, j)
            out = lax.dynamic_update_slice_in_dim(out, part, (m ^ j) * x.shape[0], 0)
        return out

    def scatter_sum(x):
        total = lax.dynamic_slice_in_dim(x, m * own, own, 0)
        for j in range(1, n_mp):
            part = lax.dynamic_slice_in_dim(x, (m ^ j) * own, own, 0).astype(BF16)
            total = total + from_peer(part, j).astype(F32)
        return total

    mixer_cols = jnp.concatenate([own_channels(w_in), own_channels(w_forget), own_channels(w_outgate)], axis=1)
    w_cat = lax.all_gather(mixer_cols, "dp", axis=0, tiled=True)
    mix_cols = cols(w_mix, m * mine, mine)
    w_mix_q = lax.all_gather(mix_cols, "dp", axis=0, tiled=True)
    wg = lax.all_gather(w_gate, "dp", axis=0, tiled=True)
    wu = lax.all_gather(w_up, "dp", axis=0, tiled=True)
    wd = lax.all_gather(w_down, "dp", axis=1, tiled=True)

    core = lax.rem(d, 2)
    hw = width // 2
    part = lax.dynamic_slice_in_dim(w_mix_q, core * hw, hw, 0)
    half_mix = jnp.zeros((hw, width), BF16)
    for j in range(n_mp):
        piece = part if j == 0 else from_peer(part, j)
        half_mix = lax.dynamic_update_slice_in_dim(half_mix, piece, (m ^ j) * mine, 1)
    other_mix = lax.ppermute(half_mix, "dp", [(q, q ^ 1) for q in range(n_dp)])
    wm = jnp.zeros((width, width), BF16)
    wm = lax.dynamic_update_slice_in_dim(wm, half_mix, core * hw, 0)
    wm = lax.dynamic_update_slice_in_dim(wm, other_mix, (1 - core) * hw, 0)

    grad_out = gather_rows(cotangent)

    stream = tokens.astype(F32)
    ident = segment_ids[0]
    previous = jnp.concatenate([ident[:1] - 1, ident[:-1]])
    starts = jnp.where(ident != previous, 1.0, 0.0).astype(F32)[:, None]
    r_in = lax.rsqrt(jnp.mean(stream * stream, axis=-1, keepdims=True) + EPS)
    normed = (stream * r_in * gain_in).astype(BF16)
    pin = dot(normed, w_cat[:, :mine])
    pf = dot(normed, w_cat[:, mine : 2 * mine])
    pg = dot(normed, w_cat[:, 2 * mine :])
    bl = lax.dynamic_slice_in_dim(bound_logit, m * ch, ch, 0)[None]
    gain = own_channels(gain_mix[None])
    lanes = ch // LANE
    scratch = [pltpu.VMEM((lanes, rows, LANE), F32)] * 4
    st, phasor, rowsq = call_local(
        scan_forward,
        (
            jax.ShapeDtypeStruct((rows, mine), F32),
            jax.ShapeDtypeStruct((rows, mine), F32),
            jax.ShapeDtypeStruct((rows, 1), F32),
        ),
        scratch,
        pin, pf, starts, bl,
        name="scan_forward",
    )
    rowsq = lax.psum(rowsq[:, 0], "mp")[:, None]
    r_mix = lax.rsqrt(rowsq / width + EPS)
    mixer_mine = (st * r_mix * gain * (pg * jax.nn.sigmoid(pg))).astype(BF16)
    mixer_out = jnp.zeros((rows, width), BF16)
    for j in range(n_mp):
        piece = mixer_mine if j == 0 else from_peer(mixer_mine, j)
        mixer_out = lax.dynamic_update_slice_in_dim(mixer_out, piece[:, :ch], (m ^ j) * ch, 1)
        mixer_out = lax.dynamic_update_slice_in_dim(mixer_out, piece[:, ch:], half + (m ^ j) * ch, 1)
    branch = dot(mixer_out, wm)
    middle = stream + branch
    r_ffn = lax.rsqrt(jnp.mean(middle * middle, axis=-1, keepdims=True) + EPS)
    ffn_in = (middle * r_ffn * gain_ffn).astype(BF16)

    gate_val = dot(ffn_in, wg)
    up_val = dot(ffn_in, wu)
    sig = jax.nn.sigmoid(gate_val)
    hidden = (gate_val * sig * up_val).astype(BF16)
    grad_hidden = dot_trans(grad_out, wd)
    grad_gate = (grad_hidden * up_val * sig * (1.0 + gate_val * (1.0 - sig))).astype(BF16)
    grad_up = (grad_hidden * gate_val * sig).astype(BF16)
    grad_ffn = scatter_sum(dot_trans(grad_gate, wg) + dot_trans(grad_up, wu))
    g_down = lax.psum_scatter(dot_rows(grad_out, hidden).astype(BF16), "dp", scatter_dimension=0, tiled=True)
    g_gate_up = lax.psum_scatter(
        jnp.concatenate([dot_rows(ffn_in, grad_gate), dot_rows(ffn_in, grad_up)], axis=1).astype(BF16),
        "dp", scatter_dimension=0, tiled=True,
    )
    down = scatter_sum(dot(hidden, wd))
    row_at = m * own

    def own_rows(x):
        return lax.dynamic_slice_in_dim(x, row_at, own, 0)

    middle_own = own_rows(middle)
    mixed = (middle_own + down).astype(BF16)

    r_own = own_rows(r_ffn)
    n_own = middle_own * r_own
    gain_ffn_part = jnp.sum(grad_ffn * n_own, axis=0)
    gn = grad_ffn * gain_ffn
    grad_middle = cotangent.astype(F32) + r_own * (gn - n_own * jnp.mean(gn * n_own, axis=-1, keepdims=True))
    grad_branch = grad_middle.astype(BF16)
    rowdot_own = jnp.mean(grad_branch.astype(F32) * (middle_own - own_rows(stream)), axis=-1, keepdims=True)
    grad_mixer_own = dot_trans(grad_branch, wm)

    gm = jnp.zeros((rows, mine), F32)
    gb_cols = jnp.zeros((rows, mine), BF16)
    rowdot = jnp.zeros((rows, 1), F32)
    for j in range(n_mp):
        q = m ^ j
        piece = jnp.concatenate([cols(grad_mixer_own, q * ch, ch), cols(grad_mixer_own, half + q * ch, ch)], axis=1)
        gb = cols(grad_branch, q * mine, mine)
        rd = rowdot_own
        if j:
            piece, gb, rd = from_peer(piece, j), from_peer(gb, j), from_peer(rd, j)
        gm = lax.dynamic_update_slice_in_dim(gm, piece, q * own, 0)
        gb_cols = lax.dynamic_update_slice_in_dim(gb_cols, gb, q * own, 0)
        rowdot = lax.dynamic_update_slice_in_dim(rowdot, rd, q * own, 0)
    gin, gf, gg, dgain, dbound = call_local(
        scan_backward,
        (
            jax.ShapeDtypeStruct((rows, mine), BF16),
            jax.ShapeDtypeStruct((rows, mine), BF16),
            jax.ShapeDtypeStruct((rows, mine), BF16),
            jax.ShapeDtypeStruct((1, mine), F32),
            jax.ShapeDtypeStruct((1, ch), F32),
        ),
        scratch,
        gm, pin, pf, pg, st, phasor, r_mix, rowdot, bl, gain,
        name="scan_backward",
    )
    g_cat = jnp.concatenate([gin, gf, gg], axis=1)
    g_mix = lax.psum_scatter(
        jnp.concatenate([dot_rows(normed, g_cat), dot_rows(mixer_out, gb_cols)], axis=1).astype(BF16),
        "dp", scatter_dimension=0, tiled=True,
    )
    grad_normed = scatter_sum(dot_trans(g_cat, w_cat))
    s_own, ri_own = own_rows(stream), own_rows(r_in)
    n_in = s_own * ri_own
    gain_in_part = jnp.sum(grad_normed * n_in, axis=0)
    gn_in = grad_normed * gain_in
    grad_tokens = grad_middle + ri_own * (gn_in - n_in * jnp.mean(gn_in * n_in, axis=-1, keepdims=True))

    g_win = jnp.zeros((shard, width), F32)
    g_wf, g_wo, g_wm = g_win, g_win, g_win
    for j in range(n_mp):
        q = m ^ j
        piece = (g_mix if j == 0 else from_peer(g_mix, j)).astype(F32)

        def put(total, lo):
            total = lax.dynamic_update_slice_in_dim(total, piece[:, lo : lo + ch], q * ch, 1)
            return lax.dynamic_update_slice_in_dim(total, piece[:, lo + ch : lo + mine], half + q * ch, 1)

        g_win, g_wf, g_wo = put(g_win, 0), put(g_wf, mine), put(g_wo, 2 * mine)
        g_wm = lax.dynamic_update_slice_in_dim(g_wm, piece[:, 3 * mine :], q * mine, 1)

    gmix_full = jnp.zeros((width,), F32)
    gmix_full = lax.dynamic_update_slice_in_dim(gmix_full, dgain[0, :ch], m * ch, 0)
    gmix_full = lax.dynamic_update_slice_in_dim(gmix_full, dgain[0, ch:], half + m * ch, 0)
    gb_full = lax.dynamic_update_slice_in_dim(jnp.zeros((half,), F32), dbound[0], m * ch, 0)
    small = lax.psum(jnp.concatenate([gain_in_part, gain_ffn_part, gmix_full, gb_full]), ("dp", "mp"))

    def part_of(lo, size):
        return lax.dynamic_slice_in_dim(small, lo + d * (size // n_dp), size // n_dp, 0)

    return (
        mixed,
        grad_tokens,
        part_of(0, width),
        g_win,
        g_wf,
        g_wo,
        part_of(3 * width, half),
        part_of(2 * width, width),
        g_wm,
        part_of(width, width),
        g_gate_up[:, :ffn].astype(F32),
        g_gate_up[:, ffn:].astype(F32),
        g_down.astype(F32).T,
    )


def solution(mesh):
    both, split = P(("dp", "mp"), None), P("dp", "mp")
    row, vec = P("dp", None), P("dp")
    return jax.shard_map(
        functools.partial(per_device, mesh.shape["dp"], mesh.shape["mp"]),
        mesh=mesh,
        in_specs=(row, row, both, P(), row, row, row, P(), P(), row, P(), split, split, P("mp", "dp")),
        out_specs=(both, both, vec, row, row, row, vec, vec, row, vec, split, split, P("mp", "dp")),
        check_vma=False,
    )
```

```python
import functools

import jax
import jax.numpy as jnp
from jax import lax
from jax.experimental import pallas as pl
from jax.experimental.pallas import tpu as pltpu
from jax.sharding import PartitionSpec as P

EPS = 1e-06
F32, BF16 = jnp.float32, jnp.bfloat16
LANE = 128
CHUNKS = 8


def dot(left, right):
    return jnp.dot(left, right, preferred_element_type=F32)


def dot_trans(left, right):
    return lax.dot_general(left, right, (((1,), (1,)), ((), ())), preferred_element_type=F32)


def dot_rows(left, right):
    return lax.dot_general(left, right, (((0,), (0,)), ((), ())), preferred_element_type=F32)


def sigmoid(v):
    return 1.0 / (1.0 + jnp.exp(-v))


def scan_forward(pin, pf, starts, bl, st, phasor, rowsq, a_re, a_im, b_re, b_im):
    rows, half = pin.shape[0], pin.shape[1] // 2
    span = rows // CHUNKS
    lanes = half // LANE
    low = sigmoid(bl[...])
    step = 48

    def prepare(i, _):
        at = pl.ds(pl.multiple_of(i * step, 8), step)
        forget = low + (1.0 - low) * sigmoid(pf[at, :half])
        phase = pf[at, half:]
        keep = 1.0 - starts[at, :]
        cos, sin = jnp.cos(phase) * keep, jnp.sin(phase) * keep
        phasor[at, :half] = cos
        phasor[at, half:] = sin
        x_re, x_im = pin[at, :half], pin[at, half:]
        inflow = 1.0 - forget
        in_re, in_im = x_re * sigmoid(x_re) * inflow, x_im * sigmoid(x_im) * inflow
        d_re, d_im = forget * cos, forget * sin
        for j in range(lanes):
            cut = slice(j * LANE, (j + 1) * LANE)
            a_re[j, at, :] = d_re[:, cut]
            a_im[j, at, :] = d_im[:, cut]
            b_re[j, at, :] = in_re[:, cut]
            b_im[j, at, :] = in_im[:, cut]
        return 0

    lax.fori_loop(0, rows // step, prepare, 0)
    zero, one = jnp.zeros((CHUNKS, LANE), F32), jnp.ones((CHUNKS, LANE), F32)

    def local(s, carry):
        at = pl.ds(s, CHUNKS, stride=span)
        out = []
        for j in range(lanes):
            p_re, p_im, s_re, s_im = carry[4 * j : 4 * j + 4]
            d_re, d_im = a_re.at[j][at, :], a_im.at[j][at, :]
            i_re, i_im = b_re.at[j][at, :], b_im.at[j][at, :]
            p_re, p_im = d_re * p_re - d_im * p_im, d_re * p_im + d_im * p_re
            s_re, s_im = d_re * s_re - d_im * s_im + i_re, d_re * s_im + d_im * s_re + i_im
            a_re.at[j][at, :] = p_re
            a_im.at[j][at, :] = p_im
            b_re.at[j][at, :] = s_re
            b_im.at[j][at, :] = s_im
            out += [p_re, p_im, s_re, s_im]
        return tuple(out)

    last = lax.fori_loop(0, span, local, (one, zero, zero, zero) * lanes, unroll=2)
    carries = []
    for j in range(lanes):
        p_re, p_im, s_re, s_im = last[4 * j : 4 * j + 4]
        c_re = c_im = jnp.zeros((1, LANE), F32)
        held = []
        for k in range(CHUNKS):
            held.append((c_re, c_im))
            q_re, q_im = p_re[k : k + 1], p_im[k : k + 1]
            c_re, c_im = (
                q_re * c_re - q_im * c_im + s_re[k : k + 1],
                q_re * c_im + q_im * c_re + s_im[k : k + 1],
            )
        carries.append(held)
    fix = 40
    for k in range(CHUNKS):

        def finish(i, _):
            at = pl.ds(pl.multiple_of(k * span + i * fix, 8), fix)
            total = jnp.zeros((fix, LANE), F32)
            for j in range(lanes):
                c_re, c_im = carries[j][k]
                p_re, p_im = a_re[j, at, :], a_im[j, at, :]
                s_re = b_re[j, at, :] + p_re * c_re - p_im * c_im
                s_im = b_im[j, at, :] + p_re * c_im + p_im * c_re
                st[at, j * LANE : (j + 1) * LANE] = s_re
                st[at, half + j * LANE : half + (j + 1) * LANE] = s_im
                total = total + s_re * s_re + s_im * s_im
            rowsq[at, :] = jnp.sum(total, axis=1, keepdims=True)
            return 0

        lax.fori_loop(0, span // fix, finish, 0)


def scan_backward(
    gm, pin, pf, pg, st, phasor, r, rowdot, bl, gain, gin, gf, gg, dgain, dbound, a_re, a_im, b_re, b_im
):
    rows, half = pin.shape[0], pin.shape[1] // 2
    width = 2 * half
    span = rows // CHUNKS
    lanes = half // LANE
    low = sigmoid(bl[...])
    step = 48

    def prepare(i, total):
        at = pl.ds(pl.multiple_of(i * step, 16), step)
        g, gate = gm[at, :], pg[at, :]
        sig = sigmoid(gate)
        silu = gate * sig
        n = st[at, :] * r[at, :]
        gs = g * silu
        gg[at, :] = (g * n * gain[...] * (sig * (1.0 + gate * (1.0 - sig)))).astype(gg.dtype)
        total = total + jnp.sum((gs * n).reshape(step // 8, 8, width), axis=0)
        d_st = r[at, :] * (gs * gain[...] - n * rowdot[at, :])
        forget = low + (1.0 - low) * sigmoid(pf[at, :half])
        d_re, d_im = forget * phasor[at, :half], forget * phasor[at, half:]
        for j in range(lanes):
            a_re[j, at, :] = d_re[:, j * LANE : (j + 1) * LANE]
            a_im[j, at, :] = d_im[:, j * LANE : (j + 1) * LANE]
            b_re[j, at, :] = d_st[:, j * LANE : (j + 1) * LANE]
            b_im[j, at, :] = d_st[:, half + j * LANE : half + (j + 1) * LANE]
        return total

    total = lax.fori_loop(0, rows // step, prepare, jnp.zeros((8, width), F32))
    dgain[...] = jnp.sum(total, axis=0, keepdims=True)
    zero, one = jnp.zeros((CHUNKS, LANE), F32), jnp.ones((CHUNKS, LANE), F32)

    def local(i, carry):
        at = pl.ds(span - 1 - i, CHUNKS, stride=span)
        out = []
        for j in range(lanes):
            p_re, p_im, s_re, s_im = carry[4 * j : 4 * j + 4]
            d_re, d_im = a_re.at[j][at, :], a_im.at[j][at, :]
            s_re, s_im = s_re + b_re.at[j][at, :], s_im + b_im.at[j][at, :]
            a_re.at[j][at, :] = p_re
            a_im.at[j][at, :] = p_im
            b_re.at[j][at, :] = s_re
            b_im.at[j][at, :] = s_im
            p_re, p_im = d_re * p_re + d_im * p_im, d_re * p_im - d_im * p_re
            s_re, s_im = d_re * s_re + d_im * s_im, d_re * s_im - d_im * s_re
            out += [p_re, p_im, s_re, s_im]
        return tuple(out)

    last = lax.fori_loop(0, span, local, (one, zero, zero, zero) * lanes, unroll=2)
    carries = []
    for j in range(lanes):
        p_re, p_im, s_re, s_im = last[4 * j : 4 * j + 4]
        c_re = c_im = jnp.zeros((1, LANE), F32)
        held = [None] * CHUNKS
        for k in reversed(range(CHUNKS)):
            held[k] = (c_re, c_im)
            q_re, q_im = p_re[k : k + 1], p_im[k : k + 1]
            c_re, c_im = (
                q_re * c_re - q_im * c_im + s_re[k : k + 1],
                q_re * c_im + q_im * c_re + s_im[k : k + 1],
            )
        carries.append(held)
    fix = 40
    for k in range(CHUNKS):

        def carry_in(i, _):
            at = pl.ds(pl.multiple_of(k * span + i * fix, 8), fix)
            for j in range(lanes):
                c_re, c_im = carries[j][k]
                p_re, p_im = a_re[j, at, :], a_im[j, at, :]
                b_re[j, at, :] += p_re * c_re - p_im * c_im
                b_im[j, at, :] += p_re * c_im + p_im * c_re
            return 0

        lax.fori_loop(0, span // fix, carry_in, 0)

    def finish(i, carry):
        before, total = carry
        at = pl.ds(pl.multiple_of(i * step, 16), step)
        g_re = jnp.concatenate([b_re[j, at, :] for j in range(lanes)], axis=1)
        g_im = jnp.concatenate([b_im[j, at, :] for j in range(lanes)], axis=1)
        now = st[at, :]
        prev = jnp.concatenate([before, now[:-1]], axis=0)
        q_re, q_im = prev[:, :half], prev[:, half:]
        dd_re, dd_im = g_re * q_re + g_im * q_im, g_im * q_re - g_re * q_im
        mag = sigmoid(pf[at, :half])
        forget = low + (1.0 - low) * mag
        cos, sin = phasor[at, :half], phasor[at, half:]
        x_re, x_im = pin[at, :half], pin[at, half:]
        sig_re, sig_im = sigmoid(x_re), sigmoid(x_im)
        inflow = 1.0 - forget
        d_forget = dd_re * cos + dd_im * sin - g_re * x_re * sig_re - g_im * x_im * sig_im
        gf[at, :half] = (d_forget * (1.0 - low) * mag * (1.0 - mag)).astype(gf.dtype)
        gf[at, half:] = (forget * (dd_im * cos - dd_re * sin)).astype(gf.dtype)
        gin[at, :half] = (g_re * inflow * sig_re * (1.0 + x_re * (1.0 - sig_re))).astype(gin.dtype)
        gin[at, half:] = (g_im * inflow * sig_im * (1.0 + x_im * (1.0 - sig_im))).astype(gin.dtype)
        total = total + jnp.sum((d_forget * (1.0 - mag)).reshape(step // 8, 8, half), axis=0)
        return now[step - 1 :], total

    first = (jnp.zeros((1, width), F32), jnp.zeros((8, half), F32))
    total = lax.fori_loop(0, rows // step, finish, first)[1]
    dbound[...] = jnp.sum(total, axis=0, keepdims=True) * low * (1.0 - low)


def call_local(body, outs, scratch, *args, name):
    return pl.pallas_call(
        body,
        out_shape=outs,
        scratch_shapes=scratch,
        compiler_params=pltpu.CompilerParams(vmem_limit_bytes=48 * 2**20),
        name=name,
    )(*args)


MESH_ID = pl.DeviceIdType.MESH
VMEM_LIMIT = 62 * 2**20
ANY = pl.BlockSpec(memory_space=pl.ANY)
VMEM = pl.BlockSpec(memory_space=pltpu.VMEM)


def remote(src, dst, send, recv, device):
    return pltpu.make_async_remote_copy(
        src_ref=src, dst_ref=dst, send_sem=send, recv_sem=recv, device_id=device, device_id_type=MESH_ID
    )


def load(src, dst, sem):
    copy = pltpu.make_async_copy(src, dst, sem)
    copy.start()
    return copy


def bounds(total, parts, unit):
    ends = [i * (total // unit) // parts * unit for i in range(parts)] + [total]
    return [(ends[i], ends[i + 1] - ends[i]) for i in range(parts)]


def subsets(masks):
    out = [0]
    for mask in masks:
        out += [sub | mask for sub in out]
    return out


class Place:
    def __init__(self, n_dp, n_mp):
        self.n_dp, self.n_mp = n_dp, n_mp
        self.d, self.m = lax.axis_index("dp"), lax.axis_index("mp")
        self.chips, self.bits = n_dp // 2, n_mp.bit_length() - 1
        self.k, self.c = lax.div(self.d, 2), lax.rem(self.d, 2)

    def twin(self):
        return (2 * self.k + 1 - self.c, self.m)

    def chip(self, step):
        return (self.d + 2 * step, self.m)

    def peer(self, mask):
        return (self.d, self.m ^ mask)

    def along(self, s):
        return (2 * lax.rem(self.k + s, self.chips) + self.c, self.m)

    def barrier(self, line=True, twin=True, far=False):
        sem = pltpu.get_barrier_semaphore()

        def greet(device):
            pl.semaphore_signal(sem, inc=1, device_id=device, device_id_type=MESH_ID)

        for mask in range(1, self.n_mp):
            greet(self.peer(mask))
        count = self.n_mp - 1
        if twin:
            greet(self.twin())
            count += 1
        if far:
            for s in range(1, self.chips):
                greet(self.along(s))
            count += self.chips - 1
        elif line:

            @pl.when(self.k > 0)
            def _():
                greet(self.chip(-1))

            @pl.when(self.k < self.chips - 1)
            def _():
                greet(self.chip(1))

            count += jnp.where(self.k > 0, 1, 0) + jnp.where(self.k < self.chips - 1, 1, 0)
        pl.semaphore_wait(sem, count)


class RowSum:
    @staticmethod
    def scratch(n_dp, blocks, rows, width):
        chips = n_dp // 2
        return [
            pltpu.VMEM((2, 2, rows, width), BF16),
            pltpu.VMEM((blocks, chips, rows, width), BF16),
            pltpu.VMEM((blocks, chips + 1, rows, width), BF16),
            pltpu.VMEM((rows, width), F32),
            pltpu.SemaphoreType.DMA((4, blocks, chips + 1)),
        ]

    def __init__(self, place, refs, piece, finish, skew):
        self.p = place
        self.out, self.summed, self.inbox, self.acc, self.sem = refs
        self.piece, self.finish = piece, finish
        self.blocks, self.skew = self.summed.shape[0], skew
        chips = place.chips
        self.steps = (self.blocks + chips - 1) * chips if skew else self.blocks * chips

    def order(self, i):
        chips = self.p.chips
        ok = (i >= 0) & (i < self.steps)
        i = jnp.clip(i, 0, self.steps - 1)
        if self.skew:
            t = lax.rem(i, chips)
            b = lax.div(i, chips) - t
            return t, jnp.clip(b, 0, self.blocks - 1), (b >= 0) & (b < self.blocks) & ok
        return lax.div(i, self.blocks), lax.rem(i, self.blocks), ok

    def targets(self, i):
        p = self.p
        t, b, ok = self.order(i)
        up, down = p.chips - 1 - t + p.k, p.k - (p.chips - 1) + t
        return b, up, ok & (up <= p.chips - 1), down, ok & (down >= 0) & (t < p.chips - 1), t == p.chips - 1

    def swap(self, b, e, ring):
        return remote(
            self.out.at[ring[0], ring[1]], self.summed.at[b, e], self.sem.at[0, b, e], self.sem.at[1, b, e],
            self.p.twin(),
        )

    def move(self, b, e, up):
        slot = e + 1 if up else e
        return remote(
            self.summed.at[b, e], self.inbox.at[b, slot], self.sem.at[2, b, e], self.sem.at[3, b, slot],
            self.p.chip(1 if up else -1),
        )

    def given(self, i):
        b, up, up_ok, down, down_ok, _ = self.targets(i)
        for side, e, ok in ((0, up, up_ok), (1, down, down_ok)):

            @pl.when(ok)
            def _():
                self.swap(b, e, (lax.rem(i + 2, 2), side)).wait_send()

    def give(self, i):
        self.given(i - 2)
        b, up, up_ok, down, down_ok, _ = self.targets(i)
        for side, e, ok in ((0, up, up_ok), (1, down, down_ok)):

            @pl.when(ok)
            def _():
                ring = (lax.rem(i, 2), side)
                self.out[ring[0], side] = self.piece(b, 2 * e + 1 - self.p.c).astype(BF16)
                self.swap(b, e, ring).start()

    def take(self, b, slot, up):
        e = slot - 1 if up else slot
        self.move(b, e, up).wait_recv()
        self.acc[...] += self.inbox[b, slot].astype(F32)

    def send(self, b, e, up):
        self.summed[b, e] = self.acc[...].astype(BF16)
        self.move(b, e, up).start()

    def work(self, i):
        p = self.p
        b, up, up_ok, down, down_ok, last = self.targets(i)

        def begin(e):
            own = self.piece(b, 2 * e + p.c)
            self.swap(b, e, (0, 0)).wait_recv()
            self.acc[...] = own + self.summed[b, e].astype(F32)

        @pl.when(up_ok)
        def _():
            begin(up)

            @pl.when(p.k > 0)
            def _():
                self.take(b, up + 1, True)

            @pl.when(jnp.logical_not(last))
            def _():
                self.send(b, up, True)

            @pl.when(last)
            def _():
                @pl.when(p.k < p.chips - 1)
                def _():
                    self.take(b, up, False)

                self.finish(b, self.acc)

        @pl.when(down_ok)
        def _():
            begin(down)

            @pl.when(p.k < p.chips - 1)
            def _():
                self.take(b, down, False)

            self.send(b, down, False)

    def run(self, lo, hi):
        if lo == 0:
            self.give(0)

        def body(i, _):
            self.give(i + 1)
            self.work(i)
            return 0

        lax.fori_loop(lo, hi, body, 0)
        if hi == self.steps:
            self.given(hi - 1)

    def drain(self):
        p = self.p

        def body(e, _):
            for b in range(self.blocks):

                @pl.when(e > p.k)
                def _():
                    self.move(b, e, True).wait_send()

                @pl.when(e < p.k)
                def _():
                    self.move(b, e, False).wait_send()

            return 0

        lax.fori_loop(0, p.chips, body, 0)


class CubeSum:
    @staticmethod
    def scratch(n_mp, rows, width):
        bits = n_mp.bit_length() - 1
        most = max(size for _, size in bounds(width, bits, LANE))
        return [
            pltpu.VMEM((bits, n_mp - 1, rows, most), BF16),
            pltpu.VMEM((bits, n_mp - 1, rows, most), BF16),
            pltpu.SemaphoreType.DMA((2, bits, n_mp - 1)),
        ]

    def __init__(self, place, refs, partial, width):
        self.p = place
        self.out, self.inbox, self.sem = refs
        self.partial = partial
        bits = place.bits
        self.cols = bounds(width, bits, LANE)
        self.slots, self.masks = {}, {}
        for part in range(bits):
            used = 0
            for s in range(bits):
                subs = subsets([1 << ((part + r) % bits) for r in range(s + 1, bits)])
                self.masks[part, s] = (1 << ((part + s) % bits), subs)
                for sub in subs:
                    self.slots[part, s, sub] = used
                    used += 1

    def copy(self, part, s, sub):
        slot, size = self.slots[part, s, sub], self.cols[part][1]
        return remote(
            self.out.at[part, slot, :, :size], self.inbox.at[part, slot, :, :size],
            self.sem.at[0, part, slot], self.sem.at[1, part, slot],
            self.p.peer(self.masks[part, s][0]),
        )

    def arrived(self, part, s, sub):
        self.copy(part, s, sub).wait_recv()
        return self.inbox[part, self.slots[part, s, sub], :, : self.cols[part][1]].astype(F32)

    def stage(self, s):
        for part in range(self.p.bits):
            bit, subs = self.masks[part, s]
            for sub in subs:
                value = self.partial(self.p.m ^ (bit | sub), part)
                for r in range(s):
                    value = value + self.arrived(part, r, bit | sub)
                self.out[part, self.slots[part, s, sub], :, : self.cols[part][1]] = value.astype(BF16)
                self.copy(part, s, sub).start()

    def result(self, part):
        value = self.partial(self.p.m, part)
        for s in range(self.p.bits):
            value = value + self.arrived(part, s, 0)
        return value

    def drain(self):
        for part, s, sub in self.slots:
            self.copy(part, s, sub).wait_send()


class CubeGather:
    @staticmethod
    def scratch(n_mp):
        bits = n_mp.bit_length() - 1
        return [pltpu.SemaphoreType.DMA((bits, n_mp)), pltpu.SemaphoreType.DMA((bits, n_mp))]

    def __init__(self, place, refs, view):
        self.p, self.view = place, view
        self.send, self.recv = refs
        bits = place.bits
        self.sends = {}
        for part in range(bits):
            for s in range(bits):
                earlier = [1 << ((part + r) % bits) for r in range(s)]
                for sub in subsets(earlier):
                    self.sends[part, s, sub] = (1 << ((part + s) % bits), sub)

    def copy(self, part, bit, sub):
        p = self.p
        ref = self.view(p.m ^ sub, part)
        return remote(ref, ref, self.send.at[part, bit | sub], self.recv.at[part, p.m ^ sub], p.peer(bit))

    def arrived(self, part, sub):
        p = self.p
        ref = self.view(p.m ^ sub, part)
        remote(ref, ref, self.send.at[part, sub], self.recv.at[part, p.m ^ sub], p.peer(sub)).wait_recv()

    def stage(self, s):
        for (part, at, sub), (bit, _) in self.sends.items():
            if at == s:
                if sub:
                    self.arrived(part, sub)
                self.copy(part, bit, sub).start()

    def last(self):
        p = self.p
        for part in range(p.bits):
            final = 1 << ((part + p.bits - 1) % p.bits)
            for sub in range(1, p.n_mp):
                if sub & final:
                    self.arrived(part, sub)

    def drain(self):
        for (part, _, sub), (bit, _) in self.sends.items():
            self.copy(part, bit, sub).wait_send()


class SmallSum:
    @staticmethod
    def scratch(n_dp, n_mp, shape):
        slots = 3 + n_mp + n_dp // 2
        return [pltpu.VMEM((slots, *shape), F32), pltpu.SemaphoreType.DMA((2, slots))]

    def __init__(self, place, refs):
        self.p = place
        self.buf, self.sem = refs

    def start(self, src, dst, device):
        remote(self.buf.at[src], self.buf.at[dst], self.sem.at[0, dst], self.sem.at[1, dst], device).start()

    def wait(self, dst):
        copy = remote(self.buf.at[dst], self.buf.at[dst], self.sem.at[0, dst], self.sem.at[1, dst], self.p.twin())
        copy.wait_recv()

    def sent(self, dst):
        copy = remote(self.buf.at[dst], self.buf.at[dst], self.sem.at[0, dst], self.sem.at[1, dst], self.p.twin())
        copy.wait_send()

    def twins(self):
        self.start(0, 1, self.p.twin())

    def cube(self):
        p = self.p
        self.wait(1)
        self.buf[2] = self.buf[0] + self.buf[1]
        for mask in range(1, p.n_mp):
            self.start(2, 3 + mask, p.peer(mask))

    def line(self):
        p = self.p
        for mask in range(1, p.n_mp):
            self.wait(3 + mask)
        total = 0.0
        for q in range(p.n_mp):
            mask = p.m ^ q
            total = total + self.buf[jnp.where(mask == 0, 2, 3 + mask)]
        self.buf[3] = total
        for s in range(1, p.chips):
            self.start(3, 3 + p.n_mp + s, p.along(s))

    def result(self):
        p = self.p
        total = self.buf[3]
        for s in range(1, p.chips):
            self.wait(3 + p.n_mp + s)
            total = total + self.buf[3 + p.n_mp + s]
        for dst in [1, *range(4, 3 + p.n_mp), *range(4 + p.n_mp, 3 + p.n_mp + p.chips)]:
            self.sent(dst)
        return total


def gather_kernel(n_dp, n_mp, mine, whole, lsem, send, recv):
    p = Place(n_dp, n_mp)
    p.barrier(line=False, twin=False)
    own = load(mine, whole.at[p.m], lsem)
    for mask in range(1, n_mp):
        remote(mine, whole.at[p.m], send.at[mask], recv.at[p.m], p.peer(mask)).start()
    own.wait()
    for mask in range(1, n_mp):
        remote(mine, whole.at[p.m ^ mask], send.at[mask], recv.at[p.m ^ mask], p.peer(mask)).wait()


def gather_mp(n_dp, n_mp, cid, x):
    return pl.pallas_call(
        functools.partial(gather_kernel, n_dp, n_mp),
        out_shape=jax.ShapeDtypeStruct((n_mp, *x.shape), x.dtype),
        in_specs=[ANY],
        out_specs=ANY,
        scratch_shapes=[
            pltpu.SemaphoreType.DMA,
            pltpu.SemaphoreType.DMA((n_mp,)),
            pltpu.SemaphoreType.DMA((n_mp,)),
        ],
        compiler_params=pltpu.CompilerParams(collective_id=cid, has_side_effects=True),
        name="gather_mp",
    )(x)


def mixer_kernel(
    n_dp, n_mp, normed, w, tokens, starts, bl, gain, gain_ffn,
    pin_o, pf_o, pg_o, st_o, phasor_o, r_o, mix_o, ffn_o, mid_o, rmid_o, wm_o,
    x, wv, pin, pf, pg, st, phasor, rowsq, a_re, a_im, b_re, b_im, mix, wm, tok, ffn_v, mid_v, rs_out, rs_in,
    lsem, osem, rs_sem, wtwin, *gsems,
):
    p = Place(n_dp, n_mp)
    rows, width = normed.shape
    mine = pin.shape[1]
    half, ch = width // 2, mine // 2
    own = rows // n_mp
    hw = width // 2
    row_parts = bounds(hw, p.bits, 16)

    def mix_view(q, part):
        lo, size = row_parts[part]
        return wm.at[pl.ds(pl.multiple_of(p.c * hw + lo, 16), size), pl.ds(pl.multiple_of(q * mine, LANE), mine)]

    loads = [load(normed, x, lsem.at[0])]
    loads += [load(w.at[:, i * mine : (i + 1) * mine], wv.at[i], lsem.at[1 + i]) for i in range(3)]
    own_mix = load(
        w.at[pl.ds(pl.multiple_of(p.c * hw, 16), hw), 3 * mine : 4 * mine],
        wm.at[pl.ds(pl.multiple_of(p.c * hw, 16), hw), pl.ds(pl.multiple_of(p.m * mine, LANE), mine)],
        lsem.at[4],
    )
    tok_load = load(tokens, tok, lsem.at[5])
    p.barrier(line=False)
    gw = CubeGather(p, gsems[0:2], mix_view)

    def to_twin(part, sub):
        ref = mix_view(p.m ^ sub, part)
        return remote(ref, ref, wtwin.at[0, part, sub], wtwin.at[1, part, sub], p.twin())

    def from_twin(part, sub):
        lo, size = row_parts[part]
        ref = wm.at[
            pl.ds(pl.multiple_of((1 - p.c) * hw + lo, 16), size),
            pl.ds(pl.multiple_of((p.m ^ sub) * mine, LANE), mine),
        ]
        return remote(ref, ref, wtwin.at[0, part, sub], wtwin.at[1, part, sub], p.twin())

    own_mix.wait()
    gw.stage(0)
    for part in range(p.bits):
        to_twin(part, 0).start()
    for copy in loads:
        copy.wait()
    step = 240

    def project(i, _):
        at = pl.ds(pl.multiple_of(i * step, 16), step)
        pin[at, :] = dot(x[at, :], wv[0])
        pf[at, :] = dot(x[at, :], wv[1])
        pg[at, :] = dot(x[at, :], wv[2])
        return 0

    lax.fori_loop(0, rows // step, project, 0)
    for s in range(1, p.bits):
        gw.stage(s)
    scan_forward(pin, pf, starts, bl, st, phasor, rowsq, a_re, a_im, b_re, b_im)
    outs = [
        load(src, dst, osem.at[i])
        for i, (src, dst) in enumerate(((pin, pin_o), (pf, pf_o), (pg, pg_o), (st, st_o), (phasor, phasor_o)))
    ]
    ones = jnp.ones((8, mine), F32)
    rs_out[...] = lax.dot_general(
        ones, st[...] * st[...], (((1,), (1,)), ((), ())), precision=lax.Precision.HIGHEST, preferred_element_type=F32
    )

    def rs_copy(mask):
        return remote(rs_out, rs_in.at[mask], rs_sem.at[0, mask], rs_sem.at[1, mask], p.peer(mask))

    for mask in range(1, n_mp):
        rs_copy(mask).start()
    total = rs_out[...]
    for mask in range(1, n_mp):
        rs_copy(mask).wait_recv()
        total = total + rs_in[mask]
    inv = lax.rsqrt(total / width + EPS)
    eighth = jnp.full((8, LANE), 0.125, F32)
    rowsq[...] = lax.dot_general(
        inv, eighth, (((0,), (0,)), ((), ())), precision=lax.Precision.HIGHEST, preferred_element_type=F32
    )[:, :1]
    outs.append(load(rowsq, r_o, osem.at[5]))
    fine = 48
    re_at = pl.ds(pl.multiple_of(p.m * ch, LANE), ch)
    im_at = pl.ds(pl.multiple_of(half + p.m * ch, LANE), ch)

    def gate_out(i, _):
        at = pl.ds(pl.multiple_of(i * fine, 16), fine)
        gate = pg[at, :]
        value = (st[at, :] * rowsq[at, :] * gain[...] * (gate * sigmoid(gate))).astype(BF16)
        mix[at, re_at] = value[:, :ch]
        mix[at, im_at] = value[:, ch:]
        return 0

    spans = 2
    span = rows // spans
    gathers = []
    for n in range(spans):
        lax.fori_loop(n * span // fine, (n + 1) * span // fine, gate_out, 0)
        for side in range(2):

            def view(q, part, n=n, side=side):
                lo, size = bounds(span, p.bits, 16)[part]
                return mix.at[n * span + lo : n * span + lo + size, pl.ds(pl.multiple_of(side * half + q * ch, LANE), ch)]

            at = 2 + 2 * (2 * n + side)
            gathers.append(CubeGather(p, gsems[at : at + 2], view))
            gathers[-1].stage(0)
    gw.last()
    for part in range(p.bits):
        for sub in range(1, n_mp):
            to_twin(part, sub).start()
    for s in range(1, p.bits):
        for g in gathers:
            g.stage(s)
    tok_load.wait()
    for part in range(p.bits):
        for sub in range(n_mp):
            from_twin(part, sub).wait_recv()
    outs.append(load(wm, wm_o, osem.at[6]))
    for n in range(spans):
        gathers[2 * n].last()
        gathers[2 * n + 1].last()

        def mix_rows(i, _):
            at = pl.ds(pl.multiple_of(i * step, 16), step)
            middle = tok[at, :].astype(F32) + dot(mix[at, :], wm[...])
            r = lax.rsqrt(jnp.mean(middle * middle, axis=-1, keepdims=True) + EPS)
            ffn_v[at, :] = (middle * r * gain_ffn[...]).astype(BF16)
            for j in range(step // own):

                @pl.when(p.m == i * (step // own) + j)
                def _():
                    mid_v[...] = middle[j * own : (j + 1) * own]
                    rmid_o[...] = r[j * own : (j + 1) * own]

            return 0

        lax.fori_loop(n * span // step, (n + 1) * span // step, mix_rows, 0)
        rows_at = slice(n * span, (n + 1) * span)
        outs.append(load(ffn_v.at[rows_at], ffn_o.at[rows_at], osem.at[7 + 2 * n]))
        outs.append(load(mix.at[rows_at], mix_o.at[rows_at], osem.at[8 + 2 * n]))
    outs.append(load(mid_v, mid_o, osem.at[7 + 2 * spans]))
    for copy in outs:
        copy.wait()
    gw.drain()
    for g in gathers:
        g.drain()
    for part in range(p.bits):
        for sub in range(n_mp):
            to_twin(part, sub).wait_send()
    for mask in range(1, n_mp):
        rs_copy(mask).wait_send()


def mixer_forward(n_dp, n_mp, cid, normed, w, tokens, starts, bl, gain, gain_ffn):
    rows, width = normed.shape
    mine = w.shape[1] // 4
    own, lanes = rows // n_mp, mine // 2 // LANE
    bits = n_mp.bit_length() - 1
    full, part, lane = (rows, width), (rows, mine), (lanes, rows, LANE)
    return pl.pallas_call(
        functools.partial(mixer_kernel, n_dp, n_mp),
        out_shape=(
            *(jax.ShapeDtypeStruct(part, F32),) * 5,
            jax.ShapeDtypeStruct((rows, 1), F32),
            jax.ShapeDtypeStruct(full, BF16),
            jax.ShapeDtypeStruct(full, BF16),
            jax.ShapeDtypeStruct((own, width), F32),
            jax.ShapeDtypeStruct((own, 1), F32),
            jax.ShapeDtypeStruct((width, width), BF16),
        ),
        in_specs=[ANY] * 3 + [VMEM] * 4,
        out_specs=(ANY,) * 9 + (VMEM, ANY),
        scratch_shapes=[
            pltpu.VMEM(full, BF16),
            pltpu.VMEM((3, width, mine), BF16),
            *[pltpu.VMEM(part, F32)] * 5,
            pltpu.VMEM((rows, 1), F32),
            *[pltpu.VMEM(lane, F32)] * 4,
            pltpu.VMEM(full, BF16),
            pltpu.VMEM((width, width), BF16),
            pltpu.VMEM(full, BF16),
            pltpu.VMEM(full, BF16),
            pltpu.VMEM((own, width), F32),
            pltpu.VMEM((8, rows), F32),
            pltpu.VMEM((n_mp, 8, rows), F32),
            pltpu.SemaphoreType.DMA((6,)),
            pltpu.SemaphoreType.DMA((12,)),
            pltpu.SemaphoreType.DMA((2, n_mp)),
            pltpu.SemaphoreType.DMA((2, bits, n_mp)),
            *CubeGather.scratch(n_mp) * 5,
        ],
        compiler_params=pltpu.CompilerParams(collective_id=cid, has_side_effects=True, vmem_limit_bytes=VMEM_LIMIT),
        name="mixer_forward",
    )(normed, w, tokens, starts, bl, gain, gain_ffn)


def ffn_kernel(n_dp, n_mp, final, ffn_in, grad_out, w, *refs):
    p = Place(n_dp, n_mp)
    rows, width = ffn_in.shape
    own = rows // n_mp
    if final:
        gffn1, down1, middle, r_mid, cot, tok, gain_ffn, w_mix, gsum, mixed, gmid, gain_part, gm, gb, rowdot = refs[:15]
        refs = refs[15:]
    else:
        gsum, gffn, down = refs[:3]
        refs = refs[3:]
    a, wv, bv, bq, lsem, gsem = refs[:6]
    sums, cube_g = refs[6:11], refs[11:14]
    cube_d = (cube_g[0], *refs[14:16])
    refs = refs[16:]
    h = bv.shape[2]
    shard = gsum.shape[1]
    loads = [load(ffn_in, a.at[0], lsem.at[0])]
    loads += [load(w.at[:, b * h : (b + 1) * h], wv.at[b], lsem.at[1 + b]) for b in range(3)]
    loads += [load(grad_out, a.at[1], lsem.at[4])]
    if final:
        gffn, mid_v, cot_v, tok_v, wmb, gbr, gm_out, gm_in, gb_in, rd_out, rd_in, wsem, ssem, rsem = refs
        late = [load(src, dst, lsem.at[5 + i]) for i, (src, dst) in enumerate(((middle, mid_v), (cot, cot_v), (tok, tok_v), (gffn1, gffn)))]
        mine = gm.shape[2]
        half, ch = width // 2, mine // 2

        def mix_load(j, s):
            q = p.m ^ j
            return pltpu.make_async_copy(
                w_mix.at[pl.ds(pl.multiple_of(s * half + q * ch, LANE), ch)], wmb.at[s], wsem.at[s]
            )

    p.barrier()
    for copy in loads:
        copy.wait()
    step = 240

    def forward(i, _):
        at = pl.ds(pl.multiple_of(i * step, 16), step)
        gate = dot(a[0, at, :], wv[0])
        up = dot(a[0, at, :], wv[1])
        sig = sigmoid(gate)
        silu = gate * sig
        grad = dot(a[1, at, :], wv[2])
        values = (grad * up * sig * (1.0 + gate * (1.0 - sig)), grad * silu, silu * up)
        for b in range(3):
            bv[b, at, :] = values[b].astype(BF16)
            if own % 16:
                for j in range(step // own):
                    bq[b, i * (step // own) + j] = values[b][j * own : (j + 1) * own].astype(BF16)
        return 0

    lax.fori_loop(0, rows // step, forward, 0)
    cols = bounds(width, p.bits, LANE)

    def rows_of(b, q):
        return bq[b, q] if own % 16 else bv[b, pl.ds(pl.multiple_of(q * own, 16), own), :]

    def part_g(q, part):
        lo, size = cols[part]
        at = slice(lo, lo + size)
        return dot_trans(rows_of(0, q), wv[0, at, :]) + dot_trans(rows_of(1, q), wv[1, at, :])

    def part_d(q, part):
        lo, size = cols[part]
        return dot_trans(rows_of(2, q), wv[2, lo : lo + size, :])

    def piece(b, e):
        left = jnp.where(b < 2, 0, 1)
        return dot_rows(a[left, :, pl.ds(pl.multiple_of(e * shard, LANE), shard)], bv[b])

    def finish(b, acc):
        out = pltpu.make_async_copy(acc, gsum.at[b], gsem)
        out.start()
        out.wait()

    total = RowSum(p, sums, piece, finish, False)
    g_cube, d_cube = CubeSum(p, cube_g, part_g, width), CubeSum(p, cube_d, part_d, width)
    n, chips = total.blocks, p.chips
    g_cube.stage(0)
    total.run(0, n)
    for s in range(1, p.bits):
        g_cube.stage(s)
    if not final:
        g_cube.drain()
        d_cube.stage(0)
    total.run(n, 2 * n)
    if final:
        late[3].wait()
        g_cube.drain()
    for part, (lo, size) in enumerate(cols):
        value = g_cube.result(part)
        gffn[:, lo : lo + size] = gffn[:, lo : lo + size] + value if final else value
    if not final:
        for s in range(1, p.bits):
            d_cube.stage(s)
    else:
        for copy in late[:3]:
            copy.wait()
        mix_load(1, 0).start()
        fine = 48 if own % 48 == 0 else own

        def norm_back(i, gains):
            at = pl.ds(pl.multiple_of(i * fine, fine), fine)
            g = gffn[at, :]
            n_own = mid_v[at, :] * r_mid[at, :]
            gains = gains + jnp.sum((g * n_own).reshape(fine // 8, 8, width), axis=0)
            gn = g * gain_ffn[...]
            back = r_mid[at, :] * (gn - n_own * jnp.mean(gn * n_own, axis=-1, keepdims=True))
            grad = cot_v[at, :].astype(F32) + back
            gmid[at, :] = grad
            low = grad.astype(BF16)
            gbr[at, :] = low
            dots = jnp.mean(low.astype(F32) * (mid_v[at, :] - tok_v[at, :].astype(F32)), axis=-1, keepdims=True)
            rd_out[at, :] = jnp.broadcast_to(dots, (fine, LANE))
            return gains

        gains = lax.fori_loop(0, own // fine, norm_back, jnp.zeros((8, width), F32))
        gain_part[...] = jnp.sum(gains, axis=0, keepdims=True)

        def across(kind, j, owner):
            send, recv, to = ssem.at[kind, j], rsem.at[kind, owner], p.peer(j)
            if kind == 0:
                return remote(gm_out.at[j], gm_in.at[owner], send, recv, to)
            if kind == 1:
                return remote(rd_out, rd_in.at[owner], send, recv, to)
            here = pl.ds(pl.multiple_of((p.m ^ j) * mine, LANE), mine)
            return remote(gbr.at[:, here], gb_in.at[owner], send, recv, to)

        for j in range(1, n_mp):
            across(1, j, p.m).start()
        turns = [(j, s) for j in (*range(1, n_mp), 0) for s in range(2)]
        for at, (j, s) in enumerate(turns):
            mix_load(j, s).wait()
            if at + 1 < len(turns):
                mix_load(*turns[at + 1]).start()
            value = dot_trans(gbr[...], wmb[s]).astype(BF16)
            if j:
                gm_out[j, :, s * ch : (s + 1) * ch] = value
                if s:
                    across(0, j, p.m).start()
            else:
                gm_in[p.m, :, s * ch : (s + 1) * ch] = value
        for j in range(1, n_mp):
            across(2, j, p.m).start()
        gb_in[p.m] = gbr[:, pl.ds(pl.multiple_of(p.m * mine, LANE), mine)]
        rd_in[p.m] = rd_out[...]
        down_load = load(down1, gffn, lsem.at[9])
        d_cube.stage(0)
    total.run(2 * n, 3 * n)
    if final:
        for s in range(1, p.bits):
            d_cube.stage(s)
    total.run(3 * n, total.steps)
    if final:
        for j in range(1, n_mp):
            for kind in range(3):
                across(kind, j, p.m ^ j).wait_recv()
        back = [load(src, dst, lsem.at[10 + i]) for i, (src, dst) in enumerate(((gm_in, gm), (gb_in, gb), (rd_in, rowdot)))]
        down_load.wait()
        for part, (lo, size) in enumerate(cols):
            at = slice(lo, lo + size)
            mixed[:, at] = (mid_v[:, at] + gffn[:, at] + d_cube.result(part)).astype(BF16)
        for j in range(1, n_mp):
            for kind in range(3):
                across(kind, j, p.m).wait_send()
        for copy in back:
            copy.wait()
    else:
        for part, (lo, size) in enumerate(cols):
            down[:, lo : lo + size] = d_cube.result(part)
    d_cube.drain()
    total.drain()


def ffn_part(n_dp, n_mp, cid, ffn_in, grad_out, w, *rest):
    rows, width = ffn_in.shape
    h, shard, own = w.shape[1] // 3, width // n_dp, rows // n_mp
    mine = width // n_mp
    final = bool(rest)
    f_own = jax.ShapeDtypeStruct((own, width), F32)
    gsum = jax.ShapeDtypeStruct((3, shard, h), F32)
    scratch = [
        pltpu.VMEM((2, rows, width), BF16),
        pltpu.VMEM((3, width, h), BF16),
        pltpu.VMEM((3, rows, h), BF16),
        pltpu.VMEM((3, n_mp, own, h) if own % 16 else (1, 1, 16, LANE), BF16),
        pltpu.SemaphoreType.DMA((13,)),
        pltpu.SemaphoreType.DMA,
        *RowSum.scratch(n_dp, 3, shard, h),
        *CubeSum.scratch(n_mp, own, width),
        *CubeSum.scratch(n_mp, own, width)[1:],
    ]
    if final:
        piece = jax.ShapeDtypeStruct((n_mp, own, mine), BF16)
        outs = (
            gsum, jax.ShapeDtypeStruct((own, width), BF16), f_own, jax.ShapeDtypeStruct((1, width), F32),
            piece, piece, jax.ShapeDtypeStruct((n_mp, own, LANE), F32),
        )
        scratch += [
            pltpu.VMEM((own, width), F32),
            pltpu.VMEM((own, width), F32),
            pltpu.VMEM((own, width), BF16),
            pltpu.VMEM((own, width), BF16),
            pltpu.VMEM((2, mine // 2, width), BF16),
            pltpu.VMEM((own, width), BF16),
            *[pltpu.VMEM((n_mp, own, mine), BF16)] * 3,
            pltpu.VMEM((own, LANE), F32),
            pltpu.VMEM((n_mp, own, LANE), F32),
            pltpu.SemaphoreType.DMA((2,)),
            pltpu.SemaphoreType.DMA((3, n_mp)),
            pltpu.SemaphoreType.DMA((3, n_mp)),
        ]
        in_specs = [ANY] * 6 + [VMEM, ANY, ANY, VMEM, ANY]
    else:
        outs = (gsum, f_own, f_own)
        in_specs = [ANY] * 3
    return pl.pallas_call(
        functools.partial(ffn_kernel, n_dp, n_mp, final),
        out_shape=outs,
        in_specs=in_specs,
        out_specs=(ANY, VMEM, VMEM, VMEM, ANY, ANY, ANY)[: len(outs)],
        scratch_shapes=scratch,
        compiler_params=pltpu.CompilerParams(collective_id=cid, has_side_effects=True, vmem_limit_bytes=VMEM_LIMIT),
        name="ffn_last" if final else "ffn_first",
    )(ffn_in, grad_out, w, *rest)


def project_kernel(
    n_dp, n_mp, normed, mixed, g_in, g_f, g_g, g_b, g_split, w, gmid, tok, r_in, gain_in, gain_ffn_part, dgain, dbound,
    gw, gtok, small, a, bv, bq, wv, lsem, rsend, rrecv, gall, *refs,
):
    p = Place(n_dp, n_mp)
    rows, width = normed.shape
    mine = bv.shape[2]
    half, ch, own = width // 2, mine // 2, rows // n_mp
    shard = gw.shape[2]
    sums, cube_refs, vec = refs[:5], refs[5:8], SmallSum(p, refs[8:10])
    loads = [load(normed, a.at[0], lsem.at[0])]
    loads += [load(src, bv.at[i], lsem.at[1 + i]) for i, src in enumerate((g_in, g_f, g_g, g_b))]
    loads += [load(mixed, a.at[1], lsem.at[5])]
    late = [load(w.at[:, i * mine : (i + 1) * mine], wv.at[i], lsem.at[6 + i]) for i in range(3)]
    if own % 16:
        late.append(load(g_split, bq, lsem.at[9]))
    p.barrier(far=True)
    for copy in loads:
        copy.wait()

    def piece(b, e):
        left = jnp.where(b < 3, 0, 1)
        return dot_rows(a[left, :, pl.ds(pl.multiple_of(e * shard, LANE), shard)], bv[b])

    def out_copy(b, mask, owner):
        return remote(gall.at[b, owner], gall.at[b, owner], rsend.at[b, mask], rrecv.at[b, owner], p.peer(mask))

    def finish(b, acc):
        gall[b, p.m] = acc[...].astype(BF16)
        for mask in range(1, n_mp):
            out_copy(b, mask, p.m).start()

    cols = bounds(width, p.bits, LANE)

    def partial(q, part):
        lo, size = cols[part]
        value = 0.0
        for b in range(3):
            left = bq[b, q] if own % 16 else bv[b, pl.ds(pl.multiple_of(q * own, 16), own), :]
            value = value + dot_trans(left, wv[b, lo : lo + size, :])
        return value

    total = RowSum(p, sums, piece, finish, True)
    cube = CubeSum(p, cube_refs, partial, width)
    tick = p.chips
    total.run(0, tick)
    for copy in late:
        copy.wait()
    cube.stage(0)
    total.run(tick, 2 * tick)
    for s in range(1, p.bits):
        cube.stage(s)
    total.run(2 * tick, 3 * tick)
    for part, (lo, size) in enumerate(cols):
        gtok[:, lo : lo + size] = cube.result(part)
    fine = 48 if own % 48 == 0 else own

    def norm_back(i, gains):
        at = pl.ds(pl.multiple_of(i * fine, fine), fine)
        g = gtok[at, :]
        n_own = tok[at, :].astype(F32) * r_in[at, :]
        gains = gains + jnp.sum((g * n_own).reshape(fine // 8, 8, width), axis=0)
        gn = g * gain_in[...]
        gtok[at, :] = gmid[at, :] + r_in[at, :] * (gn - n_own * jnp.mean(gn * n_own, axis=-1, keepdims=True))
        return gains

    gains = lax.fori_loop(0, own // fine, norm_back, jnp.zeros((8, width), F32))
    vec.buf[0] = jnp.zeros((4, width), F32)
    vec.buf[0, 0:1] = jnp.sum(gains, axis=0, keepdims=True)
    vec.buf[0, 1:2] = gain_ffn_part[...]
    here = pl.ds(pl.multiple_of(p.m * ch, LANE), ch)
    vec.buf[0, 2:3, here] = dgain[:, :ch]
    vec.buf[0, 2:3, pl.ds(pl.multiple_of(half + p.m * ch, LANE), ch)] = dgain[:, ch:]
    vec.buf[0, 3:4, here] = dbound[...]
    vec.twins()
    total.run(3 * tick, 4 * tick)
    vec.cube()
    total.run(4 * tick, 5 * tick)
    vec.line()
    total.run(5 * tick, total.steps)
    for b in range(4):
        for mask in range(1, n_mp):
            out_copy(b, mask, p.m ^ mask).wait_recv()
    out = load(gall, gw, lsem.at[10])
    small[...] = vec.result()
    out.wait()
    for b in range(4):
        for mask in range(1, n_mp):
            out_copy(b, mask, p.m).wait_send()
    cube.drain()
    total.drain()


def project_back(n_dp, n_mp, cid, normed, mixed, g_in, g_f, g_g, g_b, w, gmid, tok, r_in, gain_in, *vectors):
    rows, width = normed.shape
    mine, shard, own = g_in.shape[1], width // n_dp, rows // n_mp
    if own % 16:
        g_split = jnp.stack([g.reshape(n_mp, own, mine) for g in (g_in, g_f, g_g)])
    else:
        g_split = jnp.zeros((1, 1, 16, LANE), BF16)
    return pl.pallas_call(
        functools.partial(project_kernel, n_dp, n_mp),
        out_shape=(
            jax.ShapeDtypeStruct((4, n_mp, shard, mine), BF16),
            jax.ShapeDtypeStruct((own, width), F32),
            jax.ShapeDtypeStruct((4, width), F32),
        ),
        in_specs=[ANY] * 8 + [VMEM] * 7,
        out_specs=(ANY, VMEM, VMEM),
        scratch_shapes=[
            pltpu.VMEM((2, rows, width), BF16),
            pltpu.VMEM((4, rows, mine), BF16),
            pltpu.VMEM(g_split.shape, BF16),
            pltpu.VMEM((3, width, mine), BF16),
            pltpu.SemaphoreType.DMA((11,)),
            pltpu.SemaphoreType.DMA((4, n_mp)),
            pltpu.SemaphoreType.DMA((4, n_mp)),
            pltpu.VMEM((4, n_mp, shard, mine), BF16),
            *RowSum.scratch(n_dp, 4, shard, mine),
            *CubeSum.scratch(n_mp, own, width),
            *SmallSum.scratch(n_dp, n_mp, (4, width)),
        ],
        compiler_params=pltpu.CompilerParams(collective_id=cid, has_side_effects=True, vmem_limit_bytes=VMEM_LIMIT),
        name="project_back",
    )(normed, mixed, g_in, g_f, g_g, g_b, g_split, w, gmid, tok, r_in, gain_in, *vectors)


def per_device(n_dp, n_mp, tokens, segment_ids, cotangent, gain_in, w_in, w_forget, w_outgate, bound_logit, gain_mix,
               w_mix, gain_ffn, w_gate, w_up, w_down):
    m, d = lax.axis_index("mp"), lax.axis_index("dp")
    rows, width = tokens.shape
    half = bound_logit.shape[0]
    ch = half // n_mp
    mine = 2 * ch
    own = rows // n_mp
    ffn = w_gate.shape[1]
    padded = -(-ffn // LANE) * LANE
    cut = -(-padded // 2 // LANE) * LANE
    parts = ((0, cut), (cut, padded - cut))

    def cols(x, at, size):
        return lax.dynamic_slice_in_dim(x, at, size, 1)

    def own_channels(x):
        return jnp.concatenate([cols(x, m * ch, ch), cols(x, half + m * ch, ch)], axis=1)

    def own_rows(x):
        return lax.dynamic_slice_in_dim(x, m * own, own, 0)

    def gather_dp(x):
        return lax.all_gather(x, "dp", axis=0, tiled=True)

    w_cat = gather_dp(
        jnp.concatenate(
            [own_channels(w_in), own_channels(w_forget), own_channels(w_outgate), cols(w_mix, m * mine, mine)], axis=1
        )
    )
    fill = ((0, 0), (0, padded - ffn))
    gate_p, up_p, down_p = jnp.pad(w_gate, fill), jnp.pad(w_up, fill), jnp.pad(w_down.T, fill)
    w_ffn = []
    for lo, size in parts:
        at = slice(lo, lo + size)
        piece = jnp.concatenate([gate_p[:, at], up_p[:, at], down_p[:, at]], axis=1)
        w_ffn.append(gather_dp(piece))

    grad_out = gather_mp(n_dp, n_mp, 1, cotangent).reshape(rows, width)

    stream = tokens.astype(F32)
    ident = segment_ids[0]
    previous = jnp.concatenate([ident[:1] - 1, ident[:-1]])
    starts = jnp.where(ident != previous, 1.0, 0.0).astype(F32)[:, None]
    r_in = lax.rsqrt(jnp.mean(stream * stream, axis=-1, keepdims=True) + EPS)
    normed = (stream * r_in * gain_in).astype(BF16)
    bl = lax.dynamic_slice_in_dim(bound_logit, m * ch, ch, 0)[None]
    gain = own_channels(gain_mix[None])
    pin, pf, pg, st, phasor, r_mix, mixer_out, ffn_in, middle, r_mid, wm = mixer_forward(
        n_dp, n_mp, 2, normed, w_cat, tokens, starts, bl, gain, gain_ffn[None]
    )

    g_one, gffn, down = ffn_part(n_dp, n_mp, 3, ffn_in, grad_out, w_ffn[0])
    tok_own = own_rows(tokens)
    g_two, mixed, gmid, gain_ffn_part, gm, gb, rowdot = ffn_part(
        n_dp, n_mp, 4, ffn_in, grad_out, w_ffn[1], gffn, down, middle, r_mid, cotangent, tok_own, gain_ffn[None], wm
    )

    lanes = ch // LANE
    scratch = [pltpu.VMEM((lanes, rows, LANE), F32)] * 4
    gin, gf, gg, dgain, dbound = call_local(
        scan_backward,
        (
            jax.ShapeDtypeStruct((rows, mine), BF16),
            jax.ShapeDtypeStruct((rows, mine), BF16),
            jax.ShapeDtypeStruct((rows, mine), BF16),
            jax.ShapeDtypeStruct((1, mine), F32),
            jax.ShapeDtypeStruct((1, ch), F32),
        ),
        scratch,
        gm.reshape(rows, mine), pin, pf, pg, st, phasor, r_mix, rowdot.reshape(rows, LANE)[:, :1], bl, gain,
        name="scan_backward",
    )
    g_mixer, grad_tokens, small = project_back(
        n_dp, n_mp, 5, normed, mixer_out, gin, gf, gg, gb.reshape(rows, mine), w_cat, gmid, tok_own, own_rows(r_in),
        gain_in[None], gain_ffn_part, dgain, dbound,
    )

    def part_of(row, size):
        return lax.dynamic_slice_in_dim(small[row], d * (size // n_dp), size // n_dp, 0)

    g_mixer = g_mixer.astype(F32)

    def by_channel(g):
        return jnp.concatenate([g[q, :, lo : lo + ch] for lo in (0, ch) for q in range(n_mp)], axis=1)

    g_ffn = jnp.concatenate([g_one, g_two], axis=2)[:, :, :ffn]
    return (
        mixed,
        grad_tokens,
        part_of(0, width),
        by_channel(g_mixer[0]),
        by_channel(g_mixer[1]),
        by_channel(g_mixer[2]),
        part_of(3, half),
        part_of(2, width),
        jnp.concatenate([g_mixer[3, q] for q in range(n_mp)], axis=1),
        part_of(1, width),
        g_ffn[0],
        g_ffn[1],
        g_ffn[2].T,
    )


def solution(mesh):
    both, split = P(("dp", "mp"), None), P("dp", "mp")
    row, vec = P("dp", None), P("dp")
    return jax.shard_map(
        functools.partial(per_device, mesh.shape["dp"], mesh.shape["mp"]),
        mesh=mesh,
        in_specs=(row, row, both, P(), row, row, row, P(), P(), row, P(), split, split, P("mp", "dp")),
        out_specs=(both, both, vec, row, row, row, vec, vec, row, vec, split, split, P("mp", "dp")),
        check_vma=False,
    )
```

```python
import functools

import jax
import jax.numpy as jnp
from jax import lax
from jax.experimental import pallas as pl
from jax.experimental.pallas import tpu as pltpu
from jax.sharding import PartitionSpec as P

EPS = 1e-06
F32, BF16 = jnp.float32, jnp.bfloat16
LANE = 128
CHUNKS = 8


def dot(left, right):
    return jnp.dot(left, right, preferred_element_type=F32)


def dot_trans(left, right):
    return lax.dot_general(left, right, (((1,), (1,)), ((), ())), preferred_element_type=F32)


def dot_rows(left, right):
    return lax.dot_general(left, right, (((0,), (0,)), ((), ())), preferred_element_type=F32)


def sigmoid(v):
    return 1.0 / (1.0 + jnp.exp(-v))


def scan_forward(pin, pf, starts, bl, st, phasor, rowsq, a_re, a_im, b_re, b_im):
    rows, half = pin.shape[0], pin.shape[1] // 2
    span = rows // CHUNKS
    lanes = half // LANE
    low = sigmoid(bl[...])
    step = 48

    def prepare(i, _):
        at = pl.ds(pl.multiple_of(i * step, 8), step)
        forget = low + (1.0 - low) * sigmoid(pf[at, :half])
        phase = pf[at, half:]
        keep = 1.0 - starts[at, :]
        cos, sin = jnp.cos(phase) * keep, jnp.sin(phase) * keep
        phasor[at, :half] = cos
        phasor[at, half:] = sin
        x_re, x_im = pin[at, :half], pin[at, half:]
        inflow = 1.0 - forget
        in_re, in_im = x_re * sigmoid(x_re) * inflow, x_im * sigmoid(x_im) * inflow
        d_re, d_im = forget * cos, forget * sin
        for j in range(lanes):
            cut = slice(j * LANE, (j + 1) * LANE)
            a_re[j, at, :] = d_re[:, cut]
            a_im[j, at, :] = d_im[:, cut]
            b_re[j, at, :] = in_re[:, cut]
            b_im[j, at, :] = in_im[:, cut]
        return 0

    lax.fori_loop(0, rows // step, prepare, 0)
    zero, one = jnp.zeros((CHUNKS, LANE), F32), jnp.ones((CHUNKS, LANE), F32)

    def local(s, carry):
        at = pl.ds(s, CHUNKS, stride=span)
        out = []
        for j in range(lanes):
            p_re, p_im, s_re, s_im = carry[4 * j : 4 * j + 4]
            d_re, d_im = a_re.at[j][at, :], a_im.at[j][at, :]
            i_re, i_im = b_re.at[j][at, :], b_im.at[j][at, :]
            p_re, p_im = d_re * p_re - d_im * p_im, d_re * p_im + d_im * p_re
            s_re, s_im = d_re * s_re - d_im * s_im + i_re, d_re * s_im + d_im * s_re + i_im
            a_re.at[j][at, :] = p_re
            a_im.at[j][at, :] = p_im
            b_re.at[j][at, :] = s_re
            b_im.at[j][at, :] = s_im
            out += [p_re, p_im, s_re, s_im]
        return tuple(out)

    last = lax.fori_loop(0, span, local, (one, zero, zero, zero) * lanes, unroll=2)
    carries = []
    for j in range(lanes):
        p_re, p_im, s_re, s_im = last[4 * j : 4 * j + 4]
        c_re = c_im = jnp.zeros((1, LANE), F32)
        held = []
        for k in range(CHUNKS):
            held.append((c_re, c_im))
            q_re, q_im = p_re[k : k + 1], p_im[k : k + 1]
            c_re, c_im = (
                q_re * c_re - q_im * c_im + s_re[k : k + 1],
                q_re * c_im + q_im * c_re + s_im[k : k + 1],
            )
        carries.append(held)
    fix = 40
    for k in range(CHUNKS):

        def finish(i, _):
            at = pl.ds(pl.multiple_of(k * span + i * fix, 8), fix)
            total = jnp.zeros((fix, LANE), F32)
            for j in range(lanes):
                c_re, c_im = carries[j][k]
                p_re, p_im = a_re[j, at, :], a_im[j, at, :]
                s_re = b_re[j, at, :] + p_re * c_re - p_im * c_im
                s_im = b_im[j, at, :] + p_re * c_im + p_im * c_re
                st[at, j * LANE : (j + 1) * LANE] = s_re
                st[at, half + j * LANE : half + (j + 1) * LANE] = s_im
                total = total + s_re * s_re + s_im * s_im
            rowsq[at, :] = jnp.sum(total, axis=1, keepdims=True)
            return 0

        lax.fori_loop(0, span // fix, finish, 0)


def scan_backward(
    gm, pin, pf, pg, st, phasor, r, rowdot, bl, gain, gin, gf, gg, dgain, dbound, a_re, a_im, b_re, b_im
):
    rows, half = pin.shape[0], pin.shape[1] // 2
    width = 2 * half
    span = rows // CHUNKS
    lanes = half // LANE
    low = sigmoid(bl[...])
    step = 48

    def prepare(i, total):
        at = pl.ds(pl.multiple_of(i * step, 16), step)
        g, gate = gm[at, :], pg[at, :]
        sig = sigmoid(gate)
        silu = gate * sig
        n = st[at, :] * r[at, :]
        gs = g * silu
        gg[at, :] = (g * n * gain[...] * (sig * (1.0 + gate * (1.0 - sig)))).astype(gg.dtype)
        total = total + jnp.sum((gs * n).reshape(step // 8, 8, width), axis=0)
        d_st = r[at, :] * (gs * gain[...] - n * rowdot[at, :])
        forget = low + (1.0 - low) * sigmoid(pf[at, :half])
        d_re, d_im = forget * phasor[at, :half], forget * phasor[at, half:]
        for j in range(lanes):
            a_re[j, at, :] = d_re[:, j * LANE : (j + 1) * LANE]
            a_im[j, at, :] = d_im[:, j * LANE : (j + 1) * LANE]
            b_re[j, at, :] = d_st[:, j * LANE : (j + 1) * LANE]
            b_im[j, at, :] = d_st[:, half + j * LANE : half + (j + 1) * LANE]
        return total

    total = lax.fori_loop(0, rows // step, prepare, jnp.zeros((8, width), F32))
    dgain[...] = jnp.sum(total, axis=0, keepdims=True)
    zero, one = jnp.zeros((CHUNKS, LANE), F32), jnp.ones((CHUNKS, LANE), F32)

    def local(i, carry):
        at = pl.ds(span - 1 - i, CHUNKS, stride=span)
        out = []
        for j in range(lanes):
            p_re, p_im, s_re, s_im = carry[4 * j : 4 * j + 4]
            d_re, d_im = a_re.at[j][at, :], a_im.at[j][at, :]
            s_re, s_im = s_re + b_re.at[j][at, :], s_im + b_im.at[j][at, :]
            a_re.at[j][at, :] = p_re
            a_im.at[j][at, :] = p_im
            b_re.at[j][at, :] = s_re
            b_im.at[j][at, :] = s_im
            p_re, p_im = d_re * p_re + d_im * p_im, d_re * p_im - d_im * p_re
            s_re, s_im = d_re * s_re + d_im * s_im, d_re * s_im - d_im * s_re
            out += [p_re, p_im, s_re, s_im]
        return tuple(out)

    last = lax.fori_loop(0, span, local, (one, zero, zero, zero) * lanes, unroll=2)
    carries = []
    for j in range(lanes):
        p_re, p_im, s_re, s_im = last[4 * j : 4 * j + 4]
        c_re = c_im = jnp.zeros((1, LANE), F32)
        held = [None] * CHUNKS
        for k in reversed(range(CHUNKS)):
            held[k] = (c_re, c_im)
            q_re, q_im = p_re[k : k + 1], p_im[k : k + 1]
            c_re, c_im = (
                q_re * c_re - q_im * c_im + s_re[k : k + 1],
                q_re * c_im + q_im * c_re + s_im[k : k + 1],
            )
        carries.append(held)
    fix = 40
    for k in range(CHUNKS):

        def carry_in(i, _):
            at = pl.ds(pl.multiple_of(k * span + i * fix, 8), fix)
            for j in range(lanes):
                c_re, c_im = carries[j][k]
                p_re, p_im = a_re[j, at, :], a_im[j, at, :]
                b_re[j, at, :] += p_re * c_re - p_im * c_im
                b_im[j, at, :] += p_re * c_im + p_im * c_re
            return 0

        lax.fori_loop(0, span // fix, carry_in, 0)

    def finish(i, carry):
        before, total = carry
        at = pl.ds(pl.multiple_of(i * step, 16), step)
        g_re = jnp.concatenate([b_re[j, at, :] for j in range(lanes)], axis=1)
        g_im = jnp.concatenate([b_im[j, at, :] for j in range(lanes)], axis=1)
        now = st[at, :]
        prev = jnp.concatenate([before, now[:-1]], axis=0)
        q_re, q_im = prev[:, :half], prev[:, half:]
        dd_re, dd_im = g_re * q_re + g_im * q_im, g_im * q_re - g_re * q_im
        mag = sigmoid(pf[at, :half])
        forget = low + (1.0 - low) * mag
        cos, sin = phasor[at, :half], phasor[at, half:]
        x_re, x_im = pin[at, :half], pin[at, half:]
        sig_re, sig_im = sigmoid(x_re), sigmoid(x_im)
        inflow = 1.0 - forget
        d_forget = dd_re * cos + dd_im * sin - g_re * x_re * sig_re - g_im * x_im * sig_im
        gf[at, :half] = (d_forget * (1.0 - low) * mag * (1.0 - mag)).astype(gf.dtype)
        gf[at, half:] = (forget * (dd_im * cos - dd_re * sin)).astype(gf.dtype)
        gin[at, :half] = (g_re * inflow * sig_re * (1.0 + x_re * (1.0 - sig_re))).astype(gin.dtype)
        gin[at, half:] = (g_im * inflow * sig_im * (1.0 + x_im * (1.0 - sig_im))).astype(gin.dtype)
        total = total + jnp.sum((d_forget * (1.0 - mag)).reshape(step // 8, 8, half), axis=0)
        return now[step - 1 :], total

    first = (jnp.zeros((1, width), F32), jnp.zeros((8, half), F32))
    total = lax.fori_loop(0, rows // step, finish, first)[1]
    dbound[...] = jnp.sum(total, axis=0, keepdims=True) * low * (1.0 - low)


def call_local(body, outs, scratch, *args, name):
    return pl.pallas_call(
        body,
        out_shape=outs,
        scratch_shapes=scratch,
        compiler_params=pltpu.CompilerParams(vmem_limit_bytes=48 * 2**20),
        name=name,
    )(*args)


MESH_ID = pl.DeviceIdType.MESH
VMEM_LIMIT = 62 * 2**20
ANY = pl.BlockSpec(memory_space=pl.ANY)
VMEM = pl.BlockSpec(memory_space=pltpu.VMEM)


def remote(src, dst, send, recv, device):
    return pltpu.make_async_remote_copy(
        src_ref=src, dst_ref=dst, send_sem=send, recv_sem=recv, device_id=device, device_id_type=MESH_ID
    )


def load(src, dst, sem):
    copy = pltpu.make_async_copy(src, dst, sem)
    copy.start()
    return copy


def bounds(total, parts, unit):
    ends = [i * (total // unit) // parts * unit for i in range(parts)] + [total]
    return [(ends[i], ends[i + 1] - ends[i]) for i in range(parts)]


def subsets(masks):
    out = [0]
    for mask in masks:
        out += [sub | mask for sub in out]
    return out


class Place:
    def __init__(self, n_dp, n_mp):
        self.n_dp, self.n_mp = n_dp, n_mp
        self.d, self.m = lax.axis_index("dp"), lax.axis_index("mp")
        self.chips, self.bits = n_dp // 2, n_mp.bit_length() - 1
        self.k, self.c = lax.div(self.d, 2), lax.rem(self.d, 2)

    def twin(self):
        return (2 * self.k + 1 - self.c, self.m)

    def chip(self, step):
        return (self.d + 2 * step, self.m)

    def peer(self, mask):
        return (self.d, self.m ^ mask)

    def along(self, s):
        return (2 * lax.rem(self.k + s, self.chips) + self.c, self.m)

    def barrier(self, line=True, twin=True, far=False):
        sem = pltpu.get_barrier_semaphore()

        def greet(device):
            pl.semaphore_signal(sem, inc=1, device_id=device, device_id_type=MESH_ID)

        for mask in range(1, self.n_mp):
            greet(self.peer(mask))
        count = self.n_mp - 1
        if twin:
            greet(self.twin())
            count += 1
        if far:
            for s in range(1, self.chips):
                greet(self.along(s))
            count += self.chips - 1
        elif line:

            @pl.when(self.k > 0)
            def _():
                greet(self.chip(-1))

            @pl.when(self.k < self.chips - 1)
            def _():
                greet(self.chip(1))

            count += jnp.where(self.k > 0, 1, 0) + jnp.where(self.k < self.chips - 1, 1, 0)
        pl.semaphore_wait(sem, count)


class RowSum:
    @staticmethod
    def scratch(n_dp, blocks, rows, width):
        chips = n_dp // 2
        return [
            pltpu.VMEM((2, 2, rows, width), BF16),
            pltpu.VMEM((blocks, chips, rows, width), BF16),
            pltpu.VMEM((blocks, chips + 1, rows, width), BF16),
            pltpu.VMEM((rows, width), F32),
            pltpu.SemaphoreType.DMA((4, blocks, chips + 1)),
        ]

    def __init__(self, place, refs, piece, finish, skew):
        self.p = place
        self.out, self.summed, self.inbox, self.acc, self.sem = refs
        self.piece, self.finish = piece, finish
        self.blocks, self.skew = self.summed.shape[0], skew
        chips = place.chips
        self.steps = (self.blocks + chips - 1) * chips if skew else self.blocks * chips

    def order(self, i):
        chips = self.p.chips
        ok = (i >= 0) & (i < self.steps)
        i = jnp.clip(i, 0, self.steps - 1)
        if self.skew:
            t = lax.rem(i, chips)
            b = lax.div(i, chips) - t
            return t, jnp.clip(b, 0, self.blocks - 1), (b >= 0) & (b < self.blocks) & ok
        return lax.div(i, self.blocks), lax.rem(i, self.blocks), ok

    def targets(self, i):
        p = self.p
        t, b, ok = self.order(i)
        up, down = p.chips - 1 - t + p.k, p.k - (p.chips - 1) + t
        return b, up, ok & (up <= p.chips - 1), down, ok & (down >= 0) & (t < p.chips - 1), t == p.chips - 1

    def swap(self, b, e, ring):
        return remote(
            self.out.at[ring[0], ring[1]], self.summed.at[b, e], self.sem.at[0, b, e], self.sem.at[1, b, e],
            self.p.twin(),
        )

    def move(self, b, e, up):
        slot = e + 1 if up else e
        return remote(
            self.summed.at[b, e], self.inbox.at[b, slot], self.sem.at[2, b, e], self.sem.at[3, b, slot],
            self.p.chip(1 if up else -1),
        )

    def given(self, i):
        b, up, up_ok, down, down_ok, _ = self.targets(i)
        for side, e, ok in ((0, up, up_ok), (1, down, down_ok)):

            @pl.when(ok)
            def _():
                self.swap(b, e, (lax.rem(i + 2, 2), side)).wait_send()

    def give(self, i):
        self.given(i - 2)
        b, up, up_ok, down, down_ok, _ = self.targets(i)
        for side, e, ok in ((0, up, up_ok), (1, down, down_ok)):

            @pl.when(ok)
            def _():
                ring = (lax.rem(i, 2), side)
                self.out[ring[0], side] = self.piece(b, 2 * e + 1 - self.p.c).astype(BF16)
                self.swap(b, e, ring).start()

    def take(self, b, slot, up):
        e = slot - 1 if up else slot
        self.move(b, e, up).wait_recv()
        self.acc[...] += self.inbox[b, slot].astype(F32)

    def send(self, b, e, up):
        self.summed[b, e] = self.acc[...].astype(BF16)
        self.move(b, e, up).start()

    def work(self, i):
        p = self.p
        b, up, up_ok, down, down_ok, last = self.targets(i)

        def begin(e):
            own = self.piece(b, 2 * e + p.c)
            self.swap(b, e, (0, 0)).wait_recv()
            self.acc[...] = own + self.summed[b, e].astype(F32)

        @pl.when(up_ok)
        def _():
            begin(up)

            @pl.when(p.k > 0)
            def _():
                self.take(b, up + 1, True)

            @pl.when(jnp.logical_not(last))
            def _():
                self.send(b, up, True)

            @pl.when(last)
            def _():
                @pl.when(p.k < p.chips - 1)
                def _():
                    self.take(b, up, False)

                self.finish(b, self.acc)

        @pl.when(down_ok)
        def _():
            begin(down)

            @pl.when(p.k < p.chips - 1)
            def _():
                self.take(b, down, False)

            self.send(b, down, False)

    def run(self, lo, hi):
        if lo == 0:
            self.give(0)

        def body(i, _):
            self.give(i + 1)
            self.work(i)
            return 0

        lax.fori_loop(lo, hi, body, 0)
        if hi == self.steps:
            self.given(hi - 1)

    def drain(self):
        p = self.p

        def body(e, _):
            for b in range(self.blocks):

                @pl.when(e > p.k)
                def _():
                    self.move(b, e, True).wait_send()

                @pl.when(e < p.k)
                def _():
                    self.move(b, e, False).wait_send()

            return 0

        lax.fori_loop(0, p.chips, body, 0)


class CubeSum:
    @staticmethod
    def scratch(n_mp, rows, width):
        bits = n_mp.bit_length() - 1
        most = max(size for _, size in bounds(width, bits, LANE))
        return [
            pltpu.VMEM((bits, n_mp - 1, rows, most), BF16),
            pltpu.VMEM((bits, n_mp - 1, rows, most), BF16),
            pltpu.SemaphoreType.DMA((2, bits, n_mp - 1)),
        ]

    def __init__(self, place, refs, partial, width):
        self.p = place
        self.out, self.inbox, self.sem = refs
        self.partial = partial
        bits = place.bits
        self.cols = bounds(width, bits, LANE)
        self.slots, self.masks = {}, {}
        for part in range(bits):
            used = 0
            for s in range(bits):
                subs = subsets([1 << ((part + r) % bits) for r in range(s + 1, bits)])
                self.masks[part, s] = (1 << ((part + s) % bits), subs)
                for sub in subs:
                    self.slots[part, s, sub] = used
                    used += 1

    def copy(self, part, s, sub):
        slot, size = self.slots[part, s, sub], self.cols[part][1]
        return remote(
            self.out.at[part, slot, :, :size], self.inbox.at[part, slot, :, :size],
            self.sem.at[0, part, slot], self.sem.at[1, part, slot],
            self.p.peer(self.masks[part, s][0]),
        )

    def arrived(self, part, s, sub):
        self.copy(part, s, sub).wait_recv()
        return self.inbox[part, self.slots[part, s, sub], :, : self.cols[part][1]].astype(F32)

    def stage(self, s):
        for part in range(self.p.bits):
            bit, subs = self.masks[part, s]
            for sub in subs:
                value = self.partial(self.p.m ^ (bit | sub), part)
                for r in range(s):
                    value = value + self.arrived(part, r, bit | sub)
                self.out[part, self.slots[part, s, sub], :, : self.cols[part][1]] = value.astype(BF16)
                self.copy(part, s, sub).start()

    def result(self, part):
        value = self.partial(self.p.m, part)
        for s in range(self.p.bits):
            value = value + self.arrived(part, s, 0)
        return value

    def drain(self):
        for part, s, sub in self.slots:
            self.copy(part, s, sub).wait_send()


class CubeGather:
    @staticmethod
    def scratch(n_mp):
        bits = n_mp.bit_length() - 1
        return [pltpu.SemaphoreType.DMA((bits, n_mp)), pltpu.SemaphoreType.DMA((bits, n_mp))]

    def __init__(self, place, refs, view):
        self.p, self.view = place, view
        self.send, self.recv = refs
        bits = place.bits
        self.sends = {}
        for part in range(bits):
            for s in range(bits):
                earlier = [1 << ((part + r) % bits) for r in range(s)]
                for sub in subsets(earlier):
                    self.sends[part, s, sub] = (1 << ((part + s) % bits), sub)

    def copy(self, part, bit, sub):
        p = self.p
        ref = self.view(p.m ^ sub, part)
        return remote(ref, ref, self.send.at[part, bit | sub], self.recv.at[part, p.m ^ sub], p.peer(bit))

    def arrived(self, part, sub):
        p = self.p
        ref = self.view(p.m ^ sub, part)
        remote(ref, ref, self.send.at[part, sub], self.recv.at[part, p.m ^ sub], p.peer(sub)).wait_recv()

    def stage(self, s):
        for (part, at, sub), (bit, _) in self.sends.items():
            if at == s:
                if sub:
                    self.arrived(part, sub)
                self.copy(part, bit, sub).start()

    def last(self):
        p = self.p
        for part in range(p.bits):
            final = 1 << ((part + p.bits - 1) % p.bits)
            for sub in range(1, p.n_mp):
                if sub & final:
                    self.arrived(part, sub)

    def drain(self):
        for (part, _, sub), (bit, _) in self.sends.items():
            self.copy(part, bit, sub).wait_send()


class SmallSum:
    @staticmethod
    def scratch(n_dp, n_mp, shape):
        slots = 3 + n_mp + n_dp // 2
        return [pltpu.VMEM((slots, *shape), F32), pltpu.SemaphoreType.DMA((2, slots))]

    def __init__(self, place, refs):
        self.p = place
        self.buf, self.sem = refs

    def start(self, src, dst, device):
        remote(self.buf.at[src], self.buf.at[dst], self.sem.at[0, dst], self.sem.at[1, dst], device).start()

    def wait(self, dst):
        copy = remote(self.buf.at[dst], self.buf.at[dst], self.sem.at[0, dst], self.sem.at[1, dst], self.p.twin())
        copy.wait_recv()

    def sent(self, dst):
        copy = remote(self.buf.at[dst], self.buf.at[dst], self.sem.at[0, dst], self.sem.at[1, dst], self.p.twin())
        copy.wait_send()

    def twins(self):
        self.start(0, 1, self.p.twin())

    def cube(self):
        p = self.p
        self.wait(1)
        self.buf[2] = self.buf[0] + self.buf[1]
        for mask in range(1, p.n_mp):
            self.start(2, 3 + mask, p.peer(mask))

    def line(self):
        p = self.p
        for mask in range(1, p.n_mp):
            self.wait(3 + mask)
        total = 0.0
        for q in range(p.n_mp):
            mask = p.m ^ q
            total = total + self.buf[jnp.where(mask == 0, 2, 3 + mask)]
        self.buf[3] = total
        for s in range(1, p.chips):
            self.start(3, 3 + p.n_mp + s, p.along(s))

    def result(self):
        p = self.p
        total = self.buf[3]
        for s in range(1, p.chips):
            self.wait(3 + p.n_mp + s)
            total = total + self.buf[3 + p.n_mp + s]
        for dst in [1, *range(4, 3 + p.n_mp), *range(4 + p.n_mp, 3 + p.n_mp + p.chips)]:
            self.sent(dst)
        return total


class RowGather:
    @staticmethod
    def scratch(n_dp, units):
        return [pltpu.SemaphoreType.DMA((5, units, n_dp // 2))]

    def __init__(self, place, refs, src, dst):
        self.p, self.src, self.dst = place, src, dst
        (self.sem,) = refs

    def hop(self, u, e, side, own=False):
        p = self.p
        here = self.dst(u, e, p.c)
        device = (p.chip(1), p.chip(-1), p.twin())[side]
        recv = self.sem.at[4 if side == 2 else 3, u, e]
        return remote(self.src(u) if own else here, here, self.sem.at[side, u, e], recv, device)

    def start(self, u):
        p = self.p

        @pl.when(p.k < p.chips - 1)
        def _():
            self.hop(u, p.k, 0, True).start()

        @pl.when(p.k > 0)
        def _():
            self.hop(u, p.k, 1, True).start()

        self.hop(u, p.k, 2, True).start()

    def forward(self, u, s):
        p = self.p

        @pl.when(p.k - s >= 0)
        def _():
            self.hop(u, p.k - s, 0).wait_recv()

            @pl.when(p.k < p.chips - 1)
            def _():
                self.hop(u, p.k - s, 0).start()

            self.hop(u, p.k - s, 2).start()

        @pl.when(p.k + s < p.chips)
        def _():
            self.hop(u, p.k + s, 1).wait_recv()

            @pl.when(p.k > 0)
            def _():
                self.hop(u, p.k + s, 1).start()

            self.hop(u, p.k + s, 2).start()

    def finish(self, u):
        p = self.p
        for e in range(p.chips):
            there = self.dst(u, e, 1 - p.c)
            remote(there, there, self.sem.at[2, u, e], self.sem.at[4, u, e], p.twin()).wait_recv()

    def drain(self, u):
        p = self.p
        for e in range(p.chips):

            @pl.when((e <= p.k) & (p.k < p.chips - 1))
            def _():
                self.hop(u, e, 0).wait_send()

            @pl.when((e >= p.k) & (p.k > 0))
            def _():
                self.hop(u, e, 1).wait_send()

            self.hop(u, e, 2).wait_send()


def mixer_kernel(
    n_dp, n_mp, w_in, w_forget, w_outgate, w_mix, w_gate, w_up, w_down, cot, tokens, ident, bound, gain_mix, gain_in, gain_ffn,
    normed_o, rin_o, pin_o, pf_o, pg_o, st_o, phasor_o, r_o, mix_o, ffn_o, mid_o, rmid_o, wm_o, wcat_o, one_o, one_d, cot_o,
    x, wv, wq, pin, pf, pg, st, phasor, rowsq, rin, starts, bl, gain, a_re, a_im, b_re, b_im, mix, wm, tok, ffn_v, mid_v, rs_out, rs_in,
    lsem, osem, rs_sem, wtwin, csem, *gsems,
):
    p = Place(n_dp, n_mp)
    rows, width = tokens.shape
    mine = pin.shape[1]
    half, ch = width // 2, mine // 2
    own = rows // n_mp
    hw = width // 2
    shard, h = w_in.shape[0], one_o.shape[2]
    row_parts = bounds(hw, p.bits, 16)

    def mix_view(q, part):
        lo, size = row_parts[part]
        return wm.at[pl.ds(pl.multiple_of(p.c * hw + lo, 16), size), pl.ds(pl.multiple_of(q * mine, LANE), mine)]

    def rows_at(e, c):
        return pl.ds(pl.multiple_of((2 * e + c) * shard, 16), shard)

    def lanes_at(at, size):
        return pl.ds(pl.multiple_of(at, LANE), size)

    def unit_src(u):
        if u < 4:
            return unit_dst(u, p.k, p.c)
        return (w_gate.at[:, :h], w_up.at[:, :h], w_down.at[:h])[u - 4]

    def unit_dst(u, e, c):
        if u == 6:
            return one_d.at[:, lanes_at((2 * e + c) * shard, shard)]
        return (wv.at[u] if u < 3 else wq if u == 3 else one_o.at[u - 4]).at[rows_at(e, c)]

    mine_at = rows_at(p.k, p.c)
    keep = {3: [load(w_mix.at[:, lanes_at(p.m * mine, mine)], wq.at[mine_at], lsem.at[1])]}
    for u, w in enumerate((w_in, w_forget, w_outgate)):
        keep[u] = [
            load(w.at[:, lanes_at(side * half + p.m * ch, ch)], wv.at[u, mine_at, side * ch : (side + 1) * ch], lsem.at[2 + 2 * u + side])
            for side in range(2)
        ]
    tok_load = load(tokens, tok, lsem.at[0])
    vectors = [
        load(bound.at[:, lanes_at(p.m * ch, ch)], bl, lsem.at[10]),
        *[
            load(gain_mix.at[:, lanes_at(side * half + p.m * ch, ch)], gain.at[:, side * ch : (side + 1) * ch], lsem.at[11 + side])
            for side in range(2)
        ],
    ]
    first_own = [load(unit_src(u), unit_dst(u, p.k, p.c), lsem.at[9 + u]) for u in range(4, 7)]
    cot_own = load(cot, cot_o.at[p.m], lsem.at[8])
    p.barrier()
    z = RowGather(p, gsems[:1], unit_src, unit_dst)
    gsems = gsems[1:]
    order = (3, 0, 1, 2)
    for u in order:
        for copy in keep[u]:
            copy.wait()
        z.start(u)

    def cot_copy(mask, owner):
        return remote(cot, cot_o.at[owner], csem.at[0, mask], csem.at[1, owner], p.peer(mask))

    for mask in range(1, n_mp):
        cot_copy(mask, p.m).start()
    tok_load.wait()
    fine = 48

    def norm_in(i, _):
        at = pl.ds(pl.multiple_of(i * fine, 16), fine)
        v = tok[at, :].astype(F32)
        r = lax.rsqrt(jnp.mean(v * v, axis=-1, keepdims=True) + EPS)
        rin[at, :] = r
        x[at, :] = (v * r * gain_in[...]).astype(BF16)
        return 0

    lax.fori_loop(0, rows // fine, norm_in, 0)
    eighth = jnp.full((8, LANE), 0.125, F32)
    ids = lax.dot_general(
        jnp.broadcast_to(ident[...].astype(F32), (8, rows)), eighth, (((0,), (0,)), ((), ())),
        precision=lax.Precision.HIGHEST, preferred_element_type=F32,
    )[:, :1]
    before = jnp.concatenate([ids[:1] - 1.0, ids[:-1]], axis=0)
    starts[...] = jnp.where(jnp.abs(ids - before) > 0.5, 1.0, 0.0)
    for copy in vectors:
        copy.wait()
    outs = [load(x, normed_o, osem.at[0]), load(rin, rin_o, osem.at[1])]
    for s in range(1, p.chips - 1):
        for u in order:
            z.forward(u, s)
    for u in range(4, 7):
        z.start(u)
    z.forward(3, p.chips - 1)
    z.finish(3)
    own_mix = load(
        wq.at[pl.ds(pl.multiple_of(p.c * hw, 16), hw)],
        wm.at[pl.ds(pl.multiple_of(p.c * hw, 16), hw), pl.ds(pl.multiple_of(p.m * mine, LANE), mine)],
        lsem.at[9],
    )
    gw = CubeGather(p, gsems[0:2], mix_view)

    def to_twin(part, sub):
        ref = mix_view(p.m ^ sub, part)
        return remote(ref, ref, wtwin.at[0, part, sub], wtwin.at[1, part, sub], p.twin())

    def from_twin(part, sub):
        lo, size = row_parts[part]
        ref = wm.at[
            pl.ds(pl.multiple_of((1 - p.c) * hw + lo, 16), size),
            pl.ds(pl.multiple_of((p.m ^ sub) * mine, LANE), mine),
        ]
        return remote(ref, ref, wtwin.at[0, part, sub], wtwin.at[1, part, sub], p.twin())

    own_mix.wait()
    gw.stage(0)
    for part in range(p.bits):
        to_twin(part, 0).start()
    step = 240

    def project(u, out):
        z.forward(u, p.chips - 1)
        z.finish(u)

        def body(i, _):
            at = pl.ds(pl.multiple_of(i * step, 16), step)
            out[at, :] = dot(x[at, :], wv[u])
            return 0

        lax.fori_loop(0, rows // step, body, 0)

    project(0, pin)
    project(1, pf)
    project(2, pg)
    outs += [load(wv.at[u], wcat_o.at[u], osem.at[2 + u]) for u in range(3)]
    for s in range(1, p.bits):
        gw.stage(s)
    scan_forward(pin, pf, starts, bl, st, phasor, rowsq, a_re, a_im, b_re, b_im)
    outs += [
        load(src, dst, osem.at[5 + i])
        for i, (src, dst) in enumerate(((pin, pin_o), (pf, pf_o), (pg, pg_o), (st, st_o), (phasor, phasor_o)))
    ]
    ones = jnp.ones((8, mine), F32)
    rs_out[...] = lax.dot_general(
        ones, st[...] * st[...], (((1,), (1,)), ((), ())), precision=lax.Precision.HIGHEST, preferred_element_type=F32
    )

    def rs_copy(mask):
        return remote(rs_out, rs_in.at[mask], rs_sem.at[0, mask], rs_sem.at[1, mask], p.peer(mask))

    for mask in range(1, n_mp):
        rs_copy(mask).start()
    gw.last()
    for part in range(p.bits):
        for sub in range(1, n_mp):
            to_twin(part, sub).start()
    z.forward(4, 1)
    total = rs_out[...]
    for mask in range(1, n_mp):
        rs_copy(mask).wait_recv()
        total = total + rs_in[mask]
    inv = lax.rsqrt(total / width + EPS)
    rowsq[...] = lax.dot_general(
        inv, eighth, (((0,), (0,)), ((), ())), precision=lax.Precision.HIGHEST, preferred_element_type=F32
    )[:, :1]
    outs.append(load(rowsq, r_o, osem.at[10]))
    re_at = pl.ds(pl.multiple_of(p.m * ch, LANE), ch)
    im_at = pl.ds(pl.multiple_of(half + p.m * ch, LANE), ch)

    def gate_out(i, _):
        at = pl.ds(pl.multiple_of(i * fine, 16), fine)
        gate = pg[at, :]
        value = (st[at, :] * rowsq[at, :] * gain[...] * (gate * sigmoid(gate))).astype(BF16)
        mix[at, re_at] = value[:, :ch]
        mix[at, im_at] = value[:, ch:]
        return 0

    spans = 2
    span = rows // spans
    gathers = []
    for n in range(spans):
        lax.fori_loop(n * span // fine, (n + 1) * span // fine, gate_out, 0)
        for side in range(2):

            def view(q, part, n=n, side=side):
                lo, size = bounds(span, p.bits, 16)[part]
                return mix.at[n * span + lo : n * span + lo + size, pl.ds(pl.multiple_of(side * half + q * ch, LANE), ch)]

            at = 2 + 2 * (2 * n + side)
            gathers.append(CubeGather(p, gsems[at : at + 2], view))
            gathers[-1].stage(0)
    z.forward(5, 1)
    for s in range(1, p.bits):
        for g in gathers:
            g.stage(s)
    z.forward(6, 1)
    for part in range(p.bits):
        for sub in range(n_mp):
            from_twin(part, sub).wait_recv()
    outs.append(load(wm, wm_o, osem.at[11]))
    for n in range(spans):
        gathers[2 * n].last()
        gathers[2 * n + 1].last()

        def mix_rows(i, _):
            at = pl.ds(pl.multiple_of(i * step, 16), step)
            middle = tok[at, :].astype(F32) + dot(mix[at, :], wm[...])
            r = lax.rsqrt(jnp.mean(middle * middle, axis=-1, keepdims=True) + EPS)
            ffn_v[at, :] = (middle * r * gain_ffn[...]).astype(BF16)
            for j in range(step // own):

                @pl.when(p.m == i * (step // own) + j)
                def _():
                    mid_v[...] = middle[j * own : (j + 1) * own]
                    rmid_o[...] = r[j * own : (j + 1) * own]

            return 0

        lax.fori_loop(n * span // step, (n + 1) * span // step, mix_rows, 0)
        at = slice(n * span, (n + 1) * span)
        outs.append(load(ffn_v.at[at], ffn_o.at[at], osem.at[12 + 2 * n]))
        outs.append(load(mix.at[at], mix_o.at[at], osem.at[13 + 2 * n]))
        if n == 0:
            z.forward(4, 2)
    outs.append(load(mid_v, mid_o, osem.at[12 + 2 * spans]))
    z.forward(5, 2)
    z.forward(6, 2)
    for s in range(3, p.chips):
        for u in range(4, 7):
            z.forward(u, s)
    for u in range(4, 7):
        z.finish(u)
    for mask in range(1, n_mp):
        cot_copy(mask, p.m ^ mask).wait_recv()
    cot_own.wait()
    for copy in first_own:
        copy.wait()
    for copy in outs:
        copy.wait()
    for u in range(7):
        z.drain(u)
    gw.drain()
    for g in gathers:
        g.drain()
    for part in range(p.bits):
        for sub in range(n_mp):
            to_twin(part, sub).wait_send()
    for mask in range(1, n_mp):
        rs_copy(mask).wait_send()
        cot_copy(mask, p.m).wait_send()


def mixer_forward(n_dp, n_mp, cid, h, *args):
    rows, width = args[8].shape
    mine = width // n_mp
    own, lanes = rows // n_mp, mine // 2 // LANE
    bits = n_mp.bit_length() - 1
    full, part, lane = (rows, width), (rows, mine), (lanes, rows, LANE)

    def f32(*shape):
        return jax.ShapeDtypeStruct(shape, F32)

    def bf16(*shape):
        return jax.ShapeDtypeStruct(shape, BF16)

    return pl.pallas_call(
        functools.partial(mixer_kernel, n_dp, n_mp),
        out_shape=(
            bf16(*full), f32(rows, 1), *(f32(*part),) * 5, f32(rows, 1), bf16(*full), bf16(*full), f32(own, width), f32(own, 1),
            bf16(width, width), bf16(3, width, mine), bf16(2, width, h), bf16(h, width), bf16(n_mp, own, width),
        ),
        in_specs=[ANY] * 9 + [VMEM] + [ANY] * 2 + [VMEM] * 2,
        out_specs=(ANY,) * 11 + (VMEM,) + (ANY,) * 5,
        scratch_shapes=[
            pltpu.VMEM(full, BF16),
            pltpu.VMEM((3, width, mine), BF16),
            pltpu.VMEM((width, mine), BF16),
            *[pltpu.VMEM(part, F32)] * 5,
            *[pltpu.VMEM((rows, 1), F32)] * 3,
            pltpu.VMEM((1, mine // 2), F32),
            pltpu.VMEM((1, mine), F32),
            *[pltpu.VMEM(lane, F32)] * 4,
            pltpu.VMEM(full, BF16),
            pltpu.VMEM((width, width), BF16),
            pltpu.VMEM(full, BF16),
            pltpu.VMEM(full, BF16),
            pltpu.VMEM((own, width), F32),
            pltpu.VMEM((8, rows), F32),
            pltpu.VMEM((n_mp, 8, rows), F32),
            pltpu.SemaphoreType.DMA((17,)),
            pltpu.SemaphoreType.DMA((17,)),
            pltpu.SemaphoreType.DMA((2, n_mp)),
            pltpu.SemaphoreType.DMA((2, bits, n_mp)),
            pltpu.SemaphoreType.DMA((2, n_mp)),
            *RowGather.scratch(n_dp, 7),
            *CubeGather.scratch(n_mp) * 5,
        ],
        compiler_params=pltpu.CompilerParams(collective_id=cid, has_side_effects=True, vmem_limit_bytes=VMEM_LIMIT),
        name="mixer_forward",
    )(*args)


def ffn_kernel(n_dp, n_mp, final, ffn_in, grad_out, w, w_d, *refs):
    p = Place(n_dp, n_mp)
    rows, width = ffn_in.shape
    own = rows // n_mp
    if final:
        gffn1, down1, middle, r_mid, cot, tok, gain_ffn, w_mix, gsum, mixed, gmid, gain_part, gm, gb, rowdot = refs[:15]
        refs = refs[15:]
    else:
        w_gate, w_up, w_down, gsum, gffn, down, next_w, next_d = refs[:8]
        refs = refs[8:]
    a, wv, wd, bv, bq, lsem, gsem = refs[:7]
    sums, cube_g = refs[7:12], refs[12:15]
    cube_d = (cube_g[0], *refs[15:17])
    refs = refs[17:]
    h = bv.shape[2]
    shard = gsum.shape[1]
    loads = [load(ffn_in, a.at[0], lsem.at[0])]
    loads += [load(w.at[b], wv.at[b], lsem.at[1 + b]) for b in range(2)]
    loads += [load(grad_out, a.at[1], lsem.at[3]), load(w_d, wd, lsem.at[4])]
    if final:
        gffn, mid_v, cot_v, tok_v, wmb, gbr, gm_out, gm_in, gb_in, rd_out, rd_in, wsem, ssem, rsem = refs
        late = [load(src, dst, lsem.at[5 + i]) for i, (src, dst) in enumerate(((middle, mid_v), (cot, cot_v), (tok, tok_v), (gffn1, gffn)))]
        mine = gm.shape[2]
        half, ch = width // 2, mine // 2

        def mix_load(j, s):
            q = p.m ^ j
            return pltpu.make_async_copy(
                w_mix.at[pl.ds(pl.multiple_of(s * half + q * ch, LANE), ch)], wmb.at[s], wsem.at[s]
            )

    p.barrier()
    if not final:
        h_next = next_d.shape[0]
        srcs = (w_gate.at[:, h:], w_up.at[:, h:], w_down.at[h:])

        def next_dst(u, e, c):
            at = pl.ds(pl.multiple_of((2 * e + c) * shard, LANE), shard)
            return next_d.at[:, at] if u == 2 else next_w.at[u, at]

        z = RowGather(p, refs, lambda u: srcs[u], next_dst)
        own_next = [load(srcs[u], next_dst(u, p.k, p.c), lsem.at[5 + u]) for u in range(3)]
        for u in range(3):
            z.start(u)
    for copy in loads:
        copy.wait()
    step = 240

    def forward(i, _):
        at = pl.ds(pl.multiple_of(i * step, 16), step)
        gate = dot(a[0, at, :], wv[0])
        up = dot(a[0, at, :], wv[1])
        sig = sigmoid(gate)
        silu = gate * sig
        grad = dot_trans(a[1, at, :], wd[...])
        values = (grad * up * sig * (1.0 + gate * (1.0 - sig)), grad * silu, silu * up)
        for b in range(3):
            bv[b, at, :] = values[b].astype(BF16)
            if own % 16:
                for j in range(step // own):
                    bq[b, i * (step // own) + j] = values[b][j * own : (j + 1) * own].astype(BF16)
        return 0

    lax.fori_loop(0, rows // step, forward, 0)
    cols = bounds(width, p.bits, LANE)

    def rows_of(b, q):
        return bq[b, q] if own % 16 else bv[b, pl.ds(pl.multiple_of(q * own, 16), own), :]

    def part_g(q, part):
        lo, size = cols[part]
        at = slice(lo, lo + size)
        return dot_trans(rows_of(0, q), wv[0, at, :]) + dot_trans(rows_of(1, q), wv[1, at, :])

    def part_d(q, part):
        lo, size = cols[part]
        return dot(rows_of(2, q), wd[:, lo : lo + size])

    def piece(b, e):
        left = jnp.where(b < 2, 0, 1)
        return dot_rows(a[left, :, pl.ds(pl.multiple_of(e * shard, LANE), shard)], bv[b])

    def finish(b, acc):
        out = pltpu.make_async_copy(acc, gsum.at[b], gsem)
        out.start()
        out.wait()

    total = RowSum(p, sums, piece, finish, False)
    g_cube, d_cube = CubeSum(p, cube_g, part_g, width), CubeSum(p, cube_d, part_d, width)
    n, chips = total.blocks, p.chips
    if not final:
        z.forward(0, 1)
        total.run(0, n)
        z.forward(1, 1)
        g_cube.stage(0)
        z.forward(2, 1)
        for i in range(3):
            total.run(n + i, n + i + 1)
            z.forward(i, 2)
        for s in range(1, p.bits):
            g_cube.stage(s)
        g_cube.drain()
        d_cube.stage(0)
    else:
        total.run(0, n)
        g_cube.stage(0)
        total.run(n, 2 * n)
        for s in range(1, p.bits):
            g_cube.stage(s)
        late[3].wait()
        g_cube.drain()
    for part, (lo, size) in enumerate(cols):
        value = g_cube.result(part)
        gffn[:, lo : lo + size] = gffn[:, lo : lo + size] + value if final else value
    if not final:
        for s in range(1, p.bits):
            d_cube.stage(s)
    else:
        for copy in late[:3]:
            copy.wait()
        mix_load(1, 0).start()
        fine = 48 if own % 48 == 0 else own

        def norm_back(i, gains):
            at = pl.ds(pl.multiple_of(i * fine, fine), fine)
            g = gffn[at, :]
            n_own = mid_v[at, :] * r_mid[at, :]
            gains = gains + jnp.sum((g * n_own).reshape(fine // 8, 8, width), axis=0)
            gn = g * gain_ffn[...]
            back = r_mid[at, :] * (gn - n_own * jnp.mean(gn * n_own, axis=-1, keepdims=True))
            grad = cot_v[at, :].astype(F32) + back
            gmid[at, :] = grad
            low = grad.astype(BF16)
            gbr[at, :] = low
            dots = jnp.mean(low.astype(F32) * (mid_v[at, :] - tok_v[at, :].astype(F32)), axis=-1, keepdims=True)
            rd_out[at, :] = jnp.broadcast_to(dots, (fine, LANE))
            return gains

        gains = lax.fori_loop(0, own // fine, norm_back, jnp.zeros((8, width), F32))
        gain_part[...] = jnp.sum(gains, axis=0, keepdims=True)

        def across(kind, j, owner):
            send, recv, to = ssem.at[kind, j], rsem.at[kind, owner], p.peer(j)
            if kind == 0:
                return remote(gm_out.at[j], gm_in.at[owner], send, recv, to)
            if kind == 1:
                return remote(rd_out, rd_in.at[owner], send, recv, to)
            here = pl.ds(pl.multiple_of((p.m ^ j) * mine, LANE), mine)
            return remote(gbr.at[:, here], gb_in.at[owner], send, recv, to)

        for j in range(1, n_mp):
            across(1, j, p.m).start()
        turns = [(j, s) for j in (*range(1, n_mp), 0) for s in range(2)]
        for at, (j, s) in enumerate(turns):
            mix_load(j, s).wait()
            if at + 1 < len(turns):
                mix_load(*turns[at + 1]).start()
            value = dot_trans(gbr[...], wmb[s]).astype(BF16)
            if j:
                gm_out[j, :, s * ch : (s + 1) * ch] = value
                if s:
                    across(0, j, p.m).start()
            else:
                gm_in[p.m, :, s * ch : (s + 1) * ch] = value
        for j in range(1, n_mp):
            across(2, j, p.m).start()
        gb_in[p.m] = gbr[:, pl.ds(pl.multiple_of(p.m * mine, LANE), mine)]
        rd_in[p.m] = rd_out[...]
        down_load = load(down1, gffn, lsem.at[9])
        d_cube.stage(0)
    if final:
        total.run(2 * n, 3 * n)
        for s in range(1, p.bits):
            d_cube.stage(s)
        total.run(3 * n, total.steps)
    else:
        for i in range(2 * n, total.steps):
            total.run(i, i + 1)
            if i // n + 1 < p.chips:
                z.forward(i % n, i // n + 1)
        for u in range(3):
            z.finish(u)
            own_next[u].wait()
            z.drain(u)
    if final:
        for j in range(1, n_mp):
            for kind in range(3):
                across(kind, j, p.m ^ j).wait_recv()
        back = [load(src, dst, lsem.at[10 + i]) for i, (src, dst) in enumerate(((gm_in, gm), (gb_in, gb), (rd_in, rowdot)))]
        down_load.wait()
        for part, (lo, size) in enumerate(cols):
            at = slice(lo, lo + size)
            mixed[:, at] = (mid_v[:, at] + gffn[:, at] + d_cube.result(part)).astype(BF16)
        for j in range(1, n_mp):
            for kind in range(3):
                across(kind, j, p.m).wait_send()
        for copy in back:
            copy.wait()
    else:
        for part, (lo, size) in enumerate(cols):
            down[:, lo : lo + size] = d_cube.result(part)
    d_cube.drain()
    total.drain()


def ffn_part(n_dp, n_mp, cid, final, ffn_in, grad_out, w, w_d, *rest):
    rows, width = ffn_in.shape
    h = w.shape[2]
    shard, own = width // n_dp, rows // n_mp
    mine = width // n_mp
    f_own = jax.ShapeDtypeStruct((own, width), F32)
    gsum = jax.ShapeDtypeStruct((3, shard, h), F32)
    scratch = [
        pltpu.VMEM((2, rows, width), BF16),
        pltpu.VMEM((2, width, h), BF16),
        pltpu.VMEM((h, width), BF16),
        pltpu.VMEM((3, rows, h), BF16),
        pltpu.VMEM((3, n_mp, own, h) if own % 16 else (1, 1, 16, LANE), BF16),
        pltpu.SemaphoreType.DMA((13,)),
        pltpu.SemaphoreType.DMA,
        *RowSum.scratch(n_dp, 3, shard, h),
        *CubeSum.scratch(n_mp, own, width),
        *CubeSum.scratch(n_mp, own, width)[1:],
    ]
    if final:
        piece = jax.ShapeDtypeStruct((n_mp, own, mine), BF16)
        outs = (
            gsum, jax.ShapeDtypeStruct((own, width), BF16), f_own, jax.ShapeDtypeStruct((1, width), F32),
            piece, piece, jax.ShapeDtypeStruct((n_mp, own, LANE), F32),
        )
        scratch += [
            pltpu.VMEM((own, width), F32),
            pltpu.VMEM((own, width), F32),
            pltpu.VMEM((own, width), BF16),
            pltpu.VMEM((own, width), BF16),
            pltpu.VMEM((2, mine // 2, width), BF16),
            pltpu.VMEM((own, width), BF16),
            *[pltpu.VMEM((n_mp, own, mine), BF16)] * 3,
            pltpu.VMEM((own, LANE), F32),
            pltpu.VMEM((n_mp, own, LANE), F32),
            pltpu.SemaphoreType.DMA((2,)),
            pltpu.SemaphoreType.DMA((3, n_mp)),
            pltpu.SemaphoreType.DMA((3, n_mp)),
        ]
        in_specs = [ANY] * 7 + [VMEM, ANY, ANY, VMEM, ANY]
        out_specs = (ANY, VMEM, VMEM, VMEM, ANY, ANY, ANY)
    else:
        h_next = rest[2].shape[0] - h
        outs = (
            gsum, f_own, f_own,
            jax.ShapeDtypeStruct((2, width, h_next), BF16), jax.ShapeDtypeStruct((h_next, width), BF16),
        )
        scratch += RowGather.scratch(n_dp, 3)
        in_specs = [ANY] * 7
        out_specs = (ANY, VMEM, VMEM, ANY, ANY)
    return pl.pallas_call(
        functools.partial(ffn_kernel, n_dp, n_mp, final),
        out_shape=outs,
        in_specs=in_specs,
        out_specs=out_specs,
        scratch_shapes=scratch,
        compiler_params=pltpu.CompilerParams(collective_id=cid, has_side_effects=True, vmem_limit_bytes=VMEM_LIMIT),
        name="ffn_last" if final else "ffn_first",
    )(ffn_in, grad_out, w, w_d, *rest)


def project_kernel(
    n_dp, n_mp, normed, mixed, g_in, g_f, g_g, g_b, g_split, w, gmid, tok, r_in, gain_in, gain_ffn_part, dgain, dbound,
    gw, gtok, small, a, bv, bq, wv, lsem, rsend, rrecv, gall, *refs,
):
    p = Place(n_dp, n_mp)
    rows, width = normed.shape
    mine = bv.shape[2]
    half, ch, own = width // 2, mine // 2, rows // n_mp
    shard = gw.shape[2]
    sums, cube_refs, vec = refs[:5], refs[5:8], SmallSum(p, refs[8:10])
    loads = [load(normed, a.at[0], lsem.at[0])]
    loads += [load(src, bv.at[i], lsem.at[1 + i]) for i, src in enumerate((g_in, g_f, g_g, g_b))]
    loads += [load(mixed, a.at[1], lsem.at[5])]
    late = [load(w.at[i], wv.at[i], lsem.at[6 + i]) for i in range(3)]
    if own % 16:
        late.append(load(g_split, bq, lsem.at[9]))
    p.barrier(far=True)
    for copy in loads:
        copy.wait()

    def piece(b, e):
        left = jnp.where(b < 3, 0, 1)
        return dot_rows(a[left, :, pl.ds(pl.multiple_of(e * shard, LANE), shard)], bv[b])

    def out_copy(b, mask, owner):
        return remote(gall.at[b, owner], gall.at[b, owner], rsend.at[b, mask], rrecv.at[b, owner], p.peer(mask))

    def finish(b, acc):
        gall[b, p.m] = acc[...].astype(BF16)
        for mask in range(1, n_mp):
            out_copy(b, mask, p.m).start()

    cols = bounds(width, p.bits, LANE)

    def partial(q, part):
        lo, size = cols[part]
        value = 0.0
        for b in range(3):
            left = bq[b, q] if own % 16 else bv[b, pl.ds(pl.multiple_of(q * own, 16), own), :]
            value = value + dot_trans(left, wv[b, lo : lo + size, :])
        return value

    total = RowSum(p, sums, piece, finish, True)
    cube = CubeSum(p, cube_refs, partial, width)
    tick = p.chips
    total.run(0, tick)
    for copy in late:
        copy.wait()
    cube.stage(0)
    total.run(tick, 2 * tick)
    for s in range(1, p.bits):
        cube.stage(s)
    total.run(2 * tick, 3 * tick)
    for part, (lo, size) in enumerate(cols):
        gtok[:, lo : lo + size] = cube.result(part)
    fine = 48 if own % 48 == 0 else own

    def norm_back(i, gains):
        at = pl.ds(pl.multiple_of(i * fine, fine), fine)
        g = gtok[at, :]
        n_own = tok[at, :].astype(F32) * r_in[at, :]
        gains = gains + jnp.sum((g * n_own).reshape(fine // 8, 8, width), axis=0)
        gn = g * gain_in[...]
        gtok[at, :] = gmid[at, :] + r_in[at, :] * (gn - n_own * jnp.mean(gn * n_own, axis=-1, keepdims=True))
        return gains

    gains = lax.fori_loop(0, own // fine, norm_back, jnp.zeros((8, width), F32))
    vec.buf[0] = jnp.zeros((4, width), F32)
    vec.buf[0, 0:1] = jnp.sum(gains, axis=0, keepdims=True)
    vec.buf[0, 1:2] = gain_ffn_part[...]
    here = pl.ds(pl.multiple_of(p.m * ch, LANE), ch)
    vec.buf[0, 2:3, here] = dgain[:, :ch]
    vec.buf[0, 2:3, pl.ds(pl.multiple_of(half + p.m * ch, LANE), ch)] = dgain[:, ch:]
    vec.buf[0, 3:4, here] = dbound[...]
    vec.twins()
    total.run(3 * tick, 4 * tick)
    vec.cube()
    total.run(4 * tick, 5 * tick)
    vec.line()
    total.run(5 * tick, total.steps)
    for b in range(4):
        for mask in range(1, n_mp):
            out_copy(b, mask, p.m ^ mask).wait_recv()
    out = load(gall, gw, lsem.at[10])
    small[...] = vec.result()
    out.wait()
    for b in range(4):
        for mask in range(1, n_mp):
            out_copy(b, mask, p.m).wait_send()
    cube.drain()
    total.drain()


def project_back(n_dp, n_mp, cid, normed, mixed, g_in, g_f, g_g, g_b, w, gmid, tok, r_in, gain_in, *vectors):
    rows, width = normed.shape
    mine, shard, own = g_in.shape[1], width // n_dp, rows // n_mp
    if own % 16:
        g_split = jnp.stack([g.reshape(n_mp, own, mine) for g in (g_in, g_f, g_g)])
    else:
        g_split = jnp.zeros((1, 1, 16, LANE), BF16)
    return pl.pallas_call(
        functools.partial(project_kernel, n_dp, n_mp),
        out_shape=(
            jax.ShapeDtypeStruct((4, n_mp, shard, mine), BF16),
            jax.ShapeDtypeStruct((own, width), F32),
            jax.ShapeDtypeStruct((4, width), F32),
        ),
        in_specs=[ANY] * 8 + [VMEM] * 7,
        out_specs=(ANY, VMEM, VMEM),
        scratch_shapes=[
            pltpu.VMEM((2, rows, width), BF16),
            pltpu.VMEM((4, rows, mine), BF16),
            pltpu.VMEM(g_split.shape, BF16),
            pltpu.VMEM((3, width, mine), BF16),
            pltpu.SemaphoreType.DMA((11,)),
            pltpu.SemaphoreType.DMA((4, n_mp)),
            pltpu.SemaphoreType.DMA((4, n_mp)),
            pltpu.VMEM((4, n_mp, shard, mine), BF16),
            *RowSum.scratch(n_dp, 4, shard, mine),
            *CubeSum.scratch(n_mp, own, width),
            *SmallSum.scratch(n_dp, n_mp, (4, width)),
        ],
        compiler_params=pltpu.CompilerParams(collective_id=cid, has_side_effects=True, vmem_limit_bytes=VMEM_LIMIT),
        name="project_back",
    )(normed, mixed, g_in, g_f, g_g, g_b, g_split, w, gmid, tok, r_in, gain_in, *vectors)


def result_kernel(
    n_mp, gmix, one, two, mixed, gtok, small,
    o_mixed, o_tok, o_gin, o_win, o_wf, o_wo, o_bound, o_gmix, o_wm, o_gffn, o_gate, o_up, o_down,
    gm, gw, gffn, down, mixed_v, tok_v, sem, osem,
):
    d = lax.axis_index("dp")
    shard, mine = gmix.shape[2:]
    ch, half = mine // 2, n_mp * mine // 2
    h, h2 = one.shape[2], two.shape[2]
    mixer = [load(gmix.at[b], gm.at[b], sem.at[b]) for b in range(4)]
    through = [load(mixed, mixed_v, sem.at[4]), load(gtok, tok_v, sem.at[5])]
    ffn = [
        (load(one.at[i], gffn.at[i, :, :h], sem.at[6 + 2 * i]), load(two.at[i], gffn.at[i, :, h:], sem.at[7 + 2 * i]))
        for i in range(3)
    ]
    outs = []
    for b, out in enumerate((o_win, o_wf, o_wo, o_wm)):
        mixer[b].wait()
        for q in range(n_mp):
            value = gm[b, q].astype(F32)
            if b < 3:
                gw[b, :, q * ch : (q + 1) * ch] = value[:, :ch]
                gw[b, :, half + q * ch : half + (q + 1) * ch] = value[:, ch:]
            else:
                gw[b, :, q * mine : (q + 1) * mine] = value
        outs.append(load(gw.at[b], out, osem.at[b]))
    for i, (copy, src, out) in enumerate(zip(through, (mixed_v, tok_v), (o_mixed, o_tok))):
        copy.wait()
        outs.append(load(src, out, osem.at[4 + i]))
    for i, out in enumerate((o_gate, o_up)):
        for copy in ffn[i]:
            copy.wait()
        outs.append(load(gffn.at[i], out, osem.at[6 + i]))
    at = pl.ds(pl.multiple_of(d * shard, LANE), shard)
    for row, out in enumerate((o_gin, o_gffn, o_gmix)):
        out[...] = small[row : row + 1, at]
    size = shard // 2
    if size % LANE == 0:
        o_bound[...] = small[3:4, pl.ds(pl.multiple_of(d * size, LANE), size)]
    else:
        pair = small[3:4, pl.ds(pl.multiple_of(lax.div(d, 2) * 2 * size, LANE), 2 * size)]
        o_bound[...] = jnp.where(lax.rem(d, 2) == 0, pair[:, :size], pair[:, size:])
    for copy in ffn[2]:
        copy.wait()
    for lo in range(0, h + h2, LANE):
        down[lo : lo + LANE, :] = gffn[2, :, lo : lo + LANE].T
    outs.append(load(down, o_down, osem.at[8]))
    for copy in outs:
        copy.wait()


def results(n_dp, n_mp, gmix, one, two, mixed, gtok, small):
    shard, mine = gmix.shape[2:]
    width, ffn = n_mp * mine, one.shape[2] + two.shape[2]
    own = mixed.shape[0]

    def f32(*shape):
        return jax.ShapeDtypeStruct(shape, F32)

    row = f32(1, shard)
    return pl.pallas_call(
        functools.partial(result_kernel, n_mp),
        out_shape=(
            jax.ShapeDtypeStruct((own, width), BF16), f32(own, width), row, *(f32(shard, width),) * 3, f32(1, shard // 2), row,
            f32(shard, width), row, f32(shard, ffn), f32(shard, ffn), f32(ffn, shard),
        ),
        in_specs=[ANY] * 5 + [VMEM],
        out_specs=(ANY, ANY, VMEM, ANY, ANY, ANY, VMEM, VMEM, ANY, VMEM, ANY, ANY, ANY),
        scratch_shapes=[
            pltpu.VMEM((4, n_mp, shard, mine), BF16),
            pltpu.VMEM((4, shard, width), F32),
            pltpu.VMEM((3, shard, ffn), F32),
            pltpu.VMEM((ffn, shard), F32),
            pltpu.VMEM((own, width), BF16),
            pltpu.VMEM((own, width), F32),
            pltpu.SemaphoreType.DMA((12,)),
            pltpu.SemaphoreType.DMA((9,)),
        ],
        compiler_params=pltpu.CompilerParams(vmem_limit_bytes=VMEM_LIMIT),
        name="results",
    )(gmix, one, two, mixed, gtok, small)


def per_device(n_dp, n_mp, tokens, segment_ids, cotangent, gain_in, w_in, w_forget, w_outgate, bound_logit, gain_mix,
               w_mix, gain_ffn, w_gate, w_up, w_down):
    m, d = lax.axis_index("mp"), lax.axis_index("dp")
    rows, width = tokens.shape
    half = bound_logit.shape[0]
    ch = half // n_mp
    mine = 2 * ch
    own = rows // n_mp
    ffn = w_gate.shape[1]
    padded = -(-ffn // LANE) * LANE
    cut = -(-padded // 2 // LANE) * LANE
    if padded != ffn:
        fill = ((0, 0), (0, padded - ffn))
        w_gate, w_up, w_down = jnp.pad(w_gate, fill), jnp.pad(w_up, fill), jnp.pad(w_down, fill[::-1])

    def own_rows(x):
        return lax.dynamic_slice_in_dim(x, m * own, own, 0)

    normed, r_in, pin, pf, pg, st, phasor, r_mix, mixer_out, ffn_in, middle, r_mid, wm, w_cat, w_one, d_one, grad_out = mixer_forward(
        n_dp, n_mp, 2, cut, w_in, w_forget, w_outgate, w_mix, w_gate, w_up, w_down, cotangent, tokens, segment_ids,
        bound_logit[None], gain_mix[None], gain_in[None], gain_ffn[None],
    )
    grad_out = grad_out.reshape(rows, width)

    g_one, gffn, down, w_two, d_two = ffn_part(
        n_dp, n_mp, 3, False, ffn_in, grad_out, w_one, d_one, w_gate, w_up, w_down
    )
    tok_own = own_rows(tokens)
    g_two, mixed, gmid, gain_ffn_part, gm, gb, rowdot = ffn_part(
        n_dp, n_mp, 4, True, ffn_in, grad_out, w_two, d_two, gffn, down, middle, r_mid, cotangent, tok_own, gain_ffn[None], wm
    )

    bl = lax.dynamic_slice_in_dim(bound_logit, m * ch, ch, 0)[None]
    gain = jnp.concatenate([lax.dynamic_slice_in_dim(gain_mix, at + m * ch, ch, 0) for at in (0, half)])[None]
    lanes = ch // LANE
    scratch = [pltpu.VMEM((lanes, rows, LANE), F32)] * 4
    gin, gf, gg, dgain, dbound = call_local(
        scan_backward,
        (
            jax.ShapeDtypeStruct((rows, mine), BF16),
            jax.ShapeDtypeStruct((rows, mine), BF16),
            jax.ShapeDtypeStruct((rows, mine), BF16),
            jax.ShapeDtypeStruct((1, mine), F32),
            jax.ShapeDtypeStruct((1, ch), F32),
        ),
        scratch,
        gm.reshape(rows, mine), pin, pf, pg, st, phasor, r_mix, rowdot.reshape(rows, LANE)[:, :1], bl, gain,
        name="scan_backward",
    )
    g_mixer, grad_tokens, small = project_back(
        n_dp, n_mp, 5, normed, mixer_out, gin, gf, gg, gb.reshape(rows, mine), w_cat, gmid, tok_own, own_rows(r_in),
        gain_in[None], gain_ffn_part, dgain, dbound,
    )

    out = results(n_dp, n_mp, g_mixer, g_one, g_two, mixed, grad_tokens, small)
    out = [v[0] if v.shape[0] == 1 else v for v in out]
    if padded != ffn:
        out[10:] = [out[10][:, :ffn], out[11][:, :ffn], out[12][:ffn]]
    return tuple(out)


def solution(mesh):
    both, split = P(("dp", "mp"), None), P("dp", "mp")
    row, vec = P("dp", None), P("dp")
    return jax.shard_map(
        functools.partial(per_device, mesh.shape["dp"], mesh.shape["mp"]),
        mesh=mesh,
        in_specs=(row, row, both, P(), row, row, row, P(), P(), row, P(), split, split, P("mp", "dp")),
        out_specs=(both, both, vec, row, row, row, vec, vec, row, vec, split, split, P("mp", "dp")),
        check_vma=False,
    )
```

```python
import functools

import jax
import jax.numpy as jnp
from jax import lax
from jax.experimental import pallas as pl
from jax.experimental.pallas import tpu as pltpu
from jax.sharding import PartitionSpec as P

EPS = 1e-06
F32, BF16 = jnp.float32, jnp.bfloat16
LANE = 128
CHUNKS = 8


def dot(left, right):
    return jnp.dot(left, right, preferred_element_type=F32)


def dot_trans(left, right):
    return lax.dot_general(left, right, (((1,), (1,)), ((), ())), preferred_element_type=F32)


def dot_rows(left, right):
    return lax.dot_general(left, right, (((0,), (0,)), ((), ())), preferred_element_type=F32)


def sigmoid(v):
    return 1.0 / (1.0 + jnp.exp(-v))


def scan_forward(pin, pf, starts, bl, st, phasor, rowsq, a_re, a_im, b_re, b_im):
    rows, half = pin.shape[0], pin.shape[1] // 2
    span = rows // CHUNKS
    lanes = half // LANE
    low = sigmoid(bl[...])
    step = 48

    def prepare(i, _):
        at = pl.ds(pl.multiple_of(i * step, 8), step)
        forget = low + (1.0 - low) * sigmoid(pf[at, :half])
        phase = pf[at, half:]
        keep = 1.0 - starts[at, :]
        cos, sin = jnp.cos(phase) * keep, jnp.sin(phase) * keep
        phasor[at, :half] = cos
        phasor[at, half:] = sin
        x_re, x_im = pin[at, :half], pin[at, half:]
        inflow = 1.0 - forget
        in_re, in_im = x_re * sigmoid(x_re) * inflow, x_im * sigmoid(x_im) * inflow
        d_re, d_im = forget * cos, forget * sin
        for j in range(lanes):
            cut = slice(j * LANE, (j + 1) * LANE)
            a_re[j, at, :] = d_re[:, cut]
            a_im[j, at, :] = d_im[:, cut]
            b_re[j, at, :] = in_re[:, cut]
            b_im[j, at, :] = in_im[:, cut]
        return 0

    lax.fori_loop(0, rows // step, prepare, 0)
    zero, one = jnp.zeros((CHUNKS, LANE), F32), jnp.ones((CHUNKS, LANE), F32)

    def local(s, carry):
        at = pl.ds(s, CHUNKS, stride=span)
        out = []
        for j in range(lanes):
            p_re, p_im, s_re, s_im = carry[4 * j : 4 * j + 4]
            d_re, d_im = a_re.at[j][at, :], a_im.at[j][at, :]
            i_re, i_im = b_re.at[j][at, :], b_im.at[j][at, :]
            p_re, p_im = d_re * p_re - d_im * p_im, d_re * p_im + d_im * p_re
            s_re, s_im = d_re * s_re - d_im * s_im + i_re, d_re * s_im + d_im * s_re + i_im
            a_re.at[j][at, :] = p_re
            a_im.at[j][at, :] = p_im
            b_re.at[j][at, :] = s_re
            b_im.at[j][at, :] = s_im
            out += [p_re, p_im, s_re, s_im]
        return tuple(out)

    last = lax.fori_loop(0, span, local, (one, zero, zero, zero) * lanes, unroll=2)
    carries = []
    for j in range(lanes):
        p_re, p_im, s_re, s_im = last[4 * j : 4 * j + 4]
        c_re = c_im = jnp.zeros((1, LANE), F32)
        held = []
        for k in range(CHUNKS):
            held.append((c_re, c_im))
            q_re, q_im = p_re[k : k + 1], p_im[k : k + 1]
            c_re, c_im = (
                q_re * c_re - q_im * c_im + s_re[k : k + 1],
                q_re * c_im + q_im * c_re + s_im[k : k + 1],
            )
        carries.append(held)
    fix = 40
    for k in range(CHUNKS):

        def finish(i, _):
            at = pl.ds(pl.multiple_of(k * span + i * fix, 8), fix)
            total = jnp.zeros((fix, LANE), F32)
            for j in range(lanes):
                c_re, c_im = carries[j][k]
                p_re, p_im = a_re[j, at, :], a_im[j, at, :]
                s_re = b_re[j, at, :] + p_re * c_re - p_im * c_im
                s_im = b_im[j, at, :] + p_re * c_im + p_im * c_re
                st[at, j * LANE : (j + 1) * LANE] = s_re
                st[at, half + j * LANE : half + (j + 1) * LANE] = s_im
                total = total + s_re * s_re + s_im * s_im
            rowsq[at, :] = jnp.sum(total, axis=1, keepdims=True)
            return 0

        lax.fori_loop(0, span // fix, finish, 0)


def scan_backward(
    gm, pin, pf, pg, st, phasor, r, rowdot, bl, gain, gin, gf, gg, dgain, dbound, a_re, a_im, b_re, b_im, between=(),
):
    rows, half = pin.shape[0], pin.shape[1] // 2
    width = 2 * half
    span = rows // CHUNKS
    lanes = half // LANE
    low = sigmoid(bl[...])
    step = 48

    def prepare(i, total):
        at = pl.ds(pl.multiple_of(i * step, 16), step)
        g, gate = gm[at, :].astype(F32), pg[at, :]
        sig = sigmoid(gate)
        silu = gate * sig
        n = st[at, :] * r[at, :]
        gs = g * silu
        gg[at, :] = (g * n * gain[...] * (sig * (1.0 + gate * (1.0 - sig)))).astype(gg.dtype)
        total = total + jnp.sum((gs * n).reshape(step // 8, 8, width), axis=0)
        d_st = r[at, :] * (gs * gain[...] - n * rowdot[at, :])
        forget = low + (1.0 - low) * sigmoid(pf[at, :half])
        d_re, d_im = forget * phasor[at, :half], forget * phasor[at, half:]
        for j in range(lanes):
            a_re[j, at, :] = d_re[:, j * LANE : (j + 1) * LANE]
            a_im[j, at, :] = d_im[:, j * LANE : (j + 1) * LANE]
            b_re[j, at, :] = d_st[:, j * LANE : (j + 1) * LANE]
            b_im[j, at, :] = d_st[:, half + j * LANE : half + (j + 1) * LANE]
        return total

    total = lax.fori_loop(0, rows // step, prepare, jnp.zeros((8, width), F32))
    dgain[...] = jnp.sum(total, axis=0, keepdims=True)
    for task in between[:1]:
        task()
    zero, one = jnp.zeros((CHUNKS, LANE), F32), jnp.ones((CHUNKS, LANE), F32)

    def local(i, carry):
        at = pl.ds(span - 1 - i, CHUNKS, stride=span)
        out = []
        for j in range(lanes):
            p_re, p_im, s_re, s_im = carry[4 * j : 4 * j + 4]
            d_re, d_im = a_re.at[j][at, :], a_im.at[j][at, :]
            s_re, s_im = s_re + b_re.at[j][at, :], s_im + b_im.at[j][at, :]
            a_re.at[j][at, :] = p_re
            a_im.at[j][at, :] = p_im
            b_re.at[j][at, :] = s_re
            b_im.at[j][at, :] = s_im
            p_re, p_im = d_re * p_re + d_im * p_im, d_re * p_im - d_im * p_re
            s_re, s_im = d_re * s_re + d_im * s_im, d_re * s_im - d_im * s_re
            out += [p_re, p_im, s_re, s_im]
        return tuple(out)

    last = lax.fori_loop(0, span, local, (one, zero, zero, zero) * lanes, unroll=2)
    for task in between[1:]:
        task()
    carries = []
    for j in range(lanes):
        p_re, p_im, s_re, s_im = last[4 * j : 4 * j + 4]
        c_re = c_im = jnp.zeros((1, LANE), F32)
        held = [None] * CHUNKS
        for k in reversed(range(CHUNKS)):
            held[k] = (c_re, c_im)
            q_re, q_im = p_re[k : k + 1], p_im[k : k + 1]
            c_re, c_im = (
                q_re * c_re - q_im * c_im + s_re[k : k + 1],
                q_re * c_im + q_im * c_re + s_im[k : k + 1],
            )
        carries.append(held)
    fix = 40
    for k in range(CHUNKS):

        def carry_in(i, _):
            at = pl.ds(pl.multiple_of(k * span + i * fix, 8), fix)
            for j in range(lanes):
                c_re, c_im = carries[j][k]
                p_re, p_im = a_re[j, at, :], a_im[j, at, :]
                b_re[j, at, :] += p_re * c_re - p_im * c_im
                b_im[j, at, :] += p_re * c_im + p_im * c_re
            return 0

        lax.fori_loop(0, span // fix, carry_in, 0)

    def finish(i, carry):
        before, total = carry
        at = pl.ds(pl.multiple_of(i * step, 16), step)
        g_re = jnp.concatenate([b_re[j, at, :] for j in range(lanes)], axis=1)
        g_im = jnp.concatenate([b_im[j, at, :] for j in range(lanes)], axis=1)
        now = st[at, :]
        prev = jnp.concatenate([before, now[:-1]], axis=0)
        q_re, q_im = prev[:, :half], prev[:, half:]
        dd_re, dd_im = g_re * q_re + g_im * q_im, g_im * q_re - g_re * q_im
        mag = sigmoid(pf[at, :half])
        forget = low + (1.0 - low) * mag
        cos, sin = phasor[at, :half], phasor[at, half:]
        x_re, x_im = pin[at, :half], pin[at, half:]
        sig_re, sig_im = sigmoid(x_re), sigmoid(x_im)
        inflow = 1.0 - forget
        d_forget = dd_re * cos + dd_im * sin - g_re * x_re * sig_re - g_im * x_im * sig_im
        gf[at, :half] = (d_forget * (1.0 - low) * mag * (1.0 - mag)).astype(gf.dtype)
        gf[at, half:] = (forget * (dd_im * cos - dd_re * sin)).astype(gf.dtype)
        gin[at, :half] = (g_re * inflow * sig_re * (1.0 + x_re * (1.0 - sig_re))).astype(gin.dtype)
        gin[at, half:] = (g_im * inflow * sig_im * (1.0 + x_im * (1.0 - sig_im))).astype(gin.dtype)
        total = total + jnp.sum((d_forget * (1.0 - mag)).reshape(step // 8, 8, half), axis=0)
        return now[step - 1 :], total

    first = (jnp.zeros((1, width), F32), jnp.zeros((8, half), F32))
    total = lax.fori_loop(0, rows // step, finish, first)[1]
    dbound[...] = jnp.sum(total, axis=0, keepdims=True) * low * (1.0 - low)


def call_local(body, outs, scratch, *args, name):
    return pl.pallas_call(
        body,
        out_shape=outs,
        scratch_shapes=scratch,
        compiler_params=pltpu.CompilerParams(vmem_limit_bytes=48 * 2**20),
        name=name,
    )(*args)


MESH_ID = pl.DeviceIdType.MESH
VMEM_LIMIT = 62 * 2**20
ANY = pl.BlockSpec(memory_space=pl.ANY)
VMEM = pl.BlockSpec(memory_space=pltpu.VMEM)


def remote(src, dst, send, recv, device):
    return pltpu.make_async_remote_copy(
        src_ref=src, dst_ref=dst, send_sem=send, recv_sem=recv, device_id=device, device_id_type=MESH_ID
    )


def load(src, dst, sem):
    copy = pltpu.make_async_copy(src, dst, sem)
    copy.start()
    return copy


def bounds(total, parts, unit):
    ends = [i * (total // unit) // parts * unit for i in range(parts)] + [total]
    return [(ends[i], ends[i + 1] - ends[i]) for i in range(parts)]


def subsets(masks):
    out = [0]
    for mask in masks:
        out += [sub | mask for sub in out]
    return out


class Place:
    def __init__(self, n_dp, n_mp):
        self.n_dp, self.n_mp = n_dp, n_mp
        self.d, self.m = lax.axis_index("dp"), lax.axis_index("mp")
        self.chips, self.bits = n_dp // 2, n_mp.bit_length() - 1
        self.k, self.c = lax.div(self.d, 2), lax.rem(self.d, 2)

    def twin(self):
        return (2 * self.k + 1 - self.c, self.m)

    def chip(self, step):
        return (self.d + 2 * step, self.m)

    def peer(self, mask):
        return (self.d, self.m ^ mask)

    def along(self, s):
        return (2 * lax.rem(self.k + s, self.chips) + self.c, self.m)

    def barrier(self, line=True, twin=True, far=False):
        sem = pltpu.get_barrier_semaphore()

        def greet(device):
            pl.semaphore_signal(sem, inc=1, device_id=device, device_id_type=MESH_ID)

        for mask in range(1, self.n_mp):
            greet(self.peer(mask))
        count = self.n_mp - 1
        if twin:
            greet(self.twin())
            count += 1
        if far:
            for s in range(1, self.chips):
                greet(self.along(s))
            count += self.chips - 1
        elif line:

            @pl.when(self.k > 0)
            def _():
                greet(self.chip(-1))

            @pl.when(self.k < self.chips - 1)
            def _():
                greet(self.chip(1))

            count += jnp.where(self.k > 0, 1, 0) + jnp.where(self.k < self.chips - 1, 1, 0)
        pl.semaphore_wait(sem, count)


class RowSum:
    @staticmethod
    def scratch(n_dp, blocks, rows, width):
        chips = n_dp // 2
        return [
            pltpu.VMEM((2, 2, rows, width), BF16),
            pltpu.VMEM((blocks, chips, rows, width), BF16),
            pltpu.VMEM((blocks, chips + 1, rows, width), BF16),
            pltpu.VMEM((rows, width), F32),
            pltpu.SemaphoreType.DMA((4, blocks, chips + 1)),
        ]

    def __init__(self, place, refs, piece, finish, skew):
        self.p = place
        self.out, self.summed, self.inbox, self.acc, self.sem = refs
        self.piece, self.finish = piece, finish
        self.blocks, self.skew = self.summed.shape[0], skew
        chips = place.chips
        self.steps = chips - 1 + (self.blocks + chips - 2) * chips if skew else self.blocks * chips

    def order(self, i):
        chips = self.p.chips
        ok = (i >= 0) & (i < self.steps)
        i = jnp.clip(i, 0, self.steps - 1)
        if self.skew:
            early = i < chips - 1
            j = jnp.maximum(i - (chips - 1), 0)
            t = jnp.where(early, i, lax.rem(j, chips))
            b = jnp.where(early, 0, 1 + lax.div(j, chips) - t)
            ok = ok & (early | ((b >= 0) & (b < self.blocks) & ((b > 0) | (t == chips - 1))))
            return t, jnp.clip(b, 0, self.blocks - 1), ok
        return lax.div(i, self.blocks), lax.rem(i, self.blocks), ok

    def targets(self, i):
        p = self.p
        t, b, ok = self.order(i)
        up, down = p.chips - 1 - t + p.k, p.k - (p.chips - 1) + t
        return b, up, ok & (up <= p.chips - 1), down, ok & (down >= 0) & (t < p.chips - 1), t == p.chips - 1

    def swap(self, b, e, ring):
        return remote(
            self.out.at[ring[0], ring[1]], self.summed.at[b, e], self.sem.at[0, b, e], self.sem.at[1, b, e],
            self.p.twin(),
        )

    def move(self, b, e, up):
        slot = e + 1 if up else e
        return remote(
            self.summed.at[b, e], self.inbox.at[b, slot], self.sem.at[2, b, e], self.sem.at[3, b, slot],
            self.p.chip(1 if up else -1),
        )

    def given(self, i):
        b, up, up_ok, down, down_ok, _ = self.targets(i)
        for side, e, ok in ((0, up, up_ok), (1, down, down_ok)):

            @pl.when(ok)
            def _():
                self.swap(b, e, (lax.rem(i + 2, 2), side)).wait_send()

    def give(self, i):
        self.given(i - 2)
        b, up, up_ok, down, down_ok, _ = self.targets(i)
        for side, e, ok in ((0, up, up_ok), (1, down, down_ok)):

            @pl.when(ok)
            def _():
                ring = (lax.rem(i, 2), side)
                self.out[ring[0], side] = self.piece(b, 2 * e + 1 - self.p.c).astype(BF16)
                self.swap(b, e, ring).start()

    def take(self, b, slot, up):
        e = slot - 1 if up else slot
        self.move(b, e, up).wait_recv()
        self.acc[...] += self.inbox[b, slot].astype(F32)

    def send(self, b, e, up):
        self.summed[b, e] = self.acc[...].astype(BF16)
        self.move(b, e, up).start()

    def work(self, i):
        p = self.p
        b, up, up_ok, down, down_ok, last = self.targets(i)

        def begin(e):
            own = self.piece(b, 2 * e + p.c)
            self.swap(b, e, (0, 0)).wait_recv()
            self.acc[...] = own + self.summed[b, e].astype(F32)

        @pl.when(up_ok)
        def _():
            begin(up)

            @pl.when(p.k > 0)
            def _():
                self.take(b, up + 1, True)

            @pl.when(jnp.logical_not(last))
            def _():
                self.send(b, up, True)

            @pl.when(last)
            def _():
                @pl.when(p.k < p.chips - 1)
                def _():
                    self.take(b, up, False)

                self.finish(b, self.acc)

        @pl.when(down_ok)
        def _():
            begin(down)

            @pl.when(p.k < p.chips - 1)
            def _():
                self.take(b, down, False)

            self.send(b, down, False)

    def run(self, lo, hi, fresh=False, ahead=True):
        if lo == 0 or fresh:
            self.give(lo)

        def body(i, _):
            if ahead:
                self.give(i + 1)
            else:

                @pl.when(i + 1 < hi)
                def _():
                    self.give(i + 1)

            self.work(i)
            return 0

        lax.fori_loop(lo, hi, body, 0)
        if hi == self.steps:
            self.given(hi - 1)

    def drain(self):
        p = self.p

        def body(e, _):
            for b in range(self.blocks):

                @pl.when(e > p.k)
                def _():
                    self.move(b, e, True).wait_send()

                @pl.when(e < p.k)
                def _():
                    self.move(b, e, False).wait_send()

            return 0

        lax.fori_loop(0, p.chips, body, 0)


class CubeSum:
    @staticmethod
    def scratch(n_mp, rows, width, whole=True):
        bits = n_mp.bit_length() - 1
        most = max(size for _, size in bounds(width, bits, LANE))
        slots = n_mp - 1 if whole else n_mp - 2
        return [
            *[pltpu.VMEM((bits, slots, rows, most), BF16)] * 2,
            pltpu.SemaphoreType.DMA((2, bits, slots)),
        ]

    def __init__(self, place, refs, partial, width):
        self.p = place
        self.out, self.inbox, self.sem = refs
        self.partial = partial
        bits = place.bits
        self.cols = bounds(width, bits, LANE)
        self.slots, self.masks = {}, {}
        for part in range(bits):
            used = 0
            for s in range(bits):
                subs = subsets([1 << ((part + r) % bits) for r in range(s + 1, bits)])
                self.masks[part, s] = (1 << ((part + s) % bits), subs)
                for sub in subs:
                    self.slots[part, s, sub] = used
                    used += 1

    def copy(self, part, s, sub):
        slot, size = self.slots[part, s, sub], self.cols[part][1]
        return remote(
            self.out.at[part, slot, :, :size], self.inbox.at[part, slot, :, :size],
            self.sem.at[0, part, slot], self.sem.at[1, part, slot],
            self.p.peer(self.masks[part, s][0]),
        )

    def pieces(self, part, mask, stages):
        for r in stages:
            self.copy(part, r, mask).wait_recv()
        base, total = self.cols[part]
        for lo in range(0, total, 4 * LANE):
            size = min(4 * LANE, total - lo)
            value = self.partial(self.p.m ^ mask, base + lo, size)
            for r in stages:
                value = value + self.inbox[part, self.slots[part, r, mask], :, lo : lo + size].astype(F32)
            yield lo, size, value

    def stage(self, s, only=None):
        for part in range(self.p.bits):
            bit, subs = self.masks[part, s]
            for sub in subs:
                if only not in (None, bit | sub):
                    continue
                for lo, size, value in self.pieces(part, bit | sub, range(s)):
                    self.out[part, self.slots[part, s, sub], :, lo : lo + size] = value.astype(BF16)
                self.copy(part, s, sub).start()

    def results(self, stages=None):
        for part in range(self.p.bits):
            base = self.cols[part][0]
            for lo, size, value in self.pieces(part, 0, range(self.p.bits if stages is None else stages)):
                yield slice(base + lo, base + lo + size), value

    def parting(self):
        s = self.p.bits - 1
        for part in range(self.p.bits):
            for lo, size, value in self.pieces(part, self.masks[part, s][0], range(s)):
                yield part, slice(lo, lo + size), value

    def drain(self, stages=None):
        for part, s, sub in self.slots:
            if stages is None or s < stages:
                self.copy(part, s, sub).wait_send()


class CubeGather:
    @staticmethod
    def scratch(n_mp):
        bits = n_mp.bit_length() - 1
        return [pltpu.SemaphoreType.DMA((bits, n_mp)), pltpu.SemaphoreType.DMA((bits, n_mp))]

    def __init__(self, place, refs, view):
        self.p, self.view = place, view
        self.send, self.recv = refs
        bits = place.bits
        self.sends = {}
        for part in range(bits):
            for s in range(bits):
                earlier = [1 << ((part + r) % bits) for r in range(s)]
                for sub in subsets(earlier):
                    self.sends[part, s, sub] = (1 << ((part + s) % bits), sub)

    def copy(self, part, bit, sub):
        p = self.p
        ref = self.view(p.m ^ sub, part)
        return remote(ref, ref, self.send.at[part, bit | sub], self.recv.at[part, p.m ^ sub], p.peer(bit))

    def arrived(self, part, sub):
        p = self.p
        ref = self.view(p.m ^ sub, part)
        remote(ref, ref, self.send.at[part, sub], self.recv.at[part, p.m ^ sub], p.peer(sub)).wait_recv()

    def stage(self, s):
        for (part, at, sub), (bit, _) in self.sends.items():
            if at == s:
                if sub:
                    self.arrived(part, sub)
                self.copy(part, bit, sub).start()

    def last(self):
        p = self.p
        for part in range(p.bits):
            final = 1 << ((part + p.bits - 1) % p.bits)
            for sub in range(1, p.n_mp):
                if sub & final:
                    self.arrived(part, sub)

    def drain(self):
        for (part, _, sub), (bit, _) in self.sends.items():
            self.copy(part, bit, sub).wait_send()


class SmallSum:
    @staticmethod
    def scratch(n_dp, n_mp, shape):
        slots = 3 + n_mp + n_dp // 2
        return [pltpu.VMEM((slots, *shape), F32), pltpu.SemaphoreType.DMA((2, slots))]

    def __init__(self, place, refs):
        self.p = place
        self.buf, self.sem = refs

    def start(self, src, dst, device):
        remote(self.buf.at[src], self.buf.at[dst], self.sem.at[0, dst], self.sem.at[1, dst], device).start()

    def wait(self, dst):
        copy = remote(self.buf.at[dst], self.buf.at[dst], self.sem.at[0, dst], self.sem.at[1, dst], self.p.twin())
        copy.wait_recv()

    def sent(self, dst):
        copy = remote(self.buf.at[dst], self.buf.at[dst], self.sem.at[0, dst], self.sem.at[1, dst], self.p.twin())
        copy.wait_send()

    def twins(self):
        self.start(0, 1, self.p.twin())

    def cube(self):
        p = self.p
        self.wait(1)
        self.buf[2] = self.buf[0] + self.buf[1]
        for mask in range(1, p.n_mp):
            self.start(2, 3 + mask, p.peer(mask))

    def line(self):
        p = self.p
        for mask in range(1, p.n_mp):
            self.wait(3 + mask)
        total = 0.0
        for q in range(p.n_mp):
            mask = p.m ^ q
            total = total + self.buf[jnp.where(mask == 0, 2, 3 + mask)]
        self.buf[3] = total
        for s in range(1, p.chips):
            self.start(3, 3 + p.n_mp + s, p.along(s))

    def result(self):
        p = self.p
        total = self.buf[3]
        for s in range(1, p.chips):
            self.wait(3 + p.n_mp + s)
            total = total + self.buf[3 + p.n_mp + s]
        for dst in [1, *range(4, 3 + p.n_mp), *range(4 + p.n_mp, 3 + p.n_mp + p.chips)]:
            self.sent(dst)
        return total


class RowGather:
    @staticmethod
    def scratch(n_dp, units):
        return [pltpu.SemaphoreType.DMA((5, units, n_dp // 2))]

    def __init__(self, place, refs, src, dst):
        self.p, self.src, self.dst = place, src, dst
        (self.sem,) = refs

    def hop(self, u, e, side, own=False):
        p = self.p
        here = self.dst(u, e, p.c)
        device = (p.chip(1), p.chip(-1), p.twin())[side]
        recv = self.sem.at[4 if side == 2 else 3, u, e]
        return remote(self.src(u) if own else here, here, self.sem.at[side, u, e], recv, device)

    def start(self, u):
        p = self.p

        @pl.when(p.k < p.chips - 1)
        def _():
            self.hop(u, p.k, 0, True).start()

        @pl.when(p.k > 0)
        def _():
            self.hop(u, p.k, 1, True).start()

        self.hop(u, p.k, 2, True).start()

    def forward(self, u, s):
        p = self.p

        @pl.when(p.k - s >= 0)
        def _():
            self.hop(u, p.k - s, 0).wait_recv()

            @pl.when(p.k < p.chips - 1)
            def _():
                self.hop(u, p.k - s, 0).start()

            self.hop(u, p.k - s, 2).start()

        @pl.when(p.k + s < p.chips)
        def _():
            self.hop(u, p.k + s, 1).wait_recv()

            @pl.when(p.k > 0)
            def _():
                self.hop(u, p.k + s, 1).start()

            self.hop(u, p.k + s, 2).start()

    def finish(self, u):
        p = self.p
        for e in range(p.chips):
            there = self.dst(u, e, 1 - p.c)
            remote(there, there, self.sem.at[2, u, e], self.sem.at[4, u, e], p.twin()).wait_recv()

    def drain(self, u):
        p = self.p
        for e in range(p.chips):

            @pl.when((e <= p.k) & (p.k < p.chips - 1))
            def _():
                self.hop(u, e, 0).wait_send()

            @pl.when((e >= p.k) & (p.k > 0))
            def _():
                self.hop(u, e, 1).wait_send()

            self.hop(u, e, 2).wait_send()


def mixer_kernel(
    n_dp, n_mp, w_in, w_forget, w_outgate, w_mix, w_gate, w_up, w_down, cot, tokens, ident, bound, gain_mix, gain_in, gain_ffn,
    normed_o, rin_o, pin_o, pf_o, pg_o, st_o, phasor_o, r_o, mix_o, ffn_o, mid_o, rmid_o, wm_o, wcat_o, one_o, one_d, cot_o,
    x, wv, wq, pin, pf, pg, st, phasor, rowsq, rin, starts, bl, gain, a_re, a_im, b_re, b_im, mix, wm, tok, ffn_v, mid_v, cot_v, rs_out, rs_in,
    lsem, osem, rs_sem, wtwin, *gsems,
):
    p = Place(n_dp, n_mp)
    rows, width = tokens.shape
    mine = pin.shape[1]
    half, ch = width // 2, mine // 2
    own = rows // n_mp
    hw = width // 2
    shard, h = w_in.shape[0], one_o.shape[2]
    row_parts = bounds(hw, p.bits, 16)

    def mix_view(q, part):
        lo, size = row_parts[part]
        return wm.at[pl.ds(pl.multiple_of(p.c * hw + lo, 16), size), pl.ds(pl.multiple_of(q * mine, LANE), mine)]

    def rows_at(e, c):
        return pl.ds(pl.multiple_of((2 * e + c) * shard, 16), shard)

    def lanes_at(at, size):
        return pl.ds(pl.multiple_of(at, LANE), size)

    def unit_src(u):
        if u < 4:
            return unit_dst(u, p.k, p.c)
        return (w_gate.at[:, :h], w_up.at[:, :h], w_down.at[:h])[u - 4]

    def unit_dst(u, e, c):
        if u == 6:
            return one_d.at[:, lanes_at((2 * e + c) * shard, shard)]
        return (wv.at[u] if u < 3 else wq if u == 3 else one_o.at[u - 4]).at[rows_at(e, c)]

    mine_at = rows_at(p.k, p.c)
    keep = {3: [load(w_mix.at[:, lanes_at(p.m * mine, mine)], wq.at[mine_at], lsem.at[1])]}
    for u, w in enumerate((w_in, w_forget, w_outgate)):
        keep[u] = [
            load(w.at[:, lanes_at(side * half + p.m * ch, ch)], wv.at[u, mine_at, side * ch : (side + 1) * ch], lsem.at[2 + 2 * u + side])
            for side in range(2)
        ]
    tok_load = load(tokens, tok, lsem.at[0])
    vectors = [
        load(bound.at[:, lanes_at(p.m * ch, ch)], bl, lsem.at[10]),
        *[
            load(gain_mix.at[:, lanes_at(side * half + p.m * ch, ch)], gain.at[:, side * ch : (side + 1) * ch], lsem.at[11 + side])
            for side in range(2)
        ],
    ]
    first_own = [load(unit_src(u), unit_dst(u, p.k, p.c), lsem.at[9 + u]) for u in range(4, 7)]
    cot_own = load(cot, cot_v.at[p.m], lsem.at[8])
    p.barrier()
    z = RowGather(p, gsems[:1], unit_src, unit_dst)
    gsems = gsems[1:]
    order = (3, 0, 1, 2)

    def start(u):
        for copy in keep[u]:
            copy.wait()
        z.start(u)

    start(3)
    start(0)
    cot_parts = bounds(width, p.bits, LANE)

    def cot_view(q, part):
        lo, size = cot_parts[part]
        return cot_v.at[q, :, lo : lo + size]

    cot_own.wait()
    gc = CubeGather(p, gsems[10:12], cot_view)
    gc.stage(0)
    tok_load.wait()
    fine = 48

    def norm_in(i, _):
        at = pl.ds(pl.multiple_of(i * fine, 16), fine)
        v = tok[at, :].astype(F32)
        r = lax.rsqrt(jnp.mean(v * v, axis=-1, keepdims=True) + EPS)
        rin[at, :] = r
        x[at, :] = (v * r * gain_in[...]).astype(BF16)
        return 0

    lax.fori_loop(0, rows // fine, norm_in, 0)
    eighth = jnp.full((8, LANE), 0.125, F32)
    ids = lax.dot_general(
        jnp.broadcast_to(ident[...].astype(F32), (8, rows)), eighth, (((0,), (0,)), ((), ())),
        precision=lax.Precision.HIGHEST, preferred_element_type=F32,
    )[:, :1]
    before = jnp.concatenate([ids[:1] - 1.0, ids[:-1]], axis=0)
    starts[...] = jnp.where(jnp.abs(ids - before) > 0.5, 1.0, 0.0)
    for copy in vectors:
        copy.wait()
    outs = [load(x, normed_o, osem.at[0]), load(rin.at[pl.ds(pl.multiple_of(p.m * own, 8), own)], rin_o, osem.at[1])]
    gw = CubeGather(p, gsems[0:2], mix_view)

    def to_twin(part, sub):
        ref = mix_view(p.m ^ sub, part)
        return remote(ref, ref, wtwin.at[0, part, sub], wtwin.at[1, part, sub], p.twin())

    def from_twin(part, sub):
        lo, size = row_parts[part]
        ref = wm.at[
            pl.ds(pl.multiple_of((1 - p.c) * hw + lo, 16), size),
            pl.ds(pl.multiple_of((p.m ^ sub) * mine, LANE), mine),
        ]
        return remote(ref, ref, wtwin.at[0, part, sub], wtwin.at[1, part, sub], p.twin())

    step = 240

    def project(u, out):
        z.forward(u, p.chips - 1)
        z.finish(u)

        def body(i, _):
            at = pl.ds(pl.multiple_of(i * step, 16), step)
            out[at, :] = dot(x[at, :], wv[u])
            return 0

        lax.fori_loop(0, rows // step, body, 0)

    core_rows = pl.ds(pl.multiple_of(p.c * hw, 16), hw)
    for tau in range(1, p.chips + 2):
        for i, u in enumerate(order):
            if 1 <= tau - i <= p.chips - 2:
                z.forward(u, tau - i)
        if tau + 1 < len(order):
            start(order[tau + 1])
        if tau == p.chips - 1:
            for s in range(1, p.bits):
                gc.stage(s)
            z.forward(3, p.chips - 1)
            z.finish(3)
            own_mix = load(wq.at[core_rows], wm.at[core_rows, lanes_at(p.m * mine, mine)], lsem.at[9])
            own_mix.wait()
            gw.stage(0)
            for part in range(p.bits):
                to_twin(part, 0).start()
        if tau == p.chips:
            project(0, pin)
    for u in range(4, 7):
        z.start(u)
    project(1, pf)
    for s in range(1, p.bits):
        gw.stage(s)
    scan_forward(pin, pf, starts, bl, st, phasor, rowsq, a_re, a_im, b_re, b_im)
    outs += [
        load(src, dst, osem.at[5 + i])
        for i, (src, dst) in enumerate(((pin, pin_o), (pf, pf_o), (pg, pg_o), (st, st_o), (phasor, phasor_o)))
        if i != 2
    ]
    ones = jnp.ones((8, mine), F32)
    rs_out[...] = lax.dot_general(
        ones, st[...] * st[...], (((1,), (1,)), ((), ())), precision=lax.Precision.HIGHEST, preferred_element_type=F32
    )

    def rs_copy(mask):
        return remote(rs_out, rs_in.at[mask], rs_sem.at[0, mask], rs_sem.at[1, mask], p.peer(mask))

    for mask in range(1, n_mp):
        rs_copy(mask).start()
    project(2, pg)
    outs += [load(wv.at[u], wcat_o.at[u], osem.at[2 + u]) for u in range(3)]
    outs.append(load(pg, pg_o, osem.at[7]))
    gw.last()
    for part in range(p.bits):
        for sub in range(1, n_mp):
            to_twin(part, sub).start()
    z.forward(4, 1)
    total = rs_out[...]
    for mask in range(1, n_mp):
        rs_copy(mask).wait_recv()
        total = total + rs_in[mask]
    inv = lax.rsqrt(total / width + EPS)
    rowsq[...] = lax.dot_general(
        inv, eighth, (((0,), (0,)), ((), ())), precision=lax.Precision.HIGHEST, preferred_element_type=F32
    )[:, :1]
    outs.append(load(rowsq, r_o, osem.at[10]))
    re_at = pl.ds(pl.multiple_of(p.m * ch, LANE), ch)
    im_at = pl.ds(pl.multiple_of(half + p.m * ch, LANE), ch)

    def gate_out(i, _):
        at = pl.ds(pl.multiple_of(i * fine, 16), fine)
        gate = pg[at, :]
        value = (st[at, :] * rowsq[at, :] * gain[...] * (gate * sigmoid(gate))).astype(BF16)
        mix[at, re_at] = value[:, :ch]
        mix[at, im_at] = value[:, ch:]
        return 0

    spans = 2
    span = rows // spans
    gathers = []
    for n in range(spans):
        lax.fori_loop(n * span // fine, (n + 1) * span // fine, gate_out, 0)
        for side in range(2):

            def view(q, part, n=n, side=side):
                lo, size = bounds(span, p.bits, 16)[part]
                return mix.at[n * span + lo : n * span + lo + size, pl.ds(pl.multiple_of(side * half + q * ch, LANE), ch)]

            at = 2 + 2 * (2 * n + side)
            gathers.append(CubeGather(p, gsems[at : at + 2], view))
            gathers[-1].stage(0)
    z.forward(5, 1)
    for s in range(1, p.bits):
        for g in gathers:
            g.stage(s)
    z.forward(6, 1)
    gc.last()
    outs.append(load(cot_v, cot_o, osem.at[17]))
    for part in range(p.bits):
        for sub in range(n_mp):
            from_twin(part, sub).wait_recv()
    outs.append(load(wm, wm_o, osem.at[11]))
    for n in range(spans):
        gathers[2 * n].last()
        gathers[2 * n + 1].last()

        def mix_rows(i, _):
            at = pl.ds(pl.multiple_of(i * step, 16), step)
            middle = tok[at, :].astype(F32) + dot(mix[at, :], wm[...])
            r = lax.rsqrt(jnp.mean(middle * middle, axis=-1, keepdims=True) + EPS)
            ffn_v[at, :] = (middle * r * gain_ffn[...]).astype(BF16)
            for j in range(step // own):

                @pl.when(p.m == i * (step // own) + j)
                def _():
                    mid_v[...] = middle[j * own : (j + 1) * own]
                    rmid_o[...] = r[j * own : (j + 1) * own]

            return 0

        lax.fori_loop(n * span // step, (n + 1) * span // step, mix_rows, 0)
        at = slice(n * span, (n + 1) * span)
        outs.append(load(ffn_v.at[at], ffn_o.at[at], osem.at[12 + 2 * n]))
        outs.append(load(mix.at[at], mix_o.at[at], osem.at[13 + 2 * n]))
        if n == 0:
            z.forward(4, 2)
    outs.append(load(mid_v, mid_o, osem.at[12 + 2 * spans]))
    z.forward(5, 2)
    z.forward(6, 2)
    for s in range(3, p.chips):
        for u in range(4, 7):
            z.forward(u, s)
    for u in range(4, 7):
        z.finish(u)
    for copy in first_own:
        copy.wait()
    for copy in outs:
        copy.wait()
    for u in range(7):
        z.drain(u)
    gw.drain()
    gc.drain()
    for g in gathers:
        g.drain()
    for part in range(p.bits):
        for sub in range(n_mp):
            to_twin(part, sub).wait_send()
    for mask in range(1, n_mp):
        rs_copy(mask).wait_send()


def mixer_forward(n_dp, n_mp, cid, h, *args):
    rows, width = args[8].shape
    mine = width // n_mp
    own, lanes = rows // n_mp, mine // 2 // LANE
    bits = n_mp.bit_length() - 1
    full, part, lane = (rows, width), (rows, mine), (lanes, rows, LANE)

    def f32(*shape):
        return jax.ShapeDtypeStruct(shape, F32)

    def bf16(*shape):
        return jax.ShapeDtypeStruct(shape, BF16)

    return pl.pallas_call(
        functools.partial(mixer_kernel, n_dp, n_mp),
        out_shape=(
            bf16(*full), f32(own, 1), *(f32(*part),) * 5, f32(rows, 1), bf16(*full), bf16(*full), f32(own, width), f32(own, 1),
            bf16(width, width), bf16(3, width, mine), bf16(2, width, h), bf16(h, width), bf16(n_mp, own, width),
        ),
        in_specs=[ANY] * 9 + [VMEM] + [ANY] * 2 + [VMEM] * 2,
        out_specs=(ANY,) * 11 + (VMEM,) + (ANY,) * 5,
        scratch_shapes=[
            pltpu.VMEM(full, BF16),
            pltpu.VMEM((3, width, mine), BF16),
            pltpu.VMEM((width, mine), BF16),
            *[pltpu.VMEM(part, F32)] * 5,
            *[pltpu.VMEM((rows, 1), F32)] * 3,
            pltpu.VMEM((1, mine // 2), F32),
            pltpu.VMEM((1, mine), F32),
            *[pltpu.VMEM(lane, F32)] * 4,
            pltpu.VMEM(full, BF16),
            pltpu.VMEM((width, width), BF16),
            pltpu.VMEM(full, BF16),
            pltpu.VMEM(full, BF16),
            pltpu.VMEM((own, width), F32),
            pltpu.VMEM((n_mp, own, width), BF16),
            pltpu.VMEM((8, rows), F32),
            pltpu.VMEM((n_mp, 8, rows), F32),
            pltpu.SemaphoreType.DMA((17,)),
            pltpu.SemaphoreType.DMA((18,)),
            pltpu.SemaphoreType.DMA((2, n_mp)),
            pltpu.SemaphoreType.DMA((2, bits, n_mp)),
            *RowGather.scratch(n_dp, 7),
            *CubeGather.scratch(n_mp) * 6,
        ],
        compiler_params=pltpu.CompilerParams(collective_id=cid, has_side_effects=True, vmem_limit_bytes=VMEM_LIMIT),
        name="mixer_forward",
    )(*args)


STEP = 240


def ffn_rows(at, own, a, w_gate, w_up, w_down, put):
    gate = dot(a[0, at, :], w_gate)
    up = dot(a[0, at, :], w_up)
    sig = sigmoid(gate)
    silu = gate * sig
    grad = dot_trans(a[1, at, :], w_down)
    put(0, (grad * up * sig * (1.0 + gate * (1.0 - sig))).astype(BF16))
    put(1, (grad * silu).astype(BF16))
    put(2, (silu * up).astype(BF16))


class FfnSums:
    def __init__(self, p, a, wv, wd, h, bv, bq, gsum, gsem, sums, cube_g, cube_d):
        rows, width = a.shape[1:]
        own, shard = rows // p.n_mp, gsum.shape[1]
        def rows_of(b, q):
            return bq[b, q] if own % 16 else bv[b, pl.ds(pl.multiple_of(q * own, 16), own), :]

        def part_g(q, lo, size):
            at = slice(lo, lo + size)
            return dot_trans(rows_of(0, q), wv[0, at, :h]) + dot_trans(rows_of(1, q), wv[1, at, :h])

        def part_d(q, lo, size):
            return dot(rows_of(2, q), wd[:h, lo : lo + size])

        def piece(b, e):
            left = jnp.where(b < 2, 0, 1)
            return dot_rows(a[left, :, pl.ds(pl.multiple_of(e * shard, LANE), shard)], bv[b])

        def finish(b, acc):
            out = pltpu.make_async_copy(acc, gsum.at[b], gsem)
            out.start()
            out.wait()

        self.total = RowSum(p, sums, piece, finish, False)
        self.g_cube, self.d_cube = CubeSum(p, cube_g, part_g, width), CubeSum(p, cube_d, part_d, width)


def first_kernel(
    n_dp, n_mp, ffn_in, grad_out, w, w_d, w_gate, w_up, w_down, gsum, gffn, down, next_w, next_d, next_b, next_q,
    a, wv, wd, wv2, wd2, bv, bq, stage, stage_q, result, lsem, gsem, bsem, *refs,
):
    p = Place(n_dp, n_mp)
    rows, width = ffn_in.shape
    own, h, h_next, shard = rows // n_mp, bv.shape[2], next_d.shape[0], gsum.shape[1]
    sums, cube_g, cube_d, zsem = refs[:5], refs[5:8], refs[8:11], refs[11:12]
    loads = [load(ffn_in, a.at[0], lsem.at[0]), load(w, wv, lsem.at[1]), load(grad_out, a.at[1], lsem.at[2]), load(w_d, wd, lsem.at[3])]
    p.barrier()
    srcs = (w_gate.at[:, h:], w_up.at[:, h:], w_down.at[h:])

    def next_dst(u, e, c):
        at = pl.ds(pl.multiple_of((2 * e + c) * shard, LANE), shard)
        return next_d.at[:, at] if u == 2 else next_w.at[u, at]

    z = RowGather(p, zsem, lambda u: srcs[u], next_dst)
    own_next = [load(srcs[u], next_dst(u, p.k, p.c), lsem.at[5 + u]) for u in range(3)]
    for u in range(3):
        z.start(u)
    for copy in loads:
        copy.wait()

    f = FfnSums(p, a, wv, wd, h, bv, bq, gsum, gsem, sums, cube_g, cube_d)
    total, g_cube, d_cube = f.total, f.g_cube, f.d_cube
    n, chunks = total.blocks, rows // STEP
    for j in (*range(1, chunks), 0):
        i = lax.div(p.m * chunks, n_mp) ^ j
        at = pl.ds(pl.multiple_of(i * STEP, 16), STEP)

        def put(b, value):
            bv[b, at, :] = value
            if own % 16:
                wide = value.astype(F32)
                for q in range(STEP // own):
                    bq[b, i * (STEP // own) + q] = wide[q * own : (q + 1) * own].astype(BF16)

        ffn_rows(at, own, a, wv[0], wv[1], wd[...], put)
        if own == STEP and j:
            g_cube.stage(0, j)
    if own != STEP:
        g_cube.stage(0)
    z.forward(0, 1)
    total.run(0, n)
    z.forward(1, 1)
    d_cube.stage(0)
    z.forward(2, 1)
    for i in range(3):
        total.run(n + i, n + i + 1)
        z.forward(i, 2)
        if i == 1:
            for s in range(1, p.bits):
                g_cube.stage(s)
    last = total.steps - n
    for i in range(2 * n, last):
        total.run(i, i + 1)
        z.forward(i % n, i // n + 1)
    for s in range(1, p.bits):
        d_cube.stage(s)
    for u in range(3):
        z.finish(u)
        own_next[u].wait()
    loads = [load(next_w, wv2, lsem.at[8]), load(next_d, wd2, lsem.at[9])]
    for copy in loads:
        copy.wait()
    sent = []
    for i in range(chunks):
        slot = i % 2
        for copy in sent[i - 2 : i - 1] and sent[i - 2]:
            copy.wait()

        def put(b, value, slot=slot):
            stage[slot, b] = value
            if own % 16:
                wide = value.astype(F32)
                for j in range(STEP // own):
                    stage_q[slot, b, j] = wide[j * own : (j + 1) * own].astype(BF16)

        ffn_rows(
            slice(i * STEP, (i + 1) * STEP), own, a, wv2[0], wv2[1], wd2[...], put
        )
        copies = [load(stage.at[slot], next_b.at[:, i * STEP : (i + 1) * STEP], bsem.at[0, i])]
        if own % 16:
            per = STEP // own
            copies.append(load(stage_q.at[slot], next_q.at[:, i * per : (i + 1) * per], bsem.at[1, i]))
        sent.append(copies)
    total.run(last, total.steps)
    for at, value in g_cube.results():
        result[:, at] = value
    load(result, gffn, lsem.at[10]).wait()
    for at, value in d_cube.results():
        result[:, at] = value
    load(result, down, lsem.at[4]).wait()
    for copies in sent[-2:]:
        for copy in copies:
            copy.wait()
    g_cube.drain()
    d_cube.drain()
    total.drain()
    for u in range(3):
        z.drain(u)


def last_kernel(
    n_dp, n_mp, ffn_in, grad_out, w, w_d, b_in, q_in, gffn1, down1, middle, r_mid, cot, tok, gain_ffn, w_mix,
    gsum, base, parting, gmid, gain_part, gm, gb, rowdot,
    a, wv, wd, bv, bq, gffn, mid_v, cot_v, tok_v, wmb, gbr, gm_out, gm_in, gb_in, rd_col, rd_out, rd_in,
    lsem, gsem, wsem, ssem, rsem, *refs,
):
    p = Place(n_dp, n_mp)
    rows, width = ffn_in.shape
    own, h = rows // n_mp, bv.shape[2]
    mine = gm.shape[2]
    half, ch = width // 2, mine // 2
    sums, cube_g, cube_d = refs[:5], refs[5:8], refs[8:11]
    loads_w = [load(b_in, bv, lsem.at[1]), load(w, wv, lsem.at[3])]
    if own % 16:
        loads_w.append(load(q_in, bq, lsem.at[5]))
    loads = [load(ffn_in, a.at[0], lsem.at[0]), load(grad_out, a.at[1], lsem.at[2])]
    loads_d = [load(w_d, wd, lsem.at[4])]
    late = [
        load(src, dst, lsem.at[6 + i])
        for i, (src, dst) in enumerate(((middle, mid_v), (cot, cot_v), (tok.at[p.m], tok_v), (gffn1, gffn)))
    ]

    def mix_load(j, s):
        q = p.m ^ j
        return pltpu.make_async_copy(
            w_mix.at[pl.ds(pl.multiple_of(s * half + q * ch, LANE), ch)], wmb.at[s], wsem.at[s]
        )

    p.barrier()
    mix_load(1, 0).start()
    f = FfnSums(p, a, wv, wd, h, bv, bq, gsum, gsem, sums, cube_g, cube_d)
    total, g_cube, d_cube = f.total, f.g_cube, f.d_cube
    n = total.blocks
    for copy in loads_w:
        copy.wait()
    g_cube.stage(0)
    for copy in loads:
        copy.wait()
    total.run(0, n + 1)
    for s in range(1, p.bits):
        g_cube.stage(s)
    total.run(n + 1, n + 2)
    for copy in loads_d:
        copy.wait()
    d_cube.stage(0)
    total.run(n + 2, 2 * n)
    for copy in late:
        copy.wait()
    for at, value in g_cube.results():
        gffn[:, at] += value
    fine = 16 if own % 16 == 0 else own

    def norm_back(i, gains):
        at = pl.ds(pl.multiple_of(i * fine, fine), fine)
        g = gffn[at, :]
        n_own = mid_v[at, :] * r_mid[at, :]
        gains = gains + jnp.sum((g * n_own).reshape(fine // 8, 8, width), axis=0)
        gn = g * gain_ffn[...]
        back = r_mid[at, :] * (gn - n_own * jnp.mean(gn * n_own, axis=-1, keepdims=True))
        grad = cot_v[at, :].astype(F32) + back
        gffn[at, :] = grad
        low = grad.astype(BF16)
        gbr[at, :] = low
        dots = jnp.mean(low.astype(F32) * (mid_v[at, :] - tok_v[at, :].astype(F32)), axis=-1, keepdims=True)
        rd_col[at, :] = jnp.broadcast_to(dots, (fine, LANE))
        return gains

    gains = lax.fori_loop(0, own // fine, norm_back, jnp.zeros((8, width), F32))
    gmid_out = load(gffn, gmid, lsem.at[15])
    gain_part[...] = jnp.sum(gains, axis=0, keepdims=True)
    rd_out[...] = lax.dot_general(
        jnp.full((8, LANE), 1.0 / LANE, F32), rd_col[...], (((1,), (1,)), ((), ())),
        precision=lax.Precision.HIGHEST, preferred_element_type=F32,
    )

    def across(kind, j, owner):
        send, recv, to = ssem.at[kind, j], rsem.at[kind, owner], p.peer(j)
        if kind == 0:
            return remote(gm_out.at[j], gm_in.at[owner], send, recv, to)
        if kind == 1:
            return remote(rd_out, rd_in.at[owner], send, recv, to)
        here = pl.ds(pl.multiple_of((p.m ^ j) * mine, LANE), mine)
        return remote(gbr.at[:, here], gb_in.at[owner], send, recv, to)

    for j in range(1, n_mp):
        across(1, j, p.m).start()
    turns = [(j, s) for j in (*range(1, n_mp), 0) for s in range(2)]
    for at, (j, s) in enumerate(turns):
        mix_load(j, s).wait()
        if at + 1 < len(turns):
            mix_load(*turns[at + 1]).start()
        value = dot_trans(gbr[...], wmb[s]).astype(BF16)
        if j:
            gm_out[j, :, s * ch : (s + 1) * ch] = value
            if s:
                across(0, j, p.m).start()
        else:
            gm_in[p.m, :, s * ch : (s + 1) * ch] = value
    for j in range(1, n_mp):
        across(2, j, p.m).start()
    gb_in[p.m] = gbr[:, pl.ds(pl.multiple_of(p.m * mine, LANE), mine)]
    rd_in[p.m] = rd_out[...]
    gmid_out.wait()
    down_load = load(down1, gffn, lsem.at[10])
    total.run(2 * n, total.steps - n)
    for s in range(1, p.bits - 1):
        d_cube.stage(s)
    for part, at, value in d_cube.parting():
        parting[part, :, at] = value.astype(BF16)
    down_load.wait()
    for at, value in d_cube.results(p.bits - 1):
        gffn[:, at] += mid_v[:, at] + value
    back = [load(gffn, base, lsem.at[14])]
    total.run(total.steps - n, total.steps)
    for j in range(1, n_mp):
        for kind in range(3):
            across(kind, j, p.m ^ j).wait_recv()
    back.extend(load(src, dst, lsem.at[11 + i]) for i, (src, dst) in enumerate(((gm_in, gm), (gb_in, gb), (rd_in, rowdot))))
    for j in range(1, n_mp):
        for kind in range(3):
            across(kind, j, p.m).wait_send()
    for copy in back:
        copy.wait()
    g_cube.drain()
    d_cube.drain(p.bits - 1)
    total.drain()


def split_shape(n_mp, own, h):
    return (3, n_mp, own, h) if own % 16 else (1, 1, 16, LANE)


def parting_shape(n_mp, own, width):
    bits = n_mp.bit_length() - 1
    return (bits, own, max(size for _, size in bounds(width, bits, LANE)))


def ffn_first(n_dp, n_mp, cid, *args):
    (rows, width), h = args[0].shape, args[2].shape[2]
    shard, own, h_next = width // n_dp, rows // n_mp, args[6].shape[0] - h
    f_own = jax.ShapeDtypeStruct((own, width), F32)
    per = STEP // own if own % 16 else 1
    return pl.pallas_call(
        functools.partial(first_kernel, n_dp, n_mp),
        out_shape=(
            jax.ShapeDtypeStruct((3, shard, h), F32), f_own, f_own,
            jax.ShapeDtypeStruct((2, width, h_next), BF16), jax.ShapeDtypeStruct((h_next, width), BF16),
            jax.ShapeDtypeStruct((3, rows, h_next), BF16), jax.ShapeDtypeStruct(split_shape(n_mp, own, h_next), BF16),
        ),
        in_specs=[ANY] * 7,
        out_specs=(ANY,) * 7,
        scratch_shapes=[
            pltpu.VMEM((2, rows, width), BF16),
            pltpu.VMEM((2, width, h), BF16),
            pltpu.VMEM((h, width), BF16),
            pltpu.VMEM((2, width, h_next), BF16),
            pltpu.VMEM((h_next, width), BF16),
            pltpu.VMEM((3, rows, h), BF16),
            pltpu.VMEM(split_shape(n_mp, own, h), BF16),
            pltpu.VMEM((2, 3, STEP, h_next), BF16),
            pltpu.VMEM((2, 3, per, own, h_next) if own % 16 else (1, 1, 1, 16, LANE), BF16),
            pltpu.VMEM((own, width), F32),
            pltpu.SemaphoreType.DMA((11,)),
            pltpu.SemaphoreType.DMA,
            pltpu.SemaphoreType.DMA((2, rows // STEP)),
            *RowSum.scratch(n_dp, 3, shard, h),
            *CubeSum.scratch(n_mp, own, width),
            *CubeSum.scratch(n_mp, own, width),
            *RowGather.scratch(n_dp, 3),
        ],
        compiler_params=pltpu.CompilerParams(collective_id=cid, has_side_effects=True, vmem_limit_bytes=VMEM_LIMIT),
        name="ffn_first",
    )(*args)


def ffn_last(n_dp, n_mp, cid, *args):
    (rows, width), h = args[0].shape, args[2].shape[2]
    shard, own, mine = width // n_dp, rows // n_mp, width // n_mp
    piece = jax.ShapeDtypeStruct((n_mp, own, mine), BF16)
    return pl.pallas_call(
        functools.partial(last_kernel, n_dp, n_mp),
        out_shape=(
            jax.ShapeDtypeStruct((3, shard, h), F32), jax.ShapeDtypeStruct((own, width), F32),
            jax.ShapeDtypeStruct(parting_shape(n_mp, own, width), BF16),
            jax.ShapeDtypeStruct((own, width), F32), jax.ShapeDtypeStruct((1, width), F32),
            piece, piece, jax.ShapeDtypeStruct((n_mp, 8, own), F32),
        ),
        in_specs=[ANY] * 9 + [VMEM, ANY, ANY, VMEM, ANY],
        out_specs=(ANY, ANY, VMEM, ANY, VMEM, ANY, ANY, ANY),
        scratch_shapes=[
            pltpu.VMEM((2, rows, width), BF16),
            pltpu.VMEM((2, width, h), BF16),
            pltpu.VMEM((h, width), BF16),
            pltpu.VMEM((3, rows, h), BF16),
            pltpu.VMEM(split_shape(n_mp, own, h), BF16),
            pltpu.VMEM((own, width), F32),
            pltpu.VMEM((own, width), F32),
            pltpu.VMEM((own, width), BF16),
            pltpu.VMEM((own, width), BF16),
            pltpu.VMEM((2, mine // 2, width), BF16),
            pltpu.VMEM((own, width), BF16),
            *[pltpu.VMEM((n_mp, own, mine), BF16)] * 3,
            pltpu.VMEM((own, LANE), F32),
            pltpu.VMEM((8, own), F32),
            pltpu.VMEM((n_mp, 8, own), F32),
            pltpu.SemaphoreType.DMA((16,)),
            pltpu.SemaphoreType.DMA,
            pltpu.SemaphoreType.DMA((2,)),
            pltpu.SemaphoreType.DMA((3, n_mp)),
            pltpu.SemaphoreType.DMA((3, n_mp)),
            *RowSum.scratch(n_dp, 3, shard, h),
            *CubeSum.scratch(n_mp, own, width),
            *CubeSum.scratch(n_mp, own, width, False),
        ],
        compiler_params=pltpu.CompilerParams(collective_id=cid, has_side_effects=True, vmem_limit_bytes=VMEM_LIMIT),
        name="ffn_last",
    )(*args)


def project_kernel(
    n_dp, n_mp, normed, mixed, gm, g_b, pin, pf, pg, st, phasor, r_mix, rowdot, bound, gain_mix, w, gmid, tok, r_in, gain_in,
    gain_ffn_part, base, parting, gw, gtok, small, done,
    a, bv, bq, gall, dgain, dbound, tok_v, base_v, last_v, lsem, rsend, rrecv, dsem, *refs,
):
    p = Place(n_dp, n_mp)
    rows, width = normed.shape
    mine = bv.shape[2]
    half, ch, own = width // 2, mine // 2, rows // n_mp
    shard = gw.shape[2]
    sums, cube_refs, vec = refs[:5], refs[5:8], SmallSum(p, refs[8:10])
    loads = [load(mixed, a.at[0], lsem.at[0]), load(g_b, bv.at[0], lsem.at[1])]
    late = [load(normed, a.at[1], lsem.at[12])]
    late.append(load(tok.at[p.m], tok_v, lsem.at[16]))
    early_d = [load(parting, last_v.at[0], lsem.at[19])]
    late_d = load(base, base_v, lsem.at[20])
    p.barrier(far=True)
    for copy in loads:
        copy.wait()

    down_cols = bounds(width, p.bits, LANE)

    def last_stage(part):
        size = down_cols[part][1]
        to = p.peer(1 << ((part + p.bits - 1) % p.bits))
        return remote(last_v.at[0, part, :, :size], last_v.at[1, part, :, :size], dsem.at[0, part], dsem.at[1, part], to)

    for copy in early_d:
        copy.wait()
    for part in range(p.bits):
        last_stage(part).start()

    def piece(b, e):
        left = jnp.where(b == 0, 0, 1)
        return dot_rows(a[left, :, pl.ds(pl.multiple_of(e * shard, LANE), shard)], bv[b])

    out_cols = bounds(mine, p.bits, LANE)

    def spread(b):
        def view(q, part):
            lo, size = out_cols[part]
            return gall.at[b, q, :, lo : lo + size]

        return CubeGather(p, (rsend.at[b], rrecv.at[b]), view)

    def finish(b, acc):
        gall[b, p.m] = acc[...].astype(BF16)
        spread(b).stage(0)
        for s in range(1, p.bits):

            @pl.when(b >= s)
            def _():
                spread(b - s).stage(s)

    def partial(q, lo, size):
        value = 0.0
        for b in range(3):
            left = bq[b, q] if own % 16 else bv[1 + b, pl.ds(pl.multiple_of(q * own, 16), own), :]
            value = value + dot_trans(left, held[0][b, lo : lo + size, :])
        return value

    held = []
    total = RowSum(p, sums, piece, finish, True)
    cube = CubeSum(p, cube_refs, partial, width)
    tick, early = p.chips, p.chips - 1
    def recurrence(gm_v, pin_v, pf_v, pg_v, st_v, ph_v, r_v, rd_v, bl, gain, a_re, a_im, b_re, b_im):
        scans = [
            load(src, dst, lsem.at[2 + i])
            for i, (src, dst) in enumerate(
                ((gm, gm_v), (pg, pg_v), (st, st_v), (pf, pf_v), (phasor, ph_v), (pin, pin_v), (r_mix, r_v))
            )
        ]
        scans.append(load(bound.at[:, pl.ds(pl.multiple_of(p.m * ch, LANE), ch)], bl, lsem.at[9]))
        for side in range(2):
            at = pl.ds(pl.multiple_of(side * half + p.m * ch, LANE), ch)
            scans.append(load(gain_mix.at[:, at], gain.at[:, side * ch : (side + 1) * ch], lsem.at[10 + side]))
        eighth = jnp.full((8, LANE), 0.125, F32)
        for q in range(n_mp):
            rd_v[q * own : (q + 1) * own, :] = lax.dot_general(
                rowdot[q], eighth, (((0,), (0,)), ((), ())), precision=lax.Precision.HIGHEST, preferred_element_type=F32
            )[:, :1]
        total.run(0, 1, ahead=False)
        for copy in scans:
            copy.wait()
        scan_backward(
            gm_v, pin_v, pf_v, pg_v, st_v, ph_v, r_v, rd_v, bl, gain, bv.at[1], bv.at[2], bv.at[3], dgain, dbound,
            a_re, a_im, b_re, b_im,
            between=(lambda: total.run(1, 2, True, False), lambda: total.run(2, early, True, False)),
        )

    part, column = (rows, mine), pltpu.VMEM((rows, 1), F32)
    pl.run_scoped(
        recurrence,
        pltpu.VMEM(part, BF16), *[pltpu.VMEM(part, F32)] * 5, column, column, pltpu.VMEM((1, ch), F32), pltpu.VMEM((1, mine), F32),
        *[pltpu.VMEM((ch // LANE, rows, LANE), F32)] * 4,
    )

    def sums_over_devices(wv):
        held.append(wv)
        late.extend(load(w.at[i], wv.at[i], lsem.at[13 + i]) for i in range(3))
        for copy in late:
            copy.wait()
        if own % 16:
            for b in range(3):
                wide = bv[1 + b].astype(F32)
                for q in range(n_mp):
                    bq[b, q] = wide[q * own : (q + 1) * own].astype(BF16)
        total.run(early, early + tick, True)
        cube.stage(0)
        total.run(early + tick, early + 2 * tick)
        late_d.wait()
        done_out = []
        for part, (lo, size) in enumerate(down_cols):
            last_stage(part).wait()
            value = base_v[:, lo : lo + size] + last_v[1, part, :, :size].astype(F32)
            last_v[1, part, :, :size] = value.astype(BF16)
            done_out.append(load(last_v.at[1, part, :, :size], done.at[:, lo : lo + size], dsem.at[2, part]))
        gmid_load = load(gmid, base_v, lsem.at[17])
        total.run(early + 2 * tick, early + 3 * tick)
        for s in range(1, p.bits):
            cube.stage(s)
        total.run(early + 3 * tick, early + 4 * tick)
        for at, value in cube.results():
            gtok[:, at] = value
        gmid_load.wait()
        fine = 16 if own % 16 == 0 else own

        def norm_back(i, gains):
            at = pl.ds(pl.multiple_of(i * fine, fine), fine)
            g = gtok[at, :]
            n_own = tok_v[at, :].astype(F32) * r_in[at, :]
            gains = gains + jnp.sum((g * n_own).reshape(fine // 8, 8, width), axis=0)
            gn = g * gain_in[...]
            gtok[at, :] = base_v[at, :] + r_in[at, :] * (gn - n_own * jnp.mean(gn * n_own, axis=-1, keepdims=True))
            return gains

        gains = lax.fori_loop(0, own // fine, norm_back, jnp.zeros((8, width), F32))
        vec.buf[0] = jnp.zeros((4, width), F32)
        vec.buf[0, 0:1] = jnp.sum(gains, axis=0, keepdims=True)
        vec.buf[0, 1:2] = gain_ffn_part[...]
        here = pl.ds(pl.multiple_of(p.m * ch, LANE), ch)
        vec.buf[0, 2:3, here] = dgain[:, :ch]
        vec.buf[0, 2:3, pl.ds(pl.multiple_of(half + p.m * ch, LANE), ch)] = dgain[:, ch:]
        vec.buf[0, 3:4, here] = dbound[...]
        vec.twins()
        total.run(early + 4 * tick, early + 5 * tick)
        vec.cube()
        total.run(early + 5 * tick, total.steps)
        for b in range(total.blocks):
            for s in range(max(1, total.blocks - b), p.bits):
                spread(b).stage(s)
        vec.line()
        for b in range(total.blocks):
            spread(b).last()
        out = load(gall, gw, lsem.at[18])
        small[...] = vec.result()
        for copy in done_out:
            copy.wait()
        out.wait()
        for b in range(total.blocks):
            spread(b).drain()
        cube.drain()
        total.drain()


    pl.run_scoped(sums_over_devices, pltpu.VMEM((3, width, mine), BF16))


def project_back(n_dp, n_mp, cid, *args):
    rows, width = args[0].shape
    mine, shard, own = width // n_mp, width // n_dp, rows // n_mp
    ch = mine // 2
    return pl.pallas_call(
        functools.partial(project_kernel, n_dp, n_mp),
        out_shape=(
            jax.ShapeDtypeStruct((4, n_mp, shard, mine), BF16),
            jax.ShapeDtypeStruct((own, width), F32),
            jax.ShapeDtypeStruct((4, width), F32),
            jax.ShapeDtypeStruct((own, width), BF16),
        ),
        in_specs=[ANY] * 10 + [VMEM] + [ANY] * 5 + [VMEM] * 3 + [ANY] * 2,
        out_specs=(ANY, VMEM, VMEM, ANY),
        scratch_shapes=[
            pltpu.VMEM((2, rows, width), BF16),
            pltpu.VMEM((4, rows, mine), BF16),
            pltpu.VMEM((3, n_mp, own, mine) if own % 16 else (1, 1, 16, LANE), BF16),
            pltpu.VMEM((4, n_mp, shard, mine), BF16),
            pltpu.VMEM((1, mine), F32),
            pltpu.VMEM((1, ch), F32),
            pltpu.VMEM((own, width), BF16),
            pltpu.VMEM((own, width), F32),
            pltpu.VMEM((2, *parting_shape(n_mp, own, width)), BF16),
            pltpu.SemaphoreType.DMA((21,)),
            *[pltpu.SemaphoreType.DMA((4, n_mp.bit_length() - 1, n_mp))] * 2,
            pltpu.SemaphoreType.DMA((3, n_mp)),
            *RowSum.scratch(n_dp, 4, shard, mine),
            *CubeSum.scratch(n_mp, own, width),
            *SmallSum.scratch(n_dp, n_mp, (4, width)),
        ],
        compiler_params=pltpu.CompilerParams(collective_id=cid, has_side_effects=True, vmem_limit_bytes=VMEM_LIMIT),
        name="project_back",
    )(*args)


def result_kernel(
    n_mp, gmix, one, two, mixed, gtok, small,
    o_mixed, o_tok, o_gin, o_win, o_wf, o_wo, o_bound, o_gmix, o_wm, o_gffn, o_gate, o_up, o_down,
    gm, gw, gffn, down, mixed_v, tok_v, sem, osem,
):
    d = lax.axis_index("dp")
    shard, mine = gmix.shape[2:]
    ch, half = mine // 2, n_mp * mine // 2
    h, h2 = one.shape[2], two.shape[2]
    mixer = [load(gmix.at[b], gm.at[b], sem.at[b]) for b in range(4)]
    through = [load(mixed, mixed_v, sem.at[4]), load(gtok, tok_v, sem.at[5])]
    ffn = [
        (load(one.at[i], gffn.at[i, :, :h], sem.at[6 + 2 * i]), load(two.at[i], gffn.at[i, :, h:], sem.at[7 + 2 * i]))
        for i in range(3)
    ]
    outs = []
    for b, out in enumerate((o_wm, o_win, o_wf, o_wo)):
        mixer[b].wait()
        for q in range(n_mp):
            value = gm[b, q].astype(F32)
            if b:
                gw[b, :, q * ch : (q + 1) * ch] = value[:, :ch]
                gw[b, :, half + q * ch : half + (q + 1) * ch] = value[:, ch:]
            else:
                gw[b, :, q * mine : (q + 1) * mine] = value
        outs.append(load(gw.at[b], out, osem.at[b]))
    for i, (copy, src, out) in enumerate(zip(through, (mixed_v, tok_v), (o_mixed, o_tok))):
        copy.wait()
        outs.append(load(src, out, osem.at[4 + i]))
    for i, out in enumerate((o_gate, o_up)):
        for copy in ffn[i]:
            copy.wait()
        outs.append(load(gffn.at[i], out, osem.at[6 + i]))
    at = pl.ds(pl.multiple_of(d * shard, LANE), shard)
    for row, out in enumerate((o_gin, o_gffn, o_gmix)):
        out[...] = small[row : row + 1, at]
    size = shard // 2
    if size % LANE == 0:
        o_bound[...] = small[3:4, pl.ds(pl.multiple_of(d * size, LANE), size)]
    else:
        pair = small[3:4, pl.ds(pl.multiple_of(lax.div(d, 2) * 2 * size, LANE), 2 * size)]
        o_bound[...] = jnp.where(lax.rem(d, 2) == 0, pair[:, :size], pair[:, size:])
    for copy in ffn[2]:
        copy.wait()
    for lo in range(0, h + h2, LANE):
        down[lo : lo + LANE, :] = gffn[2, :, lo : lo + LANE].T
    outs.append(load(down, o_down, osem.at[8]))
    for copy in outs:
        copy.wait()


def results(n_dp, n_mp, gmix, one, two, mixed, gtok, small):
    shard, mine = gmix.shape[2:]
    width, ffn = n_mp * mine, one.shape[2] + two.shape[2]
    own = mixed.shape[0]

    def f32(*shape):
        return jax.ShapeDtypeStruct(shape, F32)

    row = f32(1, shard)
    return pl.pallas_call(
        functools.partial(result_kernel, n_mp),
        out_shape=(
            jax.ShapeDtypeStruct((own, width), BF16), f32(own, width), row, *(f32(shard, width),) * 3, f32(1, shard // 2), row,
            f32(shard, width), row, f32(shard, ffn), f32(shard, ffn), f32(ffn, shard),
        ),
        in_specs=[ANY] * 5 + [VMEM],
        out_specs=(ANY, ANY, VMEM, ANY, ANY, ANY, VMEM, VMEM, ANY, VMEM, ANY, ANY, ANY),
        scratch_shapes=[
            pltpu.VMEM((4, n_mp, shard, mine), BF16),
            pltpu.VMEM((4, shard, width), F32),
            pltpu.VMEM((3, shard, ffn), F32),
            pltpu.VMEM((ffn, shard), F32),
            pltpu.VMEM((own, width), BF16),
            pltpu.VMEM((own, width), F32),
            pltpu.SemaphoreType.DMA((12,)),
            pltpu.SemaphoreType.DMA((9,)),
        ],
        compiler_params=pltpu.CompilerParams(vmem_limit_bytes=VMEM_LIMIT),
        name="results",
    )(gmix, one, two, mixed, gtok, small)


def per_device(n_dp, n_mp, tokens, segment_ids, cotangent, gain_in, w_in, w_forget, w_outgate, bound_logit, gain_mix,
               w_mix, gain_ffn, w_gate, w_up, w_down):
    m, d = lax.axis_index("mp"), lax.axis_index("dp")
    rows, width = tokens.shape
    half = bound_logit.shape[0]
    ch = half // n_mp
    mine = 2 * ch
    own = rows // n_mp
    ffn = w_gate.shape[1]
    padded = -(-ffn // LANE) * LANE
    cut = padded // 2 // LANE * LANE
    if padded != ffn:
        fill = ((0, 0), (0, padded - ffn))
        w_gate, w_up, w_down = jnp.pad(w_gate, fill), jnp.pad(w_up, fill), jnp.pad(w_down, fill[::-1])

    normed, r_in, pin, pf, pg, st, phasor, r_mix, mixer_out, ffn_in, middle, r_mid, wm, w_cat, w_one, d_one, grad_out = mixer_forward(
        n_dp, n_mp, 2, cut, w_in, w_forget, w_outgate, w_mix, w_gate, w_up, w_down, cotangent, tokens, segment_ids,
        bound_logit[None], gain_mix[None], gain_in[None], gain_ffn[None],
    )
    grad_out = grad_out.reshape(rows, width)

    g_one, gffn, down, w_two, d_two, b_two, q_two = ffn_first(
        n_dp, n_mp, 3, ffn_in, grad_out, w_one, d_one, w_gate, w_up, w_down
    )
    tok_own = tokens.reshape(n_mp, own, width)
    g_two, base, parting, gmid, gain_ffn_part, gm, gb, rowdot = ffn_last(
        n_dp, n_mp, 4, ffn_in, grad_out, w_two, d_two, b_two, q_two, gffn, down, middle, r_mid, cotangent, tok_own,
        gain_ffn[None], wm,
    )
    g_mixer, grad_tokens, small, mixed = project_back(
        n_dp, n_mp, 5, normed, mixer_out, gm.reshape(rows, 2 * ch), gb.reshape(rows, 2 * ch), pin, pf, pg, st, phasor, r_mix, rowdot,
        bound_logit[None], gain_mix[None], w_cat, gmid, tok_own, r_in, gain_in[None], gain_ffn_part, base, parting,
    )

    out = results(n_dp, n_mp, g_mixer, g_one, g_two, mixed, grad_tokens, small)
    out = [v[0] if v.shape[0] == 1 else v for v in out]
    if padded != ffn:
        out[10:] = [out[10][:, :ffn], out[11][:, :ffn], out[12][:ffn]]
    return tuple(out)


def solution(mesh):
    both, split = P(("dp", "mp"), None), P("dp", "mp")
    row, vec = P("dp", None), P("dp")
    return jax.shard_map(
        functools.partial(per_device, mesh.shape["dp"], mesh.shape["mp"]),
        mesh=mesh,
        in_specs=(row, row, both, P(), row, row, row, P(), P(), row, P(), split, split, P("mp", "dp")),
        out_specs=(both, both, vec, row, row, row, vec, vec, row, vec, split, split, P("mp", "dp")),
        check_vma=False,
    )
```

```python
import functools

import jax
import jax.numpy as jnp
from jax import lax
from jax.experimental import pallas as pl
from jax.experimental.pallas import tpu as pltpu
from jax.sharding import PartitionSpec as P

EPS = 1e-06
F32, BF16 = jnp.float32, jnp.bfloat16
LANE = 128
CHUNKS = 8


def dot(left, right):
    return jnp.dot(left, right, preferred_element_type=F32)


def dot_trans(left, right):
    return lax.dot_general(left, right, (((1,), (1,)), ((), ())), preferred_element_type=F32)


def dot_rows(left, right):
    return lax.dot_general(left, right, (((0,), (0,)), ((), ())), preferred_element_type=F32)


def sigmoid(v):
    return 1.0 / (1.0 + jnp.exp(-v))


def scan_forward(pin, pf, starts, bl, st, phasor, rowsq, a_re, a_im, b_re, b_im):
    rows, half = pin.shape[0], pin.shape[1] // 2
    span = rows // CHUNKS
    lanes = half // LANE
    low = sigmoid(bl[...])
    step = 48

    def prepare(i, _):
        at = pl.ds(pl.multiple_of(i * step, 8), step)
        forget = low + (1.0 - low) * sigmoid(pf[at, :half])
        phase = pf[at, half:]
        keep = 1.0 - starts[at, :]
        cos, sin = jnp.cos(phase) * keep, jnp.sin(phase) * keep
        phasor[at, :half] = cos
        phasor[at, half:] = sin
        x_re, x_im = pin[at, :half], pin[at, half:]
        inflow = 1.0 - forget
        in_re, in_im = x_re * sigmoid(x_re) * inflow, x_im * sigmoid(x_im) * inflow
        d_re, d_im = forget * cos, forget * sin
        for j in range(lanes):
            cut = slice(j * LANE, (j + 1) * LANE)
            a_re[j, at, :] = d_re[:, cut]
            a_im[j, at, :] = d_im[:, cut]
            b_re[j, at, :] = in_re[:, cut]
            b_im[j, at, :] = in_im[:, cut]
        return 0

    lax.fori_loop(0, rows // step, prepare, 0)
    zero, one = jnp.zeros((CHUNKS, LANE), F32), jnp.ones((CHUNKS, LANE), F32)

    def local(s, carry):
        at = pl.ds(s, CHUNKS, stride=span)
        out = []
        for j in range(lanes):
            p_re, p_im, s_re, s_im = carry[4 * j : 4 * j + 4]
            d_re, d_im = a_re.at[j][at, :], a_im.at[j][at, :]
            i_re, i_im = b_re.at[j][at, :], b_im.at[j][at, :]
            p_re, p_im = d_re * p_re - d_im * p_im, d_re * p_im + d_im * p_re
            s_re, s_im = d_re * s_re - d_im * s_im + i_re, d_re * s_im + d_im * s_re + i_im
            a_re.at[j][at, :] = p_re
            a_im.at[j][at, :] = p_im
            b_re.at[j][at, :] = s_re
            b_im.at[j][at, :] = s_im
            out += [p_re, p_im, s_re, s_im]
        return tuple(out)

    last = lax.fori_loop(0, span, local, (one, zero, zero, zero) * lanes, unroll=2)
    carries = []
    for j in range(lanes):
        p_re, p_im, s_re, s_im = last[4 * j : 4 * j + 4]
        c_re = c_im = jnp.zeros((1, LANE), F32)
        held = []
        for k in range(CHUNKS):
            held.append((c_re, c_im))
            q_re, q_im = p_re[k : k + 1], p_im[k : k + 1]
            c_re, c_im = (
                q_re * c_re - q_im * c_im + s_re[k : k + 1],
                q_re * c_im + q_im * c_re + s_im[k : k + 1],
            )
        carries.append(held)
    fix = 40
    for k in range(CHUNKS):

        def finish(i, _):
            at = pl.ds(pl.multiple_of(k * span + i * fix, 8), fix)
            total = jnp.zeros((fix, LANE), F32)
            for j in range(lanes):
                c_re, c_im = carries[j][k]
                p_re, p_im = a_re[j, at, :], a_im[j, at, :]
                s_re = b_re[j, at, :] + p_re * c_re - p_im * c_im
                s_im = b_im[j, at, :] + p_re * c_im + p_im * c_re
                st[at, j * LANE : (j + 1) * LANE] = s_re
                st[at, half + j * LANE : half + (j + 1) * LANE] = s_im
                total = total + s_re * s_re + s_im * s_im
            rowsq[at, :] = jnp.sum(total, axis=1, keepdims=True)
            return 0

        lax.fori_loop(0, span // fix, finish, 0)


def scan_backward(
    gm, pin, pf, pg, st, phasor, r, rowdot, bl, gain, gin, gf, gg, dgain, dbound, a_re, a_im, b_re, b_im, between=(),
):
    rows, half = pin.shape[0], pin.shape[1] // 2
    width = 2 * half
    span = rows // CHUNKS
    lanes = half // LANE
    low = sigmoid(bl[...])
    step = 48

    def prepare(i, total):
        at = pl.ds(pl.multiple_of(i * step, 16), step)
        g, gate = gm[at, :].astype(F32), pg[at, :]
        sig = sigmoid(gate)
        silu = gate * sig
        n = st[at, :] * r[at, :]
        gs = g * silu
        gg[at, :] = (g * n * gain[...] * (sig * (1.0 + gate * (1.0 - sig)))).astype(gg.dtype)
        total = total + jnp.sum((gs * n).reshape(step // 8, 8, width), axis=0)
        d_st = r[at, :] * (gs * gain[...] - n * rowdot[at, :])
        forget = low + (1.0 - low) * sigmoid(pf[at, :half])
        d_re, d_im = forget * phasor[at, :half], forget * phasor[at, half:]
        for j in range(lanes):
            a_re[j, at, :] = d_re[:, j * LANE : (j + 1) * LANE]
            a_im[j, at, :] = d_im[:, j * LANE : (j + 1) * LANE]
            b_re[j, at, :] = d_st[:, j * LANE : (j + 1) * LANE]
            b_im[j, at, :] = d_st[:, half + j * LANE : half + (j + 1) * LANE]
        return total

    total = lax.fori_loop(0, rows // step, prepare, jnp.zeros((8, width), F32))
    dgain[...] = jnp.sum(total, axis=0, keepdims=True)
    for task in between[:1]:
        task()
    zero, one = jnp.zeros((CHUNKS, LANE), F32), jnp.ones((CHUNKS, LANE), F32)

    def local(i, carry):
        at = pl.ds(span - 1 - i, CHUNKS, stride=span)
        out = []
        for j in range(lanes):
            p_re, p_im, s_re, s_im = carry[4 * j : 4 * j + 4]
            d_re, d_im = a_re.at[j][at, :], a_im.at[j][at, :]
            s_re, s_im = s_re + b_re.at[j][at, :], s_im + b_im.at[j][at, :]
            a_re.at[j][at, :] = p_re
            a_im.at[j][at, :] = p_im
            b_re.at[j][at, :] = s_re
            b_im.at[j][at, :] = s_im
            p_re, p_im = d_re * p_re + d_im * p_im, d_re * p_im - d_im * p_re
            s_re, s_im = d_re * s_re + d_im * s_im, d_re * s_im - d_im * s_re
            out += [p_re, p_im, s_re, s_im]
        return tuple(out)

    last = lax.fori_loop(0, span, local, (one, zero, zero, zero) * lanes, unroll=2)
    for task in between[1:]:
        task()
    carries = []
    for j in range(lanes):
        p_re, p_im, s_re, s_im = last[4 * j : 4 * j + 4]
        c_re = c_im = jnp.zeros((1, LANE), F32)
        held = [None] * CHUNKS
        for k in reversed(range(CHUNKS)):
            held[k] = (c_re, c_im)
            q_re, q_im = p_re[k : k + 1], p_im[k : k + 1]
            c_re, c_im = (
                q_re * c_re - q_im * c_im + s_re[k : k + 1],
                q_re * c_im + q_im * c_re + s_im[k : k + 1],
            )
        carries.append(held)
    fix = 40
    for k in range(CHUNKS):

        def carry_in(i, _):
            at = pl.ds(pl.multiple_of(k * span + i * fix, 8), fix)
            for j in range(lanes):
                c_re, c_im = carries[j][k]
                p_re, p_im = a_re[j, at, :], a_im[j, at, :]
                b_re[j, at, :] += p_re * c_re - p_im * c_im
                b_im[j, at, :] += p_re * c_im + p_im * c_re
            return 0

        lax.fori_loop(0, span // fix, carry_in, 0)

    def finish(i, carry):
        before, total = carry
        at = pl.ds(pl.multiple_of(i * step, 16), step)
        g_re = jnp.concatenate([b_re[j, at, :] for j in range(lanes)], axis=1)
        g_im = jnp.concatenate([b_im[j, at, :] for j in range(lanes)], axis=1)
        now = st[at, :]
        prev = jnp.concatenate([before, now[:-1]], axis=0)
        q_re, q_im = prev[:, :half], prev[:, half:]
        dd_re, dd_im = g_re * q_re + g_im * q_im, g_im * q_re - g_re * q_im
        mag = sigmoid(pf[at, :half])
        forget = low + (1.0 - low) * mag
        cos, sin = phasor[at, :half], phasor[at, half:]
        x_re, x_im = pin[at, :half], pin[at, half:]
        sig_re, sig_im = sigmoid(x_re), sigmoid(x_im)
        inflow = 1.0 - forget
        d_forget = dd_re * cos + dd_im * sin - g_re * x_re * sig_re - g_im * x_im * sig_im
        gf[at, :half] = (d_forget * (1.0 - low) * mag * (1.0 - mag)).astype(gf.dtype)
        gf[at, half:] = (forget * (dd_im * cos - dd_re * sin)).astype(gf.dtype)
        gin[at, :half] = (g_re * inflow * sig_re * (1.0 + x_re * (1.0 - sig_re))).astype(gin.dtype)
        gin[at, half:] = (g_im * inflow * sig_im * (1.0 + x_im * (1.0 - sig_im))).astype(gin.dtype)
        total = total + jnp.sum((d_forget * (1.0 - mag)).reshape(step // 8, 8, half), axis=0)
        return now[step - 1 :], total

    first = (jnp.zeros((1, width), F32), jnp.zeros((8, half), F32))
    total = lax.fori_loop(0, rows // step, finish, first)[1]
    dbound[...] = jnp.sum(total, axis=0, keepdims=True) * low * (1.0 - low)


def call_local(body, outs, scratch, *args, name):
    return pl.pallas_call(
        body,
        out_shape=outs,
        scratch_shapes=scratch,
        compiler_params=pltpu.CompilerParams(vmem_limit_bytes=48 * 2**20),
        name=name,
    )(*args)


MESH_ID = pl.DeviceIdType.MESH
VMEM_LIMIT = 62 * 2**20
ANY = pl.BlockSpec(memory_space=pl.ANY)
VMEM = pl.BlockSpec(memory_space=pltpu.VMEM)


def remote(src, dst, send, recv, device):
    return pltpu.make_async_remote_copy(
        src_ref=src, dst_ref=dst, send_sem=send, recv_sem=recv, device_id=device, device_id_type=MESH_ID
    )


def load(src, dst, sem):
    copy = pltpu.make_async_copy(src, dst, sem)
    copy.start()
    return copy


def bounds(total, parts, unit):
    ends = [i * (total // unit) // parts * unit for i in range(parts)] + [total]
    return [(ends[i], ends[i + 1] - ends[i]) for i in range(parts)]


def subsets(masks):
    out = [0]
    for mask in masks:
        out += [sub | mask for sub in out]
    return out


class Place:
    def __init__(self, n_dp, n_mp):
        self.n_dp, self.n_mp = n_dp, n_mp
        self.d, self.m = lax.axis_index("dp"), lax.axis_index("mp")
        self.chips, self.bits = n_dp // 2, n_mp.bit_length() - 1
        self.k, self.c = lax.div(self.d, 2), lax.rem(self.d, 2)

    def twin(self):
        return (2 * self.k + 1 - self.c, self.m)

    def chip(self, step):
        return (self.d + 2 * step, self.m)

    def peer(self, mask):
        return (self.d, self.m ^ mask)

    def along(self, s):
        return (2 * lax.rem(self.k + s, self.chips) + self.c, self.m)

    def barrier(self, line=True, twin=True, far=False):
        sem = pltpu.get_barrier_semaphore()

        def greet(device):
            pl.semaphore_signal(sem, inc=1, device_id=device, device_id_type=MESH_ID)

        for mask in range(1, self.n_mp):
            greet(self.peer(mask))
        count = self.n_mp - 1
        if twin:
            greet(self.twin())
            count += 1
        if far:
            for s in range(1, self.chips):
                greet(self.along(s))
            count += self.chips - 1
        elif line:

            @pl.when(self.k > 0)
            def _():
                greet(self.chip(-1))

            @pl.when(self.k < self.chips - 1)
            def _():
                greet(self.chip(1))

            count += jnp.where(self.k > 0, 1, 0) + jnp.where(self.k < self.chips - 1, 1, 0)
        pl.semaphore_wait(sem, count)


class RowSum:
    @staticmethod
    def scratch(n_dp, blocks, rows, width):
        chips = n_dp // 2
        return [
            pltpu.VMEM((2, 2, rows, width), BF16),
            pltpu.VMEM((blocks, chips, rows, width), BF16),
            pltpu.VMEM((blocks, chips + 1, rows, width), BF16),
            pltpu.VMEM((rows, width), F32),
            pltpu.SemaphoreType.DMA((4, blocks, chips + 1)),
        ]

    def __init__(self, place, refs, piece, finish, skew):
        self.p = place
        self.out, self.summed, self.inbox, self.acc, self.sem = refs
        self.piece, self.finish = piece, finish
        self.blocks, self.skew = self.summed.shape[0], skew
        chips = place.chips
        self.steps = chips - 1 + (self.blocks + chips - 2) * chips if skew else self.blocks * chips

    def order(self, i):
        chips = self.p.chips
        ok = (i >= 0) & (i < self.steps)
        i = jnp.clip(i, 0, self.steps - 1)
        if self.skew:
            early = i < chips - 1
            j = jnp.maximum(i - (chips - 1), 0)
            t = jnp.where(early, i, lax.rem(j, chips))
            b = jnp.where(early, 0, 1 + lax.div(j, chips) - t)
            ok = ok & (early | ((b >= 0) & (b < self.blocks) & ((b > 0) | (t == chips - 1))))
            return t, jnp.clip(b, 0, self.blocks - 1), ok
        return lax.div(i, self.blocks), lax.rem(i, self.blocks), ok

    def targets(self, i):
        p = self.p
        t, b, ok = self.order(i)
        up, down = p.chips - 1 - t + p.k, p.k - (p.chips - 1) + t
        return b, up, ok & (up <= p.chips - 1), down, ok & (down >= 0) & (t < p.chips - 1), t == p.chips - 1

    def swap(self, b, e, ring):
        return remote(
            self.out.at[ring[0], ring[1]], self.summed.at[b, e], self.sem.at[0, b, e], self.sem.at[1, b, e],
            self.p.twin(),
        )

    def move(self, b, e, up):
        slot = e + 1 if up else e
        return remote(
            self.summed.at[b, e], self.inbox.at[b, slot], self.sem.at[2, b, e], self.sem.at[3, b, slot],
            self.p.chip(1 if up else -1),
        )

    def given(self, i):
        b, up, up_ok, down, down_ok, _ = self.targets(i)
        for side, e, ok in ((0, up, up_ok), (1, down, down_ok)):

            @pl.when(ok)
            def _():
                self.swap(b, e, (lax.rem(i + 2, 2), side)).wait_send()

    def give(self, i):
        self.given(i - 2)
        b, up, up_ok, down, down_ok, _ = self.targets(i)
        for side, e, ok in ((0, up, up_ok), (1, down, down_ok)):

            @pl.when(ok)
            def _():
                ring = (lax.rem(i, 2), side)
                self.out[ring[0], side] = self.piece(b, 2 * e + 1 - self.p.c).astype(BF16)
                self.swap(b, e, ring).start()

    def take(self, b, slot, up):
        e = slot - 1 if up else slot
        self.move(b, e, up).wait_recv()
        self.acc[...] += self.inbox[b, slot].astype(F32)

    def send(self, b, e, up):
        self.summed[b, e] = self.acc[...].astype(BF16)
        self.move(b, e, up).start()

    def work(self, i):
        p = self.p
        b, up, up_ok, down, down_ok, last = self.targets(i)

        def begin(e):
            own = self.piece(b, 2 * e + p.c)
            self.swap(b, e, (0, 0)).wait_recv()
            self.acc[...] = own + self.summed[b, e].astype(F32)

        @pl.when(up_ok)
        def _():
            begin(up)

            @pl.when(p.k > 0)
            def _():
                self.take(b, up + 1, True)

            @pl.when(jnp.logical_not(last))
            def _():
                self.send(b, up, True)

            @pl.when(last)
            def _():
                @pl.when(p.k < p.chips - 1)
                def _():
                    self.take(b, up, False)

                self.finish(b, self.acc)

        @pl.when(down_ok)
        def _():
            begin(down)

            @pl.when(p.k < p.chips - 1)
            def _():
                self.take(b, down, False)

            self.send(b, down, False)

    def run(self, lo, hi, fresh=False, ahead=True):
        if lo == 0 or fresh:
            self.give(lo)

        def body(i, _):
            if ahead:
                self.give(i + 1)
            else:

                @pl.when(i + 1 < hi)
                def _():
                    self.give(i + 1)

            self.work(i)
            return 0

        lax.fori_loop(lo, hi, body, 0)
        if hi == self.steps:
            self.given(hi - 1)

    def drain(self):
        p = self.p

        def body(e, _):
            for b in range(self.blocks):

                @pl.when(e > p.k)
                def _():
                    self.move(b, e, True).wait_send()

                @pl.when(e < p.k)
                def _():
                    self.move(b, e, False).wait_send()

            return 0

        lax.fori_loop(0, p.chips, body, 0)


class CubeSum:
    @staticmethod
    def scratch(n_mp, rows, width, whole=True):
        bits = n_mp.bit_length() - 1
        most = max(size for _, size in bounds(width, bits, LANE))
        slots = n_mp - 1 if whole else n_mp - 2
        return [
            *[pltpu.VMEM((bits, slots, rows, most), BF16)] * 2,
            pltpu.SemaphoreType.DMA((2, bits, slots)),
        ]

    def __init__(self, place, refs, partial, width):
        self.p = place
        self.out, self.inbox, self.sem = refs
        self.partial = partial
        bits = place.bits
        self.cols = bounds(width, bits, LANE)
        self.slots, self.masks = {}, {}
        for part in range(bits):
            used = 0
            for s in range(bits):
                subs = subsets([1 << ((part + r) % bits) for r in range(s + 1, bits)])
                self.masks[part, s] = (1 << ((part + s) % bits), subs)
                for sub in subs:
                    self.slots[part, s, sub] = used
                    used += 1

    def copy(self, part, s, sub):
        slot, size = self.slots[part, s, sub], self.cols[part][1]
        return remote(
            self.out.at[part, slot, :, :size], self.inbox.at[part, slot, :, :size],
            self.sem.at[0, part, slot], self.sem.at[1, part, slot],
            self.p.peer(self.masks[part, s][0]),
        )

    def pieces(self, part, mask, stages):
        for r in stages:
            self.copy(part, r, mask).wait_recv()
        base, total = self.cols[part]
        for lo in range(0, total, 4 * LANE):
            size = min(4 * LANE, total - lo)
            value = self.partial(self.p.m ^ mask, base + lo, size)
            for r in stages:
                value = value + self.inbox[part, self.slots[part, r, mask], :, lo : lo + size].astype(F32)
            yield lo, size, value

    def stage(self, s, only=None):
        for part in range(self.p.bits):
            bit, subs = self.masks[part, s]
            for sub in subs:
                if only not in (None, bit | sub):
                    continue
                for lo, size, value in self.pieces(part, bit | sub, range(s)):
                    self.out[part, self.slots[part, s, sub], :, lo : lo + size] = value.astype(BF16)
                self.copy(part, s, sub).start()

    def results(self, stages=None):
        for part in range(self.p.bits):
            base = self.cols[part][0]
            for lo, size, value in self.pieces(part, 0, range(self.p.bits if stages is None else stages)):
                yield slice(base + lo, base + lo + size), value

    def parting(self):
        s = self.p.bits - 1
        for part in range(self.p.bits):
            for lo, size, value in self.pieces(part, self.masks[part, s][0], range(s)):
                yield part, slice(lo, lo + size), value

    def drain(self, stages=None):
        for part, s, sub in self.slots:
            if stages is None or s < stages:
                self.copy(part, s, sub).wait_send()


class CubeGather:
    @staticmethod
    def scratch(n_mp):
        bits = n_mp.bit_length() - 1
        return [pltpu.SemaphoreType.DMA((bits, n_mp)), pltpu.SemaphoreType.DMA((bits, n_mp))]

    def __init__(self, place, refs, view):
        self.p, self.view = place, view
        self.send, self.recv = refs
        bits = place.bits
        self.sends = {}
        for part in range(bits):
            for s in range(bits):
                earlier = [1 << ((part + r) % bits) for r in range(s)]
                for sub in subsets(earlier):
                    self.sends[part, s, sub] = (1 << ((part + s) % bits), sub)

    def copy(self, part, bit, sub):
        p = self.p
        ref = self.view(p.m ^ sub, part)
        return remote(ref, ref, self.send.at[part, bit | sub], self.recv.at[part, p.m ^ sub], p.peer(bit))

    def arrived(self, part, sub):
        p = self.p
        ref = self.view(p.m ^ sub, part)
        remote(ref, ref, self.send.at[part, sub], self.recv.at[part, p.m ^ sub], p.peer(sub)).wait_recv()

    def stage(self, s):
        for (part, at, sub), (bit, _) in self.sends.items():
            if at == s:
                if sub:
                    self.arrived(part, sub)
                self.copy(part, bit, sub).start()

    def last(self):
        p = self.p
        for part in range(p.bits):
            final = 1 << ((part + p.bits - 1) % p.bits)
            for sub in range(1, p.n_mp):
                if sub & final:
                    self.arrived(part, sub)

    def drain(self):
        for (part, _, sub), (bit, _) in self.sends.items():
            self.copy(part, bit, sub).wait_send()


class SmallSum:
    @staticmethod
    def scratch(n_dp, n_mp, shape):
        slots = 3 + n_mp + n_dp // 2
        return [pltpu.VMEM((slots, *shape), F32), pltpu.SemaphoreType.DMA((2, slots))]

    def __init__(self, place, refs):
        self.p = place
        self.buf, self.sem = refs

    def start(self, src, dst, device):
        remote(self.buf.at[src], self.buf.at[dst], self.sem.at[0, dst], self.sem.at[1, dst], device).start()

    def wait(self, dst):
        copy = remote(self.buf.at[dst], self.buf.at[dst], self.sem.at[0, dst], self.sem.at[1, dst], self.p.twin())
        copy.wait_recv()

    def sent(self, dst):
        copy = remote(self.buf.at[dst], self.buf.at[dst], self.sem.at[0, dst], self.sem.at[1, dst], self.p.twin())
        copy.wait_send()

    def twins(self):
        self.start(0, 1, self.p.twin())

    def cube(self):
        p = self.p
        self.wait(1)
        self.buf[2] = self.buf[0] + self.buf[1]
        for mask in range(1, p.n_mp):
            self.start(2, 3 + mask, p.peer(mask))

    def line(self):
        p = self.p
        for mask in range(1, p.n_mp):
            self.wait(3 + mask)
        total = 0.0
        for q in range(p.n_mp):
            mask = p.m ^ q
            total = total + self.buf[jnp.where(mask == 0, 2, 3 + mask)]
        self.buf[3] = total
        for s in range(1, p.chips):
            self.start(3, 3 + p.n_mp + s, p.along(s))

    def result(self):
        p = self.p
        total = self.buf[3]
        for s in range(1, p.chips):
            self.wait(3 + p.n_mp + s)
            total = total + self.buf[3 + p.n_mp + s]
        for dst in [1, *range(4, 3 + p.n_mp), *range(4 + p.n_mp, 3 + p.n_mp + p.chips)]:
            self.sent(dst)
        return total


class RowGather:
    @staticmethod
    def scratch(n_dp, units):
        return [pltpu.SemaphoreType.DMA((5, units, n_dp // 2))]

    def __init__(self, place, refs, src, dst):
        self.p, self.src, self.dst = place, src, dst
        (self.sem,) = refs

    def hop(self, u, e, side, own=False):
        p = self.p
        here = self.dst(u, e, p.c)
        device = (p.chip(1), p.chip(-1), p.twin())[side]
        recv = self.sem.at[4 if side == 2 else 3, u, e]
        return remote(self.src(u) if own else here, here, self.sem.at[side, u, e], recv, device)

    def start(self, u):
        p = self.p

        @pl.when(p.k < p.chips - 1)
        def _():
            self.hop(u, p.k, 0, True).start()

        @pl.when(p.k > 0)
        def _():
            self.hop(u, p.k, 1, True).start()

        self.hop(u, p.k, 2, True).start()

    def forward(self, u, s):
        p = self.p

        @pl.when(p.k - s >= 0)
        def _():
            self.hop(u, p.k - s, 0).wait_recv()

            @pl.when(p.k < p.chips - 1)
            def _():
                self.hop(u, p.k - s, 0).start()

            self.hop(u, p.k - s, 2).start()

        @pl.when(p.k + s < p.chips)
        def _():
            self.hop(u, p.k + s, 1).wait_recv()

            @pl.when(p.k > 0)
            def _():
                self.hop(u, p.k + s, 1).start()

            self.hop(u, p.k + s, 2).start()

    def finish(self, u):
        p = self.p
        for e in range(p.chips):
            there = self.dst(u, e, 1 - p.c)
            remote(there, there, self.sem.at[2, u, e], self.sem.at[4, u, e], p.twin()).wait_recv()

    def drain(self, u):
        p = self.p
        for e in range(p.chips):

            @pl.when((e <= p.k) & (p.k < p.chips - 1))
            def _():
                self.hop(u, e, 0).wait_send()

            @pl.when((e >= p.k) & (p.k > 0))
            def _():
                self.hop(u, e, 1).wait_send()

            self.hop(u, e, 2).wait_send()


def mixer_kernel(
    n_dp, n_mp, w_in, w_forget, w_outgate, w_mix, w_gate, w_up, w_down, cot, tokens, ident, bound, gain_mix, gain_in, gain_ffn,
    normed_o, rin_o, pin_o, pf_o, pg_o, st_o, phasor_o, r_o, mix_o, ffn_o, mid_o, rmid_o, wm_o, wcat_o, one_o, one_d, cot_o,
    x, wv, wq, pin, pf, pg, st, phasor, rowsq, rin, starts, bl, gain, a_re, a_im, b_re, b_im, mix, wm, tok, ffn_v, mid_v, cot_v, rs_out, rs_in,
    lsem, osem, rs_sem, wtwin, *gsems,
):
    p = Place(n_dp, n_mp)
    rows, width = tokens.shape
    mine = pin.shape[1]
    half, ch = width // 2, mine // 2
    own = rows // n_mp
    hw = width // 2
    shard, h = w_in.shape[0], one_o.shape[2]
    row_parts = bounds(hw, p.bits, 16)

    def mix_view(q, part):
        lo, size = row_parts[part]
        return wm.at[pl.ds(pl.multiple_of(p.c * hw + lo, 16), size), pl.ds(pl.multiple_of(q * mine, LANE), mine)]

    def rows_at(e, c):
        return pl.ds(pl.multiple_of((2 * e + c) * shard, 16), shard)

    def lanes_at(at, size):
        return pl.ds(pl.multiple_of(at, LANE), size)

    def unit_src(u):
        if u < 4:
            return unit_dst(u, p.k, p.c)
        return (w_gate.at[:, :h], w_up.at[:, :h], w_down.at[:h])[u - 4]

    def unit_dst(u, e, c):
        if u == 6:
            return one_d.at[:, lanes_at((2 * e + c) * shard, shard)]
        return (wv.at[u] if u < 3 else wq if u == 3 else one_o.at[u - 4]).at[rows_at(e, c)]

    mine_at = rows_at(p.k, p.c)
    keep = {3: [load(w_mix.at[:, lanes_at(p.m * mine, mine)], wq.at[mine_at], lsem.at[1])]}
    for u, w in enumerate((w_in, w_forget, w_outgate)):
        keep[u] = [
            load(w.at[:, lanes_at(side * half + p.m * ch, ch)], wv.at[u, mine_at, side * ch : (side + 1) * ch], lsem.at[2 + 2 * u + side])
            for side in range(2)
        ]
    tok_load = load(tokens, tok, lsem.at[0])
    vectors = [
        load(bound.at[:, lanes_at(p.m * ch, ch)], bl, lsem.at[10]),
        *[
            load(gain_mix.at[:, lanes_at(side * half + p.m * ch, ch)], gain.at[:, side * ch : (side + 1) * ch], lsem.at[11 + side])
            for side in range(2)
        ],
    ]
    first_own = [load(unit_src(u), unit_dst(u, p.k, p.c), lsem.at[9 + u]) for u in range(4, 7)]
    cot_own = load(cot, cot_v.at[p.m], lsem.at[8])
    p.barrier()
    z = RowGather(p, gsems[:1], unit_src, unit_dst)
    gsems = gsems[1:]
    order = (3, 0, 1, 2)

    def start(u):
        for copy in keep[u]:
            copy.wait()
        z.start(u)

    start(3)
    start(0)
    cot_parts = bounds(width, p.bits, LANE)

    def cot_view(q, part):
        lo, size = cot_parts[part]
        return cot_v.at[q, :, lo : lo + size]

    cot_own.wait()
    gc = CubeGather(p, gsems[18:20], cot_view)
    gc.stage(0)
    tok_load.wait()
    fine = 48

    def norm_in(i, _):
        at = pl.ds(pl.multiple_of(i * fine, 16), fine)
        v = tok[at, :].astype(F32)
        r = lax.rsqrt(jnp.mean(v * v, axis=-1, keepdims=True) + EPS)
        rin[at, :] = r
        x[at, :] = (v * r * gain_in[...]).astype(BF16)
        return 0

    lax.fori_loop(0, rows // fine, norm_in, 0)
    eighth = jnp.full((8, LANE), 0.125, F32)
    ids = lax.dot_general(
        jnp.broadcast_to(ident[...].astype(F32), (8, rows)), eighth, (((0,), (0,)), ((), ())),
        precision=lax.Precision.HIGHEST, preferred_element_type=F32,
    )[:, :1]
    before = jnp.concatenate([ids[:1] - 1.0, ids[:-1]], axis=0)
    starts[...] = jnp.where(jnp.abs(ids - before) > 0.5, 1.0, 0.0)
    for copy in vectors:
        copy.wait()
    outs = [load(x, normed_o, osem.at[0]), load(rin.at[pl.ds(pl.multiple_of(p.m * own, 8), own)], rin_o, osem.at[1])]
    gw = CubeGather(p, gsems[0:2], mix_view)

    def to_twin(part, sub):
        ref = mix_view(p.m ^ sub, part)
        return remote(ref, ref, wtwin.at[0, part, sub], wtwin.at[1, part, sub], p.twin())

    def from_twin(part, sub):
        lo, size = row_parts[part]
        ref = wm.at[
            pl.ds(pl.multiple_of((1 - p.c) * hw + lo, 16), size),
            pl.ds(pl.multiple_of((p.m ^ sub) * mine, LANE), mine),
        ]
        return remote(ref, ref, wtwin.at[0, part, sub], wtwin.at[1, part, sub], p.twin())

    step = 240

    def project(u, out):
        z.forward(u, p.chips - 1)
        z.finish(u)

        def body(i, _):
            at = pl.ds(pl.multiple_of(i * step, 16), step)
            out[at, :] = dot(x[at, :], wv[u])
            return 0

        lax.fori_loop(0, rows // step, body, 0)

    core_rows = pl.ds(pl.multiple_of(p.c * hw, 16), hw)
    for tau in range(1, p.chips + 2):
        for i, u in enumerate(order):
            if 1 <= tau - i <= p.chips - 2:
                z.forward(u, tau - i)
        if tau + 1 < len(order):
            start(order[tau + 1])
        if tau == p.chips - 1:
            for s in range(1, p.bits):
                gc.stage(s)
            z.forward(3, p.chips - 1)
            z.finish(3)
            own_mix = load(wq.at[core_rows], wm.at[core_rows, lanes_at(p.m * mine, mine)], lsem.at[9])
            own_mix.wait()
            gw.stage(0)
            for part in range(p.bits):
                to_twin(part, 0).start()
        if tau == p.chips:
            project(0, pin)
    for u in range(4, 7):
        z.start(u)
    project(1, pf)
    for s in range(1, p.bits):
        gw.stage(s)
    scan_forward(pin, pf, starts, bl, st, phasor, rowsq, a_re, a_im, b_re, b_im)
    outs += [
        load(src, dst, osem.at[5 + i])
        for i, (src, dst) in enumerate(((pin, pin_o), (pf, pf_o), (pg, pg_o), (st, st_o), (phasor, phasor_o)))
        if i != 2
    ]
    ones = jnp.ones((8, mine), F32)
    rs_out[...] = lax.dot_general(
        ones, st[...] * st[...], (((1,), (1,)), ((), ())), precision=lax.Precision.HIGHEST, preferred_element_type=F32
    )

    def rs_copy(mask):
        return remote(rs_out, rs_in.at[mask], rs_sem.at[0, mask], rs_sem.at[1, mask], p.peer(mask))

    for mask in range(1, n_mp):
        rs_copy(mask).start()
    project(2, pg)
    outs += [load(wv.at[u], wcat_o.at[u], osem.at[2 + u]) for u in range(3)]
    outs.append(load(pg, pg_o, osem.at[7]))
    gw.last()
    for part in range(p.bits):
        for sub in range(1, n_mp):
            to_twin(part, sub).start()
    z.forward(4, 1)
    total = rs_out[...]
    for mask in range(1, n_mp):
        rs_copy(mask).wait_recv()
        total = total + rs_in[mask]
    inv = lax.rsqrt(total / width + EPS)
    rowsq[...] = lax.dot_general(
        inv, eighth, (((0,), (0,)), ((), ())), precision=lax.Precision.HIGHEST, preferred_element_type=F32
    )[:, :1]
    outs.append(load(rowsq, r_o, osem.at[10]))
    re_at = pl.ds(pl.multiple_of(p.m * ch, LANE), ch)
    im_at = pl.ds(pl.multiple_of(half + p.m * ch, LANE), ch)

    def gate_out(i, _):
        at = pl.ds(pl.multiple_of(i * fine, 16), fine)
        gate = pg[at, :]
        value = (st[at, :] * rowsq[at, :] * gain[...] * (gate * sigmoid(gate))).astype(BF16)
        mix[at, re_at] = value[:, :ch]
        mix[at, im_at] = value[:, ch:]
        return 0

    spans = 4
    span = rows // spans
    gathers = []
    for n in range(spans):
        lax.fori_loop(n * span // fine, (n + 1) * span // fine, gate_out, 0)
        for side in range(2):

            def view(q, part, n=n, side=side):
                lo, size = bounds(span, p.bits, 16)[part]
                return mix.at[n * span + lo : n * span + lo + size, pl.ds(pl.multiple_of(side * half + q * ch, LANE), ch)]

            at = 2 + 2 * (2 * n + side)
            gathers.append(CubeGather(p, gsems[at : at + 2], view))
            gathers[-1].stage(0)
    z.forward(5, 1)
    for s in range(1, p.bits):
        for g in gathers:
            g.stage(s)
    z.forward(6, 1)
    gc.last()
    outs.append(load(cot_v, cot_o, osem.at[21]))
    for part in range(p.bits):
        for sub in range(n_mp):
            from_twin(part, sub).wait_recv()
    outs.append(load(wm, wm_o, osem.at[11]))
    for n in range(spans):
        gathers[2 * n].last()
        gathers[2 * n + 1].last()

        def mix_rows(i, _):
            at = pl.ds(pl.multiple_of(i * step, 16), step)
            middle = tok[at, :].astype(F32) + dot(mix[at, :], wm[...])
            r = lax.rsqrt(jnp.mean(middle * middle, axis=-1, keepdims=True) + EPS)
            ffn_v[at, :] = (middle * r * gain_ffn[...]).astype(BF16)
            for j in range(step // own):

                @pl.when(p.m == i * (step // own) + j)
                def _():
                    mid_v[...] = middle[j * own : (j + 1) * own]
                    rmid_o[...] = r[j * own : (j + 1) * own]

            return 0

        lax.fori_loop(n * span // step, (n + 1) * span // step, mix_rows, 0)
        at = slice(n * span, (n + 1) * span)
        outs.append(load(ffn_v.at[at], ffn_o.at[at], osem.at[12 + 2 * n]))
        outs.append(load(mix.at[at], mix_o.at[at], osem.at[13 + 2 * n]))
        if n < 3:
            z.forward(4 + n, 2)
    outs.append(load(mid_v, mid_o, osem.at[12 + 2 * spans]))
    for s in range(3, p.chips):
        for u in range(4, 7):
            z.forward(u, s)
    for u in range(4, 7):
        z.finish(u)
    for copy in first_own:
        copy.wait()
    for copy in outs:
        copy.wait()
    for u in range(7):
        z.drain(u)
    gw.drain()
    gc.drain()
    for g in gathers:
        g.drain()
    for part in range(p.bits):
        for sub in range(n_mp):
            to_twin(part, sub).wait_send()
    for mask in range(1, n_mp):
        rs_copy(mask).wait_send()


def mixer_forward(n_dp, n_mp, cid, h, *args):
    rows, width = args[8].shape
    mine = width // n_mp
    own, lanes = rows // n_mp, mine // 2 // LANE
    bits = n_mp.bit_length() - 1
    full, part, lane = (rows, width), (rows, mine), (lanes, rows, LANE)

    def f32(*shape):
        return jax.ShapeDtypeStruct(shape, F32)

    def bf16(*shape):
        return jax.ShapeDtypeStruct(shape, BF16)

    return pl.pallas_call(
        functools.partial(mixer_kernel, n_dp, n_mp),
        out_shape=(
            bf16(*full), f32(own, 1), *(f32(*part),) * 5, f32(rows, 1), bf16(*full), bf16(*full), f32(own, width), f32(own, 1),
            bf16(width, width), bf16(3, width, mine), bf16(2, width, h), bf16(h, width), bf16(n_mp, own, width),
        ),
        in_specs=[ANY] * 9 + [VMEM] + [ANY] * 2 + [VMEM] * 2,
        out_specs=(ANY,) * 11 + (VMEM,) + (ANY,) * 5,
        scratch_shapes=[
            pltpu.VMEM(full, BF16),
            pltpu.VMEM((3, width, mine), BF16),
            pltpu.VMEM((width, mine), BF16),
            *[pltpu.VMEM(part, F32)] * 5,
            *[pltpu.VMEM((rows, 1), F32)] * 3,
            pltpu.VMEM((1, mine // 2), F32),
            pltpu.VMEM((1, mine), F32),
            *[pltpu.VMEM(lane, F32)] * 4,
            pltpu.VMEM(full, BF16),
            pltpu.VMEM((width, width), BF16),
            pltpu.VMEM(full, BF16),
            pltpu.VMEM(full, BF16),
            pltpu.VMEM((own, width), F32),
            pltpu.VMEM((n_mp, own, width), BF16),
            pltpu.VMEM((8, rows), F32),
            pltpu.VMEM((n_mp, 8, rows), F32),
            pltpu.SemaphoreType.DMA((17,)),
            pltpu.SemaphoreType.DMA((22,)),
            pltpu.SemaphoreType.DMA((2, n_mp)),
            pltpu.SemaphoreType.DMA((2, bits, n_mp)),
            *RowGather.scratch(n_dp, 7),
            *CubeGather.scratch(n_mp) * 10,
        ],
        compiler_params=pltpu.CompilerParams(collective_id=cid, has_side_effects=True, vmem_limit_bytes=VMEM_LIMIT),
        name="mixer_forward",
    )(*args)


STEP = 240


def ffn_rows(at, own, a, w_gate, w_up, w_down, put):
    gate = dot(a[0, at, :], w_gate)
    up = dot(a[0, at, :], w_up)
    sig = sigmoid(gate)
    silu = gate * sig
    grad = dot_trans(a[1, at, :], w_down)
    put(0, (grad * up * sig * (1.0 + gate * (1.0 - sig))).astype(BF16))
    put(1, (grad * silu).astype(BF16))
    put(2, (silu * up).astype(BF16))


class FfnSums:
    def __init__(self, p, a, wv, wd, h, bv, bq, gsum, gsem, sums, cube_g, cube_d):
        rows, width = a.shape[1:]
        own, shard = rows // p.n_mp, gsum.shape[1]
        def rows_of(b, q):
            return bq[b, q] if own % 16 else bv[b, pl.ds(pl.multiple_of(q * own, 16), own), :]

        def part_g(q, lo, size):
            at = slice(lo, lo + size)
            return dot_trans(rows_of(0, q), wv[0, at, :h]) + dot_trans(rows_of(1, q), wv[1, at, :h])

        def part_d(q, lo, size):
            return dot(rows_of(2, q), wd[:h, lo : lo + size])

        def piece(b, e):
            left = jnp.where(b < 2, 0, 1)
            return dot_rows(a[left, :, pl.ds(pl.multiple_of(e * shard, LANE), shard)], bv[b])

        def finish(b, acc):
            out = pltpu.make_async_copy(acc, gsum.at[b], gsem)
            out.start()
            out.wait()

        self.total = RowSum(p, sums, piece, finish, False)
        self.g_cube, self.d_cube = CubeSum(p, cube_g, part_g, width), CubeSum(p, cube_d, part_d, width)


def first_kernel(
    n_dp, n_mp, ffn_in, grad_out, w, w_d, w_gate, w_up, w_down, gsum, gffn, down, next_w, next_d, next_b, next_q,
    a, wv, wd, wv2, wd2, bv, bq, stage, stage_q, result, lsem, gsem, bsem, *refs,
):
    p = Place(n_dp, n_mp)
    rows, width = ffn_in.shape
    own, h, h_next, shard = rows // n_mp, bv.shape[2], next_d.shape[0], gsum.shape[1]
    sums, cube_g, cube_d, zsem = refs[:5], refs[5:8], refs[8:11], refs[11:12]
    loads = [load(ffn_in, a.at[0], lsem.at[0]), load(w, wv, lsem.at[1]), load(grad_out, a.at[1], lsem.at[2]), load(w_d, wd, lsem.at[3])]
    p.barrier()
    srcs = (w_gate.at[:, h:], w_up.at[:, h:], w_down.at[h:])

    def next_dst(u, e, c):
        at = pl.ds(pl.multiple_of((2 * e + c) * shard, LANE), shard)
        return next_d.at[:, at] if u == 2 else next_w.at[u, at]

    z = RowGather(p, zsem, lambda u: srcs[u], next_dst)
    own_next = [load(srcs[u], next_dst(u, p.k, p.c), lsem.at[5 + u]) for u in range(3)]
    for u in range(3):
        z.start(u)
    for copy in loads:
        copy.wait()

    f = FfnSums(p, a, wv, wd, h, bv, bq, gsum, gsem, sums, cube_g, cube_d)
    total, g_cube, d_cube = f.total, f.g_cube, f.d_cube
    n, chunks = total.blocks, rows // STEP
    for j in (*range(1, chunks), 0):
        i = lax.div(p.m * chunks, n_mp) ^ j
        at = pl.ds(pl.multiple_of(i * STEP, 16), STEP)

        def put(b, value):
            bv[b, at, :] = value
            if own % 16:
                wide = value.astype(F32)
                for q in range(STEP // own):
                    bq[b, i * (STEP // own) + q] = wide[q * own : (q + 1) * own].astype(BF16)

        ffn_rows(at, own, a, wv[0], wv[1], wd[...], put)
        if own == STEP and j:
            g_cube.stage(0, j)
    if own != STEP:
        g_cube.stage(0)
    z.forward(0, 1)
    total.run(0, n)
    z.forward(1, 1)
    d_cube.stage(0)
    z.forward(2, 1)
    for i in range(3):
        total.run(n + i, n + i + 1)
        z.forward(i, 2)
        if i == 1:
            for s in range(1, p.bits):
                g_cube.stage(s)
    last = total.steps - n
    for i in range(2 * n, last):
        total.run(i, i + 1)
        z.forward(i % n, i // n + 1)
    for s in range(1, p.bits):
        d_cube.stage(s)
    for u in range(3):
        z.finish(u)
        own_next[u].wait()
    loads = [load(next_w, wv2, lsem.at[8]), load(next_d, wd2, lsem.at[9])]
    for copy in loads:
        copy.wait()
    sent = []
    for i in range(chunks):
        slot = i % 2
        for copy in sent[i - 2 : i - 1] and sent[i - 2]:
            copy.wait()

        def put(b, value, slot=slot):
            stage[slot, b] = value
            if own % 16:
                wide = value.astype(F32)
                for j in range(STEP // own):
                    stage_q[slot, b, j] = wide[j * own : (j + 1) * own].astype(BF16)

        ffn_rows(
            slice(i * STEP, (i + 1) * STEP), own, a, wv2[0], wv2[1], wd2[...], put
        )
        copies = [load(stage.at[slot], next_b.at[:, i * STEP : (i + 1) * STEP], bsem.at[0, i])]
        if own % 16:
            per = STEP // own
            copies.append(load(stage_q.at[slot], next_q.at[:, i * per : (i + 1) * per], bsem.at[1, i]))
        sent.append(copies)
    total.run(last, total.steps)
    for at, value in g_cube.results():
        result[:, at] = value
    load(result, gffn, lsem.at[10]).wait()
    for at, value in d_cube.results():
        result[:, at] = value
    load(result, down, lsem.at[4]).wait()
    for copies in sent[-2:]:
        for copy in copies:
            copy.wait()
    g_cube.drain()
    d_cube.drain()
    total.drain()
    for u in range(3):
        z.drain(u)


def last_kernel(
    n_dp, n_mp, ffn_in, grad_out, w, w_d, b_in, q_in, gffn1, down1, middle, r_mid, cot, tok, gain_ffn, w_mix,
    gsum, base, parting, gmid, gain_part, gm, gb, rowdot,
    a, wv, wd, bv, bq, gffn, mid_v, cot_v, tok_v, wmb, gbr, gm_out, gm_in, gb_in, rd_col, rd_out, rd_in,
    lsem, gsem, wsem, ssem, rsem, *refs,
):
    p = Place(n_dp, n_mp)
    rows, width = ffn_in.shape
    own, h = rows // n_mp, bv.shape[2]
    mine = gm.shape[2]
    half, ch = width // 2, mine // 2
    sums, cube_g, cube_d = refs[:5], refs[5:8], refs[8:11]
    loads_w = [load(b_in, bv, lsem.at[1]), load(w, wv, lsem.at[3])]
    if own % 16:
        loads_w.append(load(q_in, bq, lsem.at[5]))
    loads = [load(ffn_in, a.at[0], lsem.at[0]), load(grad_out, a.at[1], lsem.at[2])]
    loads_d = [load(w_d, wd, lsem.at[4])]
    late = [
        load(src, dst, lsem.at[6 + i])
        for i, (src, dst) in enumerate(((middle, mid_v), (cot, cot_v), (tok.at[p.m], tok_v), (gffn1, gffn)))
    ]

    def mix_load(j, s):
        q = p.m ^ j
        return pltpu.make_async_copy(
            w_mix.at[pl.ds(pl.multiple_of(s * half + q * ch, LANE), ch)], wmb.at[s], wsem.at[s]
        )

    p.barrier()
    mix_load(1, 0).start()
    f = FfnSums(p, a, wv, wd, h, bv, bq, gsum, gsem, sums, cube_g, cube_d)
    total, g_cube, d_cube = f.total, f.g_cube, f.d_cube
    n = total.blocks
    for copy in loads_w:
        copy.wait()
    g_cube.stage(0)
    for copy in loads:
        copy.wait()
    total.run(0, n + 1)
    for s in range(1, p.bits):
        g_cube.stage(s)
    total.run(n + 1, n + 2)
    for copy in loads_d:
        copy.wait()
    d_cube.stage(0)
    total.run(n + 2, 2 * n)
    for copy in late:
        copy.wait()
    for at, value in g_cube.results():
        gffn[:, at] += value
    fine = 16 if own % 16 == 0 else own

    def norm_back(i, gains):
        at = pl.ds(pl.multiple_of(i * fine, fine), fine)
        g = gffn[at, :]
        n_own = mid_v[at, :] * r_mid[at, :]
        gains = gains + jnp.sum((g * n_own).reshape(fine // 8, 8, width), axis=0)
        gn = g * gain_ffn[...]
        back = r_mid[at, :] * (gn - n_own * jnp.mean(gn * n_own, axis=-1, keepdims=True))
        grad = cot_v[at, :].astype(F32) + back
        gffn[at, :] = grad
        low = grad.astype(BF16)
        gbr[at, :] = low
        dots = jnp.mean(low.astype(F32) * (mid_v[at, :] - tok_v[at, :].astype(F32)), axis=-1, keepdims=True)
        rd_col[at, :] = jnp.broadcast_to(dots, (fine, LANE))
        return gains

    gains = lax.fori_loop(0, own // fine, norm_back, jnp.zeros((8, width), F32))
    gmid_out = load(gffn, gmid, lsem.at[15])
    gain_part[...] = jnp.sum(gains, axis=0, keepdims=True)
    rd_out[...] = lax.dot_general(
        jnp.full((8, LANE), 1.0 / LANE, F32), rd_col[...], (((1,), (1,)), ((), ())),
        precision=lax.Precision.HIGHEST, preferred_element_type=F32,
    )

    def across(kind, j, owner):
        send, recv, to = ssem.at[kind, j], rsem.at[kind, owner], p.peer(j)
        if kind == 0:
            return remote(gm_out.at[j], gm_in.at[owner], send, recv, to)
        if kind == 1:
            return remote(rd_out, rd_in.at[owner], send, recv, to)
        here = pl.ds(pl.multiple_of((p.m ^ j) * mine, LANE), mine)
        return remote(gbr.at[:, here], gb_in.at[owner], send, recv, to)

    for j in range(1, n_mp):
        across(1, j, p.m).start()
    turns = [(j, s) for j in (*range(1, n_mp), 0) for s in range(2)]
    for at, (j, s) in enumerate(turns):
        mix_load(j, s).wait()
        if at + 1 < len(turns):
            mix_load(*turns[at + 1]).start()
        value = dot_trans(gbr[...], wmb[s]).astype(BF16)
        if j:
            gm_out[j, :, s * ch : (s + 1) * ch] = value
            if s:
                across(0, j, p.m).start()
        else:
            gm_in[p.m, :, s * ch : (s + 1) * ch] = value
    for j in range(1, n_mp):
        across(2, j, p.m).start()
    gb_in[p.m] = gbr[:, pl.ds(pl.multiple_of(p.m * mine, LANE), mine)]
    rd_in[p.m] = rd_out[...]
    gmid_out.wait()
    down_load = load(down1, gffn, lsem.at[10])
    total.run(2 * n, total.steps - n)
    for s in range(1, p.bits - 1):
        d_cube.stage(s)
    for part, at, value in d_cube.parting():
        parting[part, :, at] = value.astype(BF16)
    down_load.wait()
    for at, value in d_cube.results(p.bits - 1):
        gffn[:, at] += mid_v[:, at] + value
    back = [load(gffn, base, lsem.at[14])]
    total.run(total.steps - n, total.steps)
    for j in range(1, n_mp):
        for kind in range(3):
            across(kind, j, p.m ^ j).wait_recv()
    back.extend(load(src, dst, lsem.at[11 + i]) for i, (src, dst) in enumerate(((gm_in, gm), (gb_in, gb), (rd_in, rowdot))))
    for j in range(1, n_mp):
        for kind in range(3):
            across(kind, j, p.m).wait_send()
    for copy in back:
        copy.wait()
    g_cube.drain()
    d_cube.drain(p.bits - 1)
    total.drain()


def split_shape(n_mp, own, h):
    return (3, n_mp, own, h) if own % 16 else (1, 1, 16, LANE)


def parting_shape(n_mp, own, width):
    bits = n_mp.bit_length() - 1
    return (bits, own, max(size for _, size in bounds(width, bits, LANE)))


def ffn_first(n_dp, n_mp, cid, *args):
    (rows, width), h = args[0].shape, args[2].shape[2]
    shard, own, h_next = width // n_dp, rows // n_mp, args[6].shape[0] - h
    f_own = jax.ShapeDtypeStruct((own, width), F32)
    per = STEP // own if own % 16 else 1
    return pl.pallas_call(
        functools.partial(first_kernel, n_dp, n_mp),
        out_shape=(
            jax.ShapeDtypeStruct((3, shard, h), F32), f_own, f_own,
            jax.ShapeDtypeStruct((2, width, h_next), BF16), jax.ShapeDtypeStruct((h_next, width), BF16),
            jax.ShapeDtypeStruct((3, rows, h_next), BF16), jax.ShapeDtypeStruct(split_shape(n_mp, own, h_next), BF16),
        ),
        in_specs=[ANY] * 7,
        out_specs=(ANY,) * 7,
        scratch_shapes=[
            pltpu.VMEM((2, rows, width), BF16),
            pltpu.VMEM((2, width, h), BF16),
            pltpu.VMEM((h, width), BF16),
            pltpu.VMEM((2, width, h_next), BF16),
            pltpu.VMEM((h_next, width), BF16),
            pltpu.VMEM((3, rows, h), BF16),
            pltpu.VMEM(split_shape(n_mp, own, h), BF16),
            pltpu.VMEM((2, 3, STEP, h_next), BF16),
            pltpu.VMEM((2, 3, per, own, h_next) if own % 16 else (1, 1, 1, 16, LANE), BF16),
            pltpu.VMEM((own, width), F32),
            pltpu.SemaphoreType.DMA((11,)),
            pltpu.SemaphoreType.DMA,
            pltpu.SemaphoreType.DMA((2, rows // STEP)),
            *RowSum.scratch(n_dp, 3, shard, h),
            *CubeSum.scratch(n_mp, own, width),
            *CubeSum.scratch(n_mp, own, width),
            *RowGather.scratch(n_dp, 3),
        ],
        compiler_params=pltpu.CompilerParams(collective_id=cid, has_side_effects=True, vmem_limit_bytes=VMEM_LIMIT),
        name="ffn_first",
    )(*args)


def ffn_last(n_dp, n_mp, cid, *args):
    (rows, width), h = args[0].shape, args[2].shape[2]
    shard, own, mine = width // n_dp, rows // n_mp, width // n_mp
    piece = jax.ShapeDtypeStruct((n_mp, own, mine), BF16)
    return pl.pallas_call(
        functools.partial(last_kernel, n_dp, n_mp),
        out_shape=(
            jax.ShapeDtypeStruct((3, shard, h), F32), jax.ShapeDtypeStruct((own, width), F32),
            jax.ShapeDtypeStruct(parting_shape(n_mp, own, width), BF16),
            jax.ShapeDtypeStruct((own, width), F32), jax.ShapeDtypeStruct((1, width), F32),
            piece, piece, jax.ShapeDtypeStruct((n_mp, 8, own), F32),
        ),
        in_specs=[ANY] * 9 + [VMEM, ANY, ANY, VMEM, ANY],
        out_specs=(ANY, ANY, VMEM, ANY, VMEM, ANY, ANY, ANY),
        scratch_shapes=[
            pltpu.VMEM((2, rows, width), BF16),
            pltpu.VMEM((2, width, h), BF16),
            pltpu.VMEM((h, width), BF16),
            pltpu.VMEM((3, rows, h), BF16),
            pltpu.VMEM(split_shape(n_mp, own, h), BF16),
            pltpu.VMEM((own, width), F32),
            pltpu.VMEM((own, width), F32),
            pltpu.VMEM((own, width), BF16),
            pltpu.VMEM((own, width), BF16),
            pltpu.VMEM((2, mine // 2, width), BF16),
            pltpu.VMEM((own, width), BF16),
            *[pltpu.VMEM((n_mp, own, mine), BF16)] * 3,
            pltpu.VMEM((own, LANE), F32),
            pltpu.VMEM((8, own), F32),
            pltpu.VMEM((n_mp, 8, own), F32),
            pltpu.SemaphoreType.DMA((16,)),
            pltpu.SemaphoreType.DMA,
            pltpu.SemaphoreType.DMA((2,)),
            pltpu.SemaphoreType.DMA((3, n_mp)),
            pltpu.SemaphoreType.DMA((3, n_mp)),
            *RowSum.scratch(n_dp, 3, shard, h),
            *CubeSum.scratch(n_mp, own, width),
            *CubeSum.scratch(n_mp, own, width, False),
        ],
        compiler_params=pltpu.CompilerParams(collective_id=cid, has_side_effects=True, vmem_limit_bytes=VMEM_LIMIT),
        name="ffn_last",
    )(*args)


def project_kernel(
    n_dp, n_mp, normed, mixed, gm, g_b, pin, pf, pg, st, phasor, r_mix, rowdot, bound, gain_mix, w, gmid, tok, r_in, gain_in,
    gain_ffn_part, base, parting, gw, gtok, small, done,
    a, bv, bq, gall, dgain, dbound, tok_v, base_v, last_v, lsem, rsend, rrecv, dsem, *refs,
):
    p = Place(n_dp, n_mp)
    rows, width = normed.shape
    mine = bv.shape[2]
    half, ch, own = width // 2, mine // 2, rows // n_mp
    shard = gw.shape[2]
    sums, cube_refs, vec = refs[:5], refs[5:8], SmallSum(p, refs[8:10])
    loads = [load(mixed, a.at[0], lsem.at[0]), load(g_b, bv.at[0], lsem.at[1])]
    late = [load(normed, a.at[1], lsem.at[12])]
    late.append(load(tok.at[p.m], tok_v, lsem.at[16]))
    early_d = [load(parting, last_v.at[0], lsem.at[19])]
    late_d = load(base, base_v, lsem.at[20])
    p.barrier(far=True)
    for copy in loads:
        copy.wait()

    down_cols = bounds(width, p.bits, LANE)

    def last_stage(part):
        size = down_cols[part][1]
        to = p.peer(1 << ((part + p.bits - 1) % p.bits))
        return remote(last_v.at[0, part, :, :size], last_v.at[1, part, :, :size], dsem.at[0, part], dsem.at[1, part], to)

    for copy in early_d:
        copy.wait()
    for part in range(p.bits):
        last_stage(part).start()

    def piece(b, e):
        left = jnp.where(b == 0, 0, 1)
        return dot_rows(a[left, :, pl.ds(pl.multiple_of(e * shard, LANE), shard)], bv[b])

    out_cols = bounds(mine, p.bits, LANE)

    def spread(b):
        def view(q, part):
            lo, size = out_cols[part]
            return gall.at[b, q, :, lo : lo + size]

        return CubeGather(p, (rsend.at[b], rrecv.at[b]), view)

    def finish(b, acc):
        gall[b, p.m] = acc[...].astype(BF16)
        spread(b).stage(0)
        for s in range(1, p.bits):

            @pl.when(b >= s)
            def _():
                spread(b - s).stage(s)

    def partial(q, lo, size):
        value = 0.0
        for b in range(3):
            left = bq[b, q] if own % 16 else bv[1 + b, pl.ds(pl.multiple_of(q * own, 16), own), :]
            value = value + dot_trans(left, held[0][b, lo : lo + size, :])
        return value

    held = []
    total = RowSum(p, sums, piece, finish, True)
    cube = CubeSum(p, cube_refs, partial, width)
    tick, early = p.chips, p.chips - 1
    def recurrence(gm_v, pin_v, pf_v, pg_v, st_v, ph_v, r_v, rd_v, bl, gain, a_re, a_im, b_re, b_im):
        scans = [
            load(src, dst, lsem.at[2 + i])
            for i, (src, dst) in enumerate(
                ((gm, gm_v), (pg, pg_v), (st, st_v), (pf, pf_v), (phasor, ph_v), (pin, pin_v), (r_mix, r_v))
            )
        ]
        scans.append(load(bound.at[:, pl.ds(pl.multiple_of(p.m * ch, LANE), ch)], bl, lsem.at[9]))
        for side in range(2):
            at = pl.ds(pl.multiple_of(side * half + p.m * ch, LANE), ch)
            scans.append(load(gain_mix.at[:, at], gain.at[:, side * ch : (side + 1) * ch], lsem.at[10 + side]))
        eighth = jnp.full((8, LANE), 0.125, F32)
        for q in range(n_mp):
            rd_v[q * own : (q + 1) * own, :] = lax.dot_general(
                rowdot[q], eighth, (((0,), (0,)), ((), ())), precision=lax.Precision.HIGHEST, preferred_element_type=F32
            )[:, :1]
        total.run(0, 1, ahead=False)
        for copy in scans:
            copy.wait()
        scan_backward(
            gm_v, pin_v, pf_v, pg_v, st_v, ph_v, r_v, rd_v, bl, gain, bv.at[1], bv.at[2], bv.at[3], dgain, dbound,
            a_re, a_im, b_re, b_im,
            between=(lambda: total.run(1, 2, True, False), lambda: total.run(2, early, True, False)),
        )

    part, column = (rows, mine), pltpu.VMEM((rows, 1), F32)
    pl.run_scoped(
        recurrence,
        pltpu.VMEM(part, BF16), *[pltpu.VMEM(part, F32)] * 5, column, column, pltpu.VMEM((1, ch), F32), pltpu.VMEM((1, mine), F32),
        *[pltpu.VMEM((ch // LANE, rows, LANE), F32)] * 4,
    )

    def sums_over_devices(wv):
        held.append(wv)
        late.extend(load(w.at[i], wv.at[i], lsem.at[13 + i]) for i in range(3))
        for copy in late:
            copy.wait()
        if own % 16:
            for b in range(3):
                wide = bv[1 + b].astype(F32)
                for q in range(n_mp):
                    bq[b, q] = wide[q * own : (q + 1) * own].astype(BF16)
        cube.stage(0)
        total.run(early, early + tick, True)
        total.run(early + tick, early + 2 * tick)
        late_d.wait()
        done_out = []
        for part, (lo, size) in enumerate(down_cols):
            last_stage(part).wait()
            value = base_v[:, lo : lo + size] + last_v[1, part, :, :size].astype(F32)
            last_v[1, part, :, :size] = value.astype(BF16)
            done_out.append(load(last_v.at[1, part, :, :size], done.at[:, lo : lo + size], dsem.at[2, part]))
        gmid_load = load(gmid, base_v, lsem.at[17])
        total.run(early + 2 * tick, early + 3 * tick)
        for s in range(1, p.bits):
            cube.stage(s)
        total.run(early + 3 * tick, early + 4 * tick)
        total.run(early + 4 * tick, early + 5 * tick)
        for at, value in cube.results():
            gtok[:, at] = value
        gmid_load.wait()
        fine = 16 if own % 16 == 0 else own

        def norm_back(i, gains):
            at = pl.ds(pl.multiple_of(i * fine, fine), fine)
            g = gtok[at, :]
            n_own = tok_v[at, :].astype(F32) * r_in[at, :]
            gains = gains + jnp.sum((g * n_own).reshape(fine // 8, 8, width), axis=0)
            gn = g * gain_in[...]
            gtok[at, :] = base_v[at, :] + r_in[at, :] * (gn - n_own * jnp.mean(gn * n_own, axis=-1, keepdims=True))
            return gains

        gains = lax.fori_loop(0, own // fine, norm_back, jnp.zeros((8, width), F32))
        vec.buf[0] = jnp.zeros((4, width), F32)
        vec.buf[0, 0:1] = jnp.sum(gains, axis=0, keepdims=True)
        vec.buf[0, 1:2] = gain_ffn_part[...]
        here = pl.ds(pl.multiple_of(p.m * ch, LANE), ch)
        vec.buf[0, 2:3, here] = dgain[:, :ch]
        vec.buf[0, 2:3, pl.ds(pl.multiple_of(half + p.m * ch, LANE), ch)] = dgain[:, ch:]
        vec.buf[0, 3:4, here] = dbound[...]
        vec.twins()
        total.run(early + 5 * tick, total.steps)
        vec.cube()
        for b in range(total.blocks):
            for s in range(max(1, total.blocks - b), p.bits):
                spread(b).stage(s)
        vec.line()
        for b in range(total.blocks):
            spread(b).last()
        out = load(gall, gw, lsem.at[18])
        small[...] = vec.result()
        for copy in done_out:
            copy.wait()
        out.wait()
        for b in range(total.blocks):
            spread(b).drain()
        cube.drain()
        total.drain()


    pl.run_scoped(sums_over_devices, pltpu.VMEM((3, width, mine), BF16))


def project_back(n_dp, n_mp, cid, *args):
    rows, width = args[0].shape
    mine, shard, own = width // n_mp, width // n_dp, rows // n_mp
    ch = mine // 2
    return pl.pallas_call(
        functools.partial(project_kernel, n_dp, n_mp),
        out_shape=(
            jax.ShapeDtypeStruct((4, n_mp, shard, mine), BF16),
            jax.ShapeDtypeStruct((own, width), F32),
            jax.ShapeDtypeStruct((4, width), F32),
            jax.ShapeDtypeStruct((own, width), BF16),
        ),
        in_specs=[ANY] * 10 + [VMEM] + [ANY] * 5 + [VMEM] * 3 + [ANY] * 2,
        out_specs=(ANY, VMEM, VMEM, ANY),
        scratch_shapes=[
            pltpu.VMEM((2, rows, width), BF16),
            pltpu.VMEM((4, rows, mine), BF16),
            pltpu.VMEM((3, n_mp, own, mine) if own % 16 else (1, 1, 16, LANE), BF16),
            pltpu.VMEM((4, n_mp, shard, mine), BF16),
            pltpu.VMEM((1, mine), F32),
            pltpu.VMEM((1, ch), F32),
            pltpu.VMEM((own, width), BF16),
            pltpu.VMEM((own, width), F32),
            pltpu.VMEM((2, *parting_shape(n_mp, own, width)), BF16),
            pltpu.SemaphoreType.DMA((21,)),
            *[pltpu.SemaphoreType.DMA((4, n_mp.bit_length() - 1, n_mp))] * 2,
            pltpu.SemaphoreType.DMA((3, n_mp)),
            *RowSum.scratch(n_dp, 4, shard, mine),
            *CubeSum.scratch(n_mp, own, width),
            *SmallSum.scratch(n_dp, n_mp, (4, width)),
        ],
        compiler_params=pltpu.CompilerParams(collective_id=cid, has_side_effects=True, vmem_limit_bytes=VMEM_LIMIT),
        name="project_back",
    )(*args)


def result_kernel(
    n_mp, gmix, one, two, mixed, gtok, small,
    o_mixed, o_tok, o_gin, o_win, o_wf, o_wo, o_bound, o_gmix, o_wm, o_gffn, o_gate, o_up, o_down,
    gm, gw, gffn, down, mixed_v, tok_v, sem, osem,
):
    d = lax.axis_index("dp")
    shard, mine = gmix.shape[2:]
    ch, half = mine // 2, n_mp * mine // 2
    h, h2 = one.shape[2], two.shape[2]
    mixer = [load(gmix.at[b], gm.at[b], sem.at[b]) for b in range(4)]
    through = [load(mixed, mixed_v, sem.at[4]), load(gtok, tok_v, sem.at[5])]
    ffn = [
        (load(one.at[i], gffn.at[i, :, :h], sem.at[6 + 2 * i]), load(two.at[i], gffn.at[i, :, h:], sem.at[7 + 2 * i]))
        for i in range(3)
    ]
    outs = []
    for b, out in enumerate((o_wm, o_win, o_wf, o_wo)):
        mixer[b].wait()
        for q in range(n_mp):
            value = gm[b, q].astype(F32)
            if b:
                gw[b, :, q * ch : (q + 1) * ch] = value[:, :ch]
                gw[b, :, half + q * ch : half + (q + 1) * ch] = value[:, ch:]
            else:
                gw[b, :, q * mine : (q + 1) * mine] = value
        outs.append(load(gw.at[b], out, osem.at[b]))
    for i, (copy, src, out) in enumerate(zip(through, (mixed_v, tok_v), (o_mixed, o_tok))):
        copy.wait()
        outs.append(load(src, out, osem.at[4 + i]))
    for i, out in enumerate((o_gate, o_up)):
        for copy in ffn[i]:
            copy.wait()
        outs.append(load(gffn.at[i], out, osem.at[6 + i]))
    at = pl.ds(pl.multiple_of(d * shard, LANE), shard)
    for row, out in enumerate((o_gin, o_gffn, o_gmix)):
        out[...] = small[row : row + 1, at]
    size = shard // 2
    if size % LANE == 0:
        o_bound[...] = small[3:4, pl.ds(pl.multiple_of(d * size, LANE), size)]
    else:
        pair = small[3:4, pl.ds(pl.multiple_of(lax.div(d, 2) * 2 * size, LANE), 2 * size)]
        o_bound[...] = jnp.where(lax.rem(d, 2) == 0, pair[:, :size], pair[:, size:])
    for copy in ffn[2]:
        copy.wait()
    for lo in range(0, h + h2, LANE):
        down[lo : lo + LANE, :] = gffn[2, :, lo : lo + LANE].T
    outs.append(load(down, o_down, osem.at[8]))
    for copy in outs:
        copy.wait()


def results(n_dp, n_mp, gmix, one, two, mixed, gtok, small):
    shard, mine = gmix.shape[2:]
    width, ffn = n_mp * mine, one.shape[2] + two.shape[2]
    own = mixed.shape[0]

    def f32(*shape):
        return jax.ShapeDtypeStruct(shape, F32)

    row = f32(1, shard)
    return pl.pallas_call(
        functools.partial(result_kernel, n_mp),
        out_shape=(
            jax.ShapeDtypeStruct((own, width), BF16), f32(own, width), row, *(f32(shard, width),) * 3, f32(1, shard // 2), row,
            f32(shard, width), row, f32(shard, ffn), f32(shard, ffn), f32(ffn, shard),
        ),
        in_specs=[ANY] * 5 + [VMEM],
        out_specs=(ANY, ANY, VMEM, ANY, ANY, ANY, VMEM, VMEM, ANY, VMEM, ANY, ANY, ANY),
        scratch_shapes=[
            pltpu.VMEM((4, n_mp, shard, mine), BF16),
            pltpu.VMEM((4, shard, width), F32),
            pltpu.VMEM((3, shard, ffn), F32),
            pltpu.VMEM((ffn, shard), F32),
            pltpu.VMEM((own, width), BF16),
            pltpu.VMEM((own, width), F32),
            pltpu.SemaphoreType.DMA((12,)),
            pltpu.SemaphoreType.DMA((9,)),
        ],
        compiler_params=pltpu.CompilerParams(vmem_limit_bytes=VMEM_LIMIT),
        name="results",
    )(gmix, one, two, mixed, gtok, small)


def per_device(n_dp, n_mp, tokens, segment_ids, cotangent, gain_in, w_in, w_forget, w_outgate, bound_logit, gain_mix,
               w_mix, gain_ffn, w_gate, w_up, w_down):
    m, d = lax.axis_index("mp"), lax.axis_index("dp")
    rows, width = tokens.shape
    half = bound_logit.shape[0]
    ch = half // n_mp
    mine = 2 * ch
    own = rows // n_mp
    ffn = w_gate.shape[1]
    padded = -(-ffn // LANE) * LANE
    cut = padded // 2 // LANE * LANE
    if padded != ffn:
        fill = ((0, 0), (0, padded - ffn))
        w_gate, w_up, w_down = jnp.pad(w_gate, fill), jnp.pad(w_up, fill), jnp.pad(w_down, fill[::-1])

    normed, r_in, pin, pf, pg, st, phasor, r_mix, mixer_out, ffn_in, middle, r_mid, wm, w_cat, w_one, d_one, grad_out = mixer_forward(
        n_dp, n_mp, 2, cut, w_in, w_forget, w_outgate, w_mix, w_gate, w_up, w_down, cotangent, tokens, segment_ids,
        bound_logit[None], gain_mix[None], gain_in[None], gain_ffn[None],
    )
    grad_out = grad_out.reshape(rows, width)

    g_one, gffn, down, w_two, d_two, b_two, q_two = ffn_first(
        n_dp, n_mp, 3, ffn_in, grad_out, w_one, d_one, w_gate, w_up, w_down
    )
    tok_own = tokens.reshape(n_mp, own, width)
    g_two, base, parting, gmid, gain_ffn_part, gm, gb, rowdot = ffn_last(
        n_dp, n_mp, 4, ffn_in, grad_out, w_two, d_two, b_two, q_two, gffn, down, middle, r_mid, cotangent, tok_own,
        gain_ffn[None], wm,
    )
    g_mixer, grad_tokens, small, mixed = project_back(
        n_dp, n_mp, 5, normed, mixer_out, gm.reshape(rows, 2 * ch), gb.reshape(rows, 2 * ch), pin, pf, pg, st, phasor, r_mix, rowdot,
        bound_logit[None], gain_mix[None], w_cat, gmid, tok_own, r_in, gain_in[None], gain_ffn_part, base, parting,
    )

    out = results(n_dp, n_mp, g_mixer, g_one, g_two, mixed, grad_tokens, small)
    out = [v[0] if v.shape[0] == 1 else v for v in out]
    if padded != ffn:
        out[10:] = [out[10][:, :ffn], out[11][:, :ffn], out[12][:ffn]]
    return tuple(out)


def solution(mesh):
    both, split = P(("dp", "mp"), None), P("dp", "mp")
    row, vec = P("dp", None), P("dp")
    return jax.shard_map(
        functools.partial(per_device, mesh.shape["dp"], mesh.shape["mp"]),
        mesh=mesh,
        in_specs=(row, row, both, P(), row, row, row, P(), P(), row, P(), split, split, P("mp", "dp")),
        out_specs=(both, both, vec, row, row, row, vec, vec, row, vec, split, split, P("mp", "dp")),
        check_vma=False,
    )
```
